32 devices in a mesh: batch: 8 (over z, y), col: 4 (over x, core).
Axes of the slice: x: 2, y: 2, z: 4, core: 2. Of those that a mesh axis runs over, the one named last changes fastest.
Arguments:
- watch_ids: int32 [1024, 50], P('batch'), may hold values from 0 to 65535
- search_ids: int32 [1024, 50], P('batch'), may hold values from 0 to 65535
- demo_ids: int32 [1024, 4], P('batch'), may hold values from 0 to 255
- pos_ids: int32 [1024], P('batch'), may hold values from 0 to 65535
- neg_ids: int32 [5120], replicated, may hold values from 0 to 65535
- valid_counts: int32 [8], P('batch'), may hold values from 1 to 128, as said below
- watch_table: bfloat16 [256, 65536], P('col', 'batch'), may hold values from -15 to 15
- search_table: bfloat16 [256, 65536], P('col', 'batch'), may hold values from -15 to 15
- demo_table: bfloat16 [256, 88], replicated, may hold values from -3 to 3
- out_table: bfloat16 [256, 65536], P('col', 'batch'), may hold values from -1.796875 to 1.796875
- w_first: bfloat16 [600, 1024], replicated, may hold values from -0.25 to 0.25
- b_first: float32 [1024], replicated, may hold values from -1.8 to 1.8
- w_second: bfloat16 [1024, 512], replicated, may hold values from -0.1875 to 0.1875
- b_second: float32 [512], replicated, may hold values from -1.8 to 1.8
- w_third: bfloat16 [512, 256], replicated, may hold values from -0.25 to 0.25
- b_third: float32 [256], replicated, may hold values from -1.8 to 1.8
Outputs:
- user_vecs: bfloat16 [1024, 256], P(('batch', 'col'))
- loss: float32 [], replicated
- grad_watch: float32 [256, 65536], P('col', 'batch')
- grad_search: float32 [256, 65536], P('col', 'batch')
- grad_out: float32 [256, 65536], P('col', 'batch')
- grad_demo: float32 [256, 88], replicated
- grad_w_first: float32 [600, 1024], replicated
- grad_b_first: float32 [1024], replicated
- grad_w_second: float32 [1024, 512], replicated
- grad_b_second: float32 [512], replicated
- grad_w_third: float32 [512, 256], replicated
- grad_b_third: float32 [256], replicated
The draws below stay inside these ranges and needn't reach their ends.
Inputs may be any that keep to these rules, and one draw needn't show every extreme that they name: `valid_counts`: each index of batch has that many valid examples, its first slots; the last index of batch has exactly 128.
All inputs are finite; a program needn't handle non-finite values.
Results may differ from the reference program's by a relative error of at most 0.015.
Values may be sent and summed in bfloat16 or wider, within the bound.
A program may use at most 128 MiB of HBM per device.

```python
import math
import jax
import jax.numpy as jnp
import numpy as np
from jax import lax

D_EMB = 256
DEMO_W = 88
H1 = 1024
H2 = 512
BAG = 50
FIELDS = 4
DEMO_BUCKETS = 256
NEG = 5120
E_DEV = 128
VOCAB = 65536
TOTAL_EX = 1024
CONCAT = 600
N_BATCH = 8


def draw_valid_counts(key, part):
    key = jax.random.fold_in(key, 11)
    place = jnp.arange(N_BATCH)
    low_end = E_DEV // 3
    rising = low_end + (E_DEV - low_end) * place // max(N_BATCH - 1, 1)
    jitter = jax.random.randint(key, (N_BATCH,), 0, E_DEV // 8 + 1)
    counts_drawn = jnp.where(place == N_BATCH - 1, E_DEV, jnp.maximum(rising - jitter, 1))
    return counts_drawn.astype(jnp.int32)


def plant(result, own_key, low, largest):
    spot = [jax.random.randint(jax.random.fold_in(own_key, axis), (), 0, length) for axis, length in enumerate(result.shape)]
    main_axis = result.shape.index(max(result.shape))
    neighbour = spot[:main_axis] + [(spot[main_axis] + 1) % result.shape[main_axis]] + spot[main_axis + 1:]
    return result.at[tuple(spot)].set(low).at[tuple(neighbour)].set(largest)


def steps_of(rng, dims, cuts, low, top_value):
    loudness, own = 1.0, jax.random.fold_in(rng, 6)
    for dim, shards_of in cuts:
        steps = jnp.exp(jax.random.uniform(jax.random.fold_in(own, dim), (shards_of,), jnp.float32, low / len(cuts), top_value / len(cuts)))
        loudness = loudness * jnp.repeat(steps, dims[dim] // shards_of).reshape([-1 if axis == dim else 1 for axis in range(len(dims))])
    return loudness


def rank_bounds(count, lean):
    weights = [(1 << 20) // math.isqrt(grade ** lean) + 1 for grade in range(1, count + 1)]
    spread = 1 + sum(weights) // (1 << 30)
    return np.cumsum(np.array([max(1, weight // spread) for weight in weights]))


def skewed_ids(own_key, dims, count, lean):
    listing = rank_bounds(count, lean)
    ticket = jax.random.randint(jax.random.fold_in(own_key, 1), dims, 0, int(listing[count - 1]))
    rank = jnp.searchsorted(jnp.asarray(listing, jnp.int32), ticket, side="right")
    return jax.random.permutation(jax.random.fold_in(own_key, 2), count)[rank].astype(jnp.int32)


def centred(key, shape, spread, reach, cuts=(), held_as=jnp.bfloat16):
    values = jax.random.normal(key, shape, jnp.float32) * spread
    if len(cuts) > 0:
        values = steps_of(key, shape, cuts, -0.22, 0.18) * values
    return jnp.clip(values, min=-reach, max=reach).astype(held_as)


def setup_inputs(seed: int = 0) -> dict:
    arg_keys = jax.random.split(jax.random.key(seed), 17)
    watch_ids = plant(skewed_ids(arg_keys[0], (TOTAL_EX, BAG), VOCAB, 1), jax.random.fold_in(arg_keys[0], 3), 0, VOCAB - 1).astype(jnp.int32)
    search_ids = plant(skewed_ids(arg_keys[1], (TOTAL_EX, BAG), VOCAB, 2), jax.random.fold_in(arg_keys[1], 3), 0, VOCAB - 1).astype(jnp.int32)
    demo_ids = plant(jax.random.randint(arg_keys[2], (TOTAL_EX, FIELDS), 0, DEMO_BUCKETS), jax.random.fold_in(arg_keys[2], 1), 0, DEMO_BUCKETS - 1).astype(jnp.int32)
    pos_ids = plant(jax.random.randint(arg_keys[3], (TOTAL_EX,), 0, VOCAB), jax.random.fold_in(arg_keys[3], 1), 0, VOCAB - 1).astype(jnp.int32)
    neg_ids = plant(jax.random.randint(arg_keys[4], (NEG,), 0, VOCAB), jax.random.fold_in(arg_keys[4], 1), 0, VOCAB - 1).astype(jnp.int32)
    valid_counts = draw_valid_counts(jax.random.fold_in(arg_keys[16], 71), 0)
    watch_table = centred(arg_keys[6], (D_EMB, VOCAB), 2.5, 15.0, ((0, 4), (1, 8)))
    search_table = centred(arg_keys[7], (D_EMB, VOCAB), 2.5, 15.0, ((0, 4), (1, 8)))
    demo_table = centred(arg_keys[8], (DEMO_BUCKETS, DEMO_W), 0.5, 3.0)
    out_table = centred(arg_keys[9], (D_EMB, VOCAB), 0.3, 1.796875, ((0, 4), (1, 8)))
    w_first = centred(arg_keys[10], (CONCAT, H1), CONCAT ** -0.5, 0.25)
    b_first = centred(arg_keys[11], (H1,), 0.3, 1.8, (), jnp.float32)
    w_second = centred(arg_keys[12], (H1, H2), H1 ** -0.5, 0.1875)
    b_second = centred(arg_keys[13], (H2,), 0.3, 1.8, (), jnp.float32)
    w_third = centred(arg_keys[14], (H2, D_EMB), H2 ** -0.5, 0.25)
    b_third = centred(arg_keys[15], (D_EMB,), 0.3, 1.8, (), jnp.float32)
    return dict(watch_ids=watch_ids, search_ids=search_ids, demo_ids=demo_ids, pos_ids=pos_ids, neg_ids=neg_ids, valid_counts=valid_counts, watch_table=watch_table, search_table=search_table, demo_table=demo_table, out_table=out_table, w_first=w_first, b_first=b_first, w_second=w_second, b_second=b_second, w_third=w_third, b_third=b_third)


@jax.custom_vjp
def low(v):
    return lax.optimization_barrier(v.astype(jnp.bfloat16)).astype(jnp.float32)

@jax.custom_vjp
def low_back(v):
    return v

def low_keep(v):
    return (low(v), None)

def low_pass(kept, grad):
    return (grad,)

def back_keep(v):
    return (v, None)

def back_low(kept, grad):
    return (low(grad),)
low.defvjp(low_keep, low_pass)
low_back.defvjp(back_keep, back_low)

def product(left, right):
    return jnp.dot(left, right, precision=lax.Precision.HIGHEST)

def reference(watch_ids, search_ids, demo_ids, pos_ids, neg_ids, valid_counts, watch_table, search_table, demo_table, out_table, w_first, b_first, w_second, b_second, w_third, b_third):
    floats_in = (watch_table.astype(jnp.float32), search_table.astype(jnp.float32), demo_table.astype(jnp.float32), out_table.astype(jnp.float32), w_first.astype(jnp.float32), b_first.astype(jnp.float32), w_second.astype(jnp.float32), b_second.astype(jnp.float32), w_third.astype(jnp.float32), b_third.astype(jnp.float32))
    valid_total = jnp.sum(valid_counts).astype(jnp.float32)
    row_index = jnp.arange(TOTAL_EX).astype(jnp.int32)
    live_rows = row_index % E_DEV < jnp.take(valid_counts, row_index // E_DEV)
    weight = jnp.where(live_rows, 1.0 / valid_total, 0.0).astype(jnp.float32)
    block_rows = min(1024, TOTAL_EX)
    block_count = TOTAL_EX // block_rows
    blocks = (watch_ids.reshape(block_count, block_rows, BAG), search_ids.reshape(block_count, block_rows, BAG), demo_ids.reshape(block_count, block_rows, FIELDS), pos_ids.reshape(block_count, block_rows), weight.reshape(block_count, block_rows))

    def forward(watch_float, search_float, demo_float, out_float, first_w, first_b, second_w, second_b, third_w, third_b):
        watch_rows = watch_float.T
        search_rows = search_float.T
        out_rows = out_float.T
        neg_table = jnp.take(out_rows, neg_ids, axis=0)

        def block_loss(inputs_block):
            watch_block, search_block, demo_block, pos_block, weight_block = inputs_block
            pooled_watch = lax.optimization_barrier(jnp.sum(jnp.take(watch_rows, watch_block, axis=0), axis=1)) / BAG
            pooled_search = lax.optimization_barrier(jnp.sum(jnp.take(search_rows, search_block, axis=0), axis=1)) / BAG
            bucket_counts = lax.optimization_barrier(jnp.sum((demo_block[:, :, None] == jnp.arange(DEMO_BUCKETS)[None, None, :]).astype(jnp.float32), axis=1))
            demo_vec = product(bucket_counts, demo_float)
            joined = low(low_back(jnp.concatenate([pooled_watch, pooled_search, demo_vec], axis=1)))
            pre_first = low_back(product(joined, first_w) + first_b)
            act_first = low(jax.nn.gelu(pre_first))
            pre_second = low_back(product(act_first, second_w) + second_b)
            act_second = low(jax.nn.gelu(pre_second))
            user_block = low(low_back(product(act_second, third_w) + third_b))
            pos_table = low_back(jnp.take(out_rows, pos_block, axis=0))
            neg_logits = low_back(product(user_block, neg_table.T))
            pos_logit = low_back(lax.optimization_barrier(jnp.sum(user_block * pos_table, axis=1)))
            row_peak = jnp.maximum(lax.optimization_barrier(jnp.max(neg_logits, axis=1)), pos_logit)
            row_total = lax.optimization_barrier(jnp.sum(jnp.exp(neg_logits - row_peak[:, None]), axis=1)) + jnp.exp(pos_logit - row_peak)
            lse = row_peak + jnp.log(row_total)
            return (jnp.sum(weight_block * (lse - pos_logit)), user_block)
        losses, user_blocks = lax.map(jax.checkpoint(block_loss), blocks)
        return (jnp.sum(losses), user_blocks.reshape(TOTAL_EX, D_EMB))
    (loss, user_vecs), pull = jax.vjp(forward, *floats_in)
    grads = pull((jnp.ones((), jnp.float32), jnp.zeros_like(user_vecs)))
    return (user_vecs.astype(jnp.bfloat16), loss, grads[0], grads[1], grads[3], grads[2], grads[4], grads[5], grads[6], grads[7], grads[8], grads[9])
```

```python
import functools
import math

import jax
import jax.numpy as jnp
from jax import lax
from jax.experimental import pallas as pl
from jax.experimental.pallas import tpu as pltpu
from jax.sharding import PartitionSpec as P


def contract_rows(left, right):
    return lax.dot_general(
        left, right, (((0,), (0,)), ((), ())), preferred_element_type=jnp.float32
    )


def contract_cols(left, right):
    return lax.dot_general(
        left, right, (((1,), (1,)), ((), ())), preferred_element_type=jnp.float32
    )


def gelu_back(pre_value, grad_value):
    return jax.vjp(jax.nn.gelu, pre_value)[1](grad_value)[0]


def per_device(
    watch_ids,
    search_ids,
    demo_ids,
    pos_ids,
    neg_ids,
    valid_counts,
    watch_table,
    search_table,
    demo_table,
    out_table,
    w_first,
    b_first,
    w_second,
    b_second,
    w_third,
    b_third,
):
    row_count = watch_ids.shape[0]
    bag_size = watch_ids.shape[1]
    col_width = watch_table.shape[0]
    vocab_rows = watch_table.shape[1]
    embed_width = col_width * lax.axis_size("col")
    offset = lax.axis_index("batch") * vocab_rows
    col_slot = lax.axis_index("col")
    quarter = row_count // lax.axis_size("col")
    low_width = math.gcd(vocab_rows, 128)
    high_width = vocab_rows // low_width

    def owned(id_values):
        local_ids = id_values - offset
        return jnp.where((local_ids >= 0) & (local_ids < vocab_rows), local_ids, vocab_rows)

    def bag_counts(id_block):
        local_ids = owned(id_block)
        high_hot = (
            local_ids[:, :, None] // low_width == jnp.arange(high_width)[None, None, :]
        ).astype(jnp.bfloat16)
        low_hot = (
            local_ids[:, :, None] % low_width == jnp.arange(low_width)[None, None, :]
        ).astype(jnp.bfloat16)
        counted = jnp.einsum("rbh,rbl->rhl", high_hot, low_hot, preferred_element_type=jnp.bfloat16)
        return counted.reshape(id_block.shape[0], vocab_rows)

    def single_hot(id_block):
        return (owned(id_block)[:, None] == jnp.arange(vocab_rows)[None, :]).astype(jnp.bfloat16)

    zero_col = jnp.zeros((col_width, 1), jnp.bfloat16)
    padded_out = jnp.concatenate([out_table, zero_col], axis=1)
    all_watch, all_search, all_pos = (
        lax.all_gather(watch_ids, "batch", axis=0, tiled=True),
        lax.all_gather(search_ids, "batch", axis=0, tiled=True),
        lax.all_gather(pos_ids, "batch", axis=0, tiled=True),
    )
    total_rows = all_watch.shape[0]
    block_rows = min(1024, total_rows)
    block_count = total_rows // block_rows
    neg_local = owned(neg_ids)
    neg_part = jnp.take(padded_out, neg_local, axis=1).astype(jnp.float32)

    def flatten_blocks(stacked):
        return stacked.transpose(1, 0, 2).reshape(col_width, total_rows)

    def bag_block(inputs_block):
        watch_block, search_block, pos_block = inputs_block
        watch_part = contract_cols(watch_table, bag_counts(watch_block))
        search_part = contract_cols(search_table, bag_counts(search_block))
        pos_part = contract_cols(out_table, single_hot(pos_block))
        return (watch_part, search_part, pos_part)

    id_blocks = (
        all_watch.reshape(block_count, block_rows, bag_size),
        all_search.reshape(block_count, block_rows, bag_size),
        all_pos.reshape(block_count, block_rows),
    )
    watch_parts, search_parts, pos_parts = lax.map(bag_block, id_blocks)
    watch_sum, search_sum, pos_rows = (
        lax.psum_scatter(flatten_blocks(watch_parts), "batch", scatter_dimension=1, tiled=True),
        lax.psum_scatter(flatten_blocks(search_parts), "batch", scatter_dimension=1, tiled=True),
        lax.psum_scatter(flatten_blocks(pos_parts), "batch", scatter_dimension=1, tiled=True),
    )
    neg_rows, valid_total = lax.psum((neg_part, jnp.sum(valid_counts).astype(jnp.float32)), "batch")
    pooled_watch = (watch_sum / bag_size).astype(jnp.bfloat16)
    pooled_search = (search_sum / bag_size).astype(jnp.bfloat16)
    pos_bf = pos_rows.astype(jnp.bfloat16)
    neg_bf = neg_rows.astype(jnp.bfloat16)
    count_here = valid_counts[0]
    full_watch, full_search, full_pos, full_neg = (
        lax.all_gather(pooled_watch, "col", axis=0, tiled=True),
        lax.all_gather(pooled_search, "col", axis=0, tiled=True),
        lax.all_gather(pos_bf, "col", axis=0, tiled=True),
        lax.all_gather(neg_bf, "col", axis=0, tiled=True),
    )
    watch_rows = full_watch.T
    search_rows = full_search.T
    pos_full = full_pos.T
    live_rows = jnp.arange(row_count) < count_here
    weight = jnp.where(live_rows, 1.0 / valid_total, 0.0)
    buckets = demo_table.shape[0]
    bucket_counts = jnp.sum(
        (demo_ids[:, :, None] == jnp.arange(buckets)[None, None, :]).astype(jnp.float32), axis=1
    ).astype(jnp.bfloat16)
    demo_vec = jnp.dot(bucket_counts, demo_table, preferred_element_type=jnp.float32)
    joined = jnp.concatenate([watch_rows, search_rows, demo_vec.astype(jnp.bfloat16)], axis=1)
    pre_first = jnp.dot(joined, w_first, preferred_element_type=jnp.float32) + b_first
    act_first = jax.nn.gelu(pre_first).astype(jnp.bfloat16)
    pre_second = jnp.dot(act_first, w_second, preferred_element_type=jnp.float32) + b_second
    act_second = jax.nn.gelu(pre_second).astype(jnp.bfloat16)
    user_block = (
        jnp.dot(act_second, w_third, preferred_element_type=jnp.float32) + b_third
    ).astype(jnp.bfloat16)
    neg_logits = jnp.dot(user_block, full_neg, preferred_element_type=jnp.float32)
    pos_logit = jnp.sum(user_block.astype(jnp.float32) * pos_full.astype(jnp.float32), axis=1)
    row_peak = jnp.maximum(jnp.max(neg_logits, axis=1), pos_logit)
    exp_neg = jnp.exp(neg_logits - row_peak[:, None])
    exp_pos = jnp.exp(pos_logit - row_peak)
    row_total = jnp.sum(exp_neg, axis=1) + exp_pos
    lse = row_peak + jnp.log(row_total)
    loss_here = jnp.sum(weight * (lse - pos_logit))
    grad_neg = (weight[:, None] * exp_neg / row_total[:, None]).astype(jnp.bfloat16)
    grad_pos = (weight * (exp_pos / row_total - 1.0)).astype(jnp.bfloat16)
    grad_user = (
        contract_cols(grad_neg, full_neg)
        + grad_pos.astype(jnp.float32)[:, None] * pos_full.astype(jnp.float32)
    ).astype(jnp.bfloat16)
    neg_row_grad = contract_rows(user_block, grad_neg)
    pos_row_grad = (grad_pos.astype(jnp.float32)[:, None] * user_block.astype(jnp.float32)).astype(
        jnp.bfloat16
    )
    grad_w_third = contract_rows(act_second, grad_user)
    grad_b_third = jnp.sum(grad_user.astype(jnp.float32), axis=0)
    grad_pre_second = gelu_back(pre_second, contract_cols(grad_user, w_third)).astype(jnp.bfloat16)
    grad_w_second = contract_rows(act_first, grad_pre_second)
    grad_b_second = jnp.sum(grad_pre_second.astype(jnp.float32), axis=0)
    grad_pre_first = gelu_back(pre_first, contract_cols(grad_pre_second, w_second)).astype(
        jnp.bfloat16
    )
    grad_w_first = contract_rows(joined, grad_pre_first)
    grad_b_first = jnp.sum(grad_pre_first.astype(jnp.float32), axis=0)
    grad_joined = contract_cols(grad_pre_first, w_first).astype(jnp.bfloat16)
    grad_pw = grad_joined[:, :embed_width]
    grad_ps = grad_joined[:, embed_width : 2 * embed_width]
    grad_demo = contract_rows(bucket_counts, grad_joined[:, 2 * embed_width :])
    col_start = col_slot * col_width
    own_pw = lax.dynamic_slice_in_dim(grad_pw, col_start, col_width, 1).T
    own_ps = lax.dynamic_slice_in_dim(grad_ps, col_start, col_width, 1).T
    own_pos = lax.dynamic_slice_in_dim(pos_row_grad, col_start, col_width, 1).T
    user_vecs = lax.dynamic_slice_in_dim(user_block, col_slot * quarter, quarter, 0)
    all_pw, all_ps, all_dpos = (
        lax.all_gather(own_pw, "batch", axis=1, tiled=True),
        lax.all_gather(own_ps, "batch", axis=1, tiled=True),
        lax.all_gather(own_pos, "batch", axis=1, tiled=True),
    )
    neg_own = lax.dynamic_slice_in_dim(neg_row_grad, col_slot * col_width, col_width, 0)
    sums_out = lax.psum(
        (
            grad_w_first,
            grad_b_first,
            grad_w_second,
            grad_b_second,
            grad_w_third,
            grad_b_third,
            grad_demo,
            neg_own,
            loss_here,
        ),
        "batch",
    )
    neg_sum_own = sums_out[7]

    def split_blocks(columns):
        return columns.reshape(col_width, block_count, block_rows).transpose(1, 0, 2)

    def grad_block(running, inputs_block):
        watch_block, search_block, pos_block, block_pw, block_ps, block_pos = inputs_block
        new_watch = running[0] + jnp.dot(
            block_pw, bag_counts(watch_block), preferred_element_type=jnp.float32
        )
        new_search = running[1] + jnp.dot(
            block_ps, bag_counts(search_block), preferred_element_type=jnp.float32
        )
        new_out = running[2] + jnp.dot(
            block_pos, single_hot(pos_block), preferred_element_type=jnp.float32
        )
        return ((new_watch, new_search, new_out), None)

    zeros_table = jnp.zeros((col_width, vocab_rows), jnp.float32)
    (table_watch, table_search, table_out), _ = lax.scan(
        grad_block,
        (zeros_table, zeros_table, zeros_table),
        id_blocks + (split_blocks(all_pw), split_blocks(all_ps), split_blocks(all_dpos)),
    )
    neg_added = (
        jnp.zeros((col_width, vocab_rows + 1), jnp.float32).at[:, neg_local].add(neg_sum_own)
    )
    table_out = table_out + neg_added[:, :vocab_rows]
    return (
        user_vecs,
        sums_out[8],
        table_watch / bag_size,
        table_search / bag_size,
        table_out,
        sums_out[6],
        sums_out[0],
        sums_out[1],
        sums_out[2],
        sums_out[3],
        sums_out[4],
        sums_out[5],
    )


F32, BF16, FP8, I32 = jnp.float32, jnp.bfloat16, jnp.float8_e4m3fn, jnp.int32
MESH = pl.DeviceIdType.MESH
LOW = 256
ROWS_IN_GROUP = 4
BAG_PAD = 64
CHUNK = 256
NEG_FLOOR = -1e30


def dot_as(left, right, left_dim, right_dim):
    return lax.dot_general(
        left, right, (((left_dim,), (right_dim,)), ((), ())), preferred_element_type=F32
    )


def iota(shape, dim):
    return lax.broadcasted_iota(I32, shape, dim)


def one_where(mask, kind):
    return jnp.where(mask, jnp.ones((), BF16), jnp.zeros((), BF16)).astype(kind)


def slot_cap(neg_count, batch):
    mean = neg_count / batch
    return int(math.ceil((mean + 4.5 * math.sqrt(mean)) / 128.0)) * 128


def gelu_and_slope(pre):
    inner_scale = math.sqrt(2.0 / math.pi)
    square = pre * pre
    bent = jnp.tanh(inner_scale * (pre + 0.044715 * (square * pre)))
    value = 0.5 * pre * (1.0 + bent)
    slope = 0.5 * (1.0 + bent) + 0.5 * pre * (1.0 - bent * bent) * (
        inner_scale * (1.0 + 3.0 * 0.044715 * square)
    )
    return value, slope


def spread_matrix(rows):
    shape = (rows, 4 * rows)
    r, m = iota(shape, 0), iota(shape, 1)
    groups = rows // ROWS_IN_GROUP
    return one_where((r % groups == m // 16) & (r // groups == m % ROWS_IN_GROUP), BF16)


class Sizes:
    def __init__(self, batch, col, rows, bag, width, vocab, negs, embed):
        self.batch, self.col, self.rows, self.bag = batch, col, rows, bag
        self.width, self.vocab, self.negs, self.embed = width, vocab, negs, embed
        self.total = batch * rows
        self.quarter = rows // col
        self.users = batch * self.quarter
        self.groups = rows // ROWS_IN_GROUP
        self.high = vocab // LOW
        self.high_parts = self.high // 4
        self.cap = slot_cap(negs, batch)
        self.neg_rows = -(-negs // CHUNK)
        self.neg_pad = -(-self.neg_rows // 16) * 16


def front_kernel(
    sz,
    watch_ids, search_ids, extra, neg_ids, demo_table, b_first, b_second, b_third, w_demo,
    watch_table, search_table, out_table, w_first, w_second, w_third,
    watch_counts, search_counts, x_out, act1_out, slope1_out, act2_out, slope2_out, gu_out,
    buckets_out, neg_rows_out, pos_rows_out, slots_out, pos_out, user_out, small_out,
    tabs, mix, w1, w2, w3, ids, neg_dest, neg_digits, counts, sums, pieces, x, acts1, slopes1,
    acts2, slopes2, users, buckets, neg_own, neg_all, pos_own, pos_all, e_cols, e_rows, probs,
    stats, g_send, g_recv, gu, rg_send, rg_recv, loss_all,
    local_sem, out_sem, count_sem, ids_s, ids_r, rs_s, rs_r, ag_s, ag_r, xx_s, xx_r, co_s, co_r,
    ne_s, ne_r, pe_s, pe_r, st_s, st_r, gs_s, gs_r, ga_s, ga_r, gx_s, gx_r, gc_s, gc_r,
    rg_s, rg_r, lo_s, lo_r,
):
    b, c = lax.axis_index("batch"), lax.axis_index("col")
    nb, nc = sz.batch, sz.col
    offset = b * sz.vocab
    cap, width, embed = sz.cap, sz.width, sz.embed
    cx = lax.rem(c + 2, nc)
    ck = c + 1 - 2 * lax.rem(c, 2)

    def batch_peer(i):
        return lax.rem(b + i, nb)

    def batch_from(i):
        return lax.rem(b + nb - i, nb)

    def col_peer(i):
        return lax.rem(c + i, nc)

    def col_from(i):
        return lax.rem(c + nc - i, nc)

    def send(src, dst, ssem, rsem, to):
        return pltpu.make_async_remote_copy(
            src_ref=src, dst_ref=dst, send_sem=ssem, recv_sem=rsem,
            device_id=to, device_id_type=MESH,
        )

    barrier = pltpu.get_barrier_semaphore()
    for i in range(1, nb):
        pl.semaphore_signal(barrier, inc=1, device_id=(batch_peer(i), c), device_id_type=MESH)
    for i in range(1, nc):
        pl.semaphore_signal(barrier, inc=1, device_id=(b, col_peer(i)), device_id_type=MESH)

    loads = [
        (out_table, tabs.at[2]), (watch_table, tabs.at[0]), (search_table, tabs.at[1]),
        (w_second, w2), (w_third, w3), (w_demo, w1.at[pl.ds(nc * 128, 128)]),
    ]
    for i in range(nc):
        loads.append((w_first.at[pl.ds(i * width, width)], w1.at[pl.ds(i * 128, width)]))
        loads.append((w_first.at[pl.ds(embed + i * width, width)], w1.at[pl.ds(i * 128 + width, width)]))
    loads = [pltpu.make_async_copy(s, d, local_sem.at[i]) for i, (s, d) in enumerate(loads)]
    for load in loads:
        load.start()

    packed = (watch_ids[...] & 0xFFFF) | (search_ids[...] << 16)
    zero_ids = jnp.zeros((sz.groups + 8, CHUNK), I32)
    ids[b] = zero_ids
    for r4 in range(ROWS_IN_GROUP):
        ids[b, 0 : sz.groups, r4 * BAG_PAD : r4 * BAG_PAD + sz.bag] = packed[
            r4 * sz.groups : (r4 + 1) * sz.groups, :
        ]
    ids[b, sz.groups : sz.groups + 8, 0:128] = extra[...]

    pl.semaphore_wait(barrier, nb - 1 + nc - 1)
    ids_sends = []
    for i in range(1, nb):
        copy = send(ids.at[b], ids.at[b], ids_s.at[i - 1], ids_r.at[i - 1], (batch_peer(i), c))
        copy.start()
        ids_sends.append(copy)

    negs = neg_ids[...]
    neg_local = negs - offset
    own = (neg_local >= 0) & (neg_local < sz.vocab)
    own_bf = one_where(own, BF16)
    pads = sz.neg_pad
    upper = one_where(iota((CHUNK, CHUNK), 0) < iota((CHUNK, CHUNK), 1), BF16)
    before = dot_as(own_bf, upper, 1, 0)
    in_row = dot_as(own_bf, jnp.ones((CHUNK, CHUNK), BF16), 1, 0)
    lower = one_where(iota((pads, pads), 1) < iota((pads, pads), 0), BF16)
    rows_before = dot_as(lower, in_row.astype(BF16), 1, 0)
    neg_dest[...] = jnp.where(own, before + rows_before, -1.0)
    owned_count = dot_as(jnp.ones((8, pads), BF16), in_row.astype(BF16), 1, 0)
    most = jnp.zeros((1, 1), F32)
    for shard in range(nb):
        part = negs - shard * sz.vocab
        hits = jnp.where((part >= 0) & (part < sz.vocab), 1.0, 0.0)
        most = jnp.maximum(most, jnp.sum(jnp.sum(hits, axis=1, keepdims=True), axis=0, keepdims=True))
    for digit in range(4):
        neg_digits[digit] = ((neg_local >> (4 * digit)) & 15).astype(F32)

    def compact(k, total):
        place = neg_dest[pl.ds(k, 1), :]
        hot = one_where(place == iota((cap, CHUNK), 0).astype(F32), FP8)
        line = iota((32, CHUNK), 0)
        value = jnp.where(line == 4, 1.0, 0.0)
        for digit in range(4):
            value = jnp.where(line == digit, neg_digits[digit, pl.ds(k, 1), :], value)
        return total + dot_as(value.astype(FP8), hot, 1, 1)

    slot = lax.fori_loop(0, sz.neg_rows, compact, jnp.zeros((32, cap), F32))
    neg_low = slot[0:1] + 16.0 * slot[1:2]
    neg_high = jnp.where(slot[4:5] > 0.5, slot[2:3] + 16.0 * slot[3:4], -1.0)

    def pick_columns(high_row, low_row, count):
        low_hot = one_where(low_row.astype(BF16) == iota((LOW, count), 0).astype(BF16), BF16)

        def part(hq, total):
            base = pl.multiple_of(hq * 4 * LOW, 4 * LOW)
            left = jnp.concatenate(
                [tabs[2, :, pl.ds(base + i * LOW, LOW)] for i in range(4)], axis=0
            )
            got = dot_as(left, low_hot, 1, 0)
            for i in range(4):
                at = (hq * 4 + i).astype(F32)
                total = total + jnp.where(high_row == at, got[i * width : (i + 1) * width], 0.0)
            return total

        return lax.fori_loop(0, sz.high_parts, part, jnp.zeros((width, count), F32)).astype(BF16)

    loads[0].wait()
    neg_own[...] = pick_columns(neg_high, neg_low, cap)
    neg_all[c] = neg_own[...]
    e_sends = []
    for i in range(1, nc):
        copy = send(neg_own, neg_all.at[c], ne_s.at[i - 1], ne_r.at[i - 1], (b, col_peer(i)))
        copy.start()
        e_sends.append(copy)

    for t in range(2):
        loads[1 + t].wait()

        def turn(hh, _):
            base = pl.multiple_of(hh * 4 * LOW, 4 * LOW)
            tall = jnp.concatenate([tabs[t, :, pl.ds(base + i * LOW, LOW)] for i in range(4)], axis=0)
            mix[t, pl.ds(pl.multiple_of(hh * LOW, LOW), LOW), :] = tall.T
            return 0

        lax.fori_loop(0, sz.high_parts, turn, 0)

    for i in range(1, nb):
        src = batch_from(i)
        send(ids.at[src], ids.at[src], ids_s.at[i - 1], ids_r.at[i - 1], (b, c)).wait_recv()

    pos_ids = jnp.concatenate([ids[j, sz.groups : sz.groups + 1, 0:128] for j in range(nb)], axis=0)
    valid = jnp.concatenate([ids[j, sz.groups + 1 : sz.groups + 2, 0:128] for j in range(nb)], axis=0)
    pos_local = pos_ids - offset
    pos_owned = (pos_local >= 0) & (pos_local < sz.vocab)
    pos_pair = jnp.concatenate(
        [
            jnp.where(pos_owned, pos_local >> 8, 255).astype(F32),
            (pos_local & 255).astype(F32),
        ],
        axis=0,
    ).astype(BF16)
    shape = (128, sz.total)
    lane = iota(shape, 1)
    pick = one_where(
        iota(shape, 0) == (lane // sz.users) * sz.quarter + lane % sz.quarter, BF16
    )
    pos_wide = dot_as(pos_pair, pick, 1, 0)
    shape = (nb, sz.total)
    at_block = (iota(shape, 1) // sz.quarter) % nb == iota(shape, 0)
    pos_high = jnp.sum(jnp.where(at_block, pos_wide[0:nb], 0.0), axis=0, keepdims=True)
    pos_low = jnp.sum(jnp.where(at_block, pos_wide[nb : 2 * nb], 0.0), axis=0, keepdims=True)
    pos_high = jnp.where(pos_high > 254.0, -1.0, pos_high)

    slots_out[...] = jnp.concatenate([neg_high, neg_low, jnp.zeros((6, cap), F32)], axis=0)
    pos_out[...] = jnp.concatenate([pos_high, pos_low, jnp.zeros((6, sz.total), F32)], axis=0)

    for quarter in range(nc):
        lanes = slice(quarter * sz.users, (quarter + 1) * sz.users)
        pos_own[quarter] = pick_columns(pos_high[:, lanes], pos_low[:, lanes], sz.users)
    pos_all[c] = pos_own[c]
    for i in range(1, nc):
        to = col_peer(i)
        copy = send(pos_own.at[to], pos_all.at[c], pe_s.at[i - 1], pe_r.at[i - 1], (b, to))
        copy.start()
        e_sends.append(copy)

    shape = (nb, sz.users)
    user_block = iota(shape, 1) // sz.quarter == iota(shape, 0)
    valid_wide = jnp.concatenate([valid] * (sz.users // 128), axis=1).astype(F32)
    live_count = jnp.sum(jnp.where(user_block, valid_wide, 0.0), axis=0, keepdims=True)
    valid_total = jnp.sum(valid_wide, axis=0, keepdims=True)
    user_place = c * sz.quarter + iota((1, sz.users), 1) % sz.quarter
    weight = jnp.where(user_place.astype(F32) < live_count, 1.0 / valid_total, 0.0)

    bucket_total = jnp.zeros((demo_table.shape[0], sz.total), BF16)
    bucket_line = iota((demo_table.shape[0], sz.total), 0).astype(BF16)
    for field in range(4):
        row = sz.groups + 2 + field
        line = jnp.concatenate([ids[j, row : row + 1, 0:128] for j in range(nb)], axis=1)
        bucket_total = bucket_total + one_where(line.astype(F32).astype(BF16) == bucket_line, BF16)
    buckets[...] = bucket_total
    x[:, nc * 128 :] = dot_as(bucket_total, demo_table[...], 0, 0).astype(BF16)
    buckets_copy = pltpu.make_async_copy(buckets, buckets_out, out_sem.at[0])
    buckets_copy.start()

    for load in loads[3:]:
        load.wait()

    spread = spread_matrix(sz.rows)
    piece = sz.rows // nb
    block_lines = 4 * sz.rows
    lane_mod = iota((16, CHUNK), 1) % BAG_PAD
    lane_r4 = iota((16, CHUNK), 1) // BAG_PAD

    def count_copy(t, table, slot_at):
        out = (watch_counts, search_counts)[table]
        return pltpu.make_async_copy(counts.at[table, slot_at], out.at[t], count_sem.at[table, slot_at])

    def bag_block(t):
        slot_at = lax.rem(t, 2)
        results = []
        for table in range(2):

            @pl.when(t >= 2)
            def _():
                count_copy(t - 2, table, slot_at).wait()

            code_line = iota((4 * sz.high, CHUNK), 0).astype(BF16)
            low_line = iota((LOW, CHUNK), 0).astype(BF16)

            def groups_of(q, _):
                word = ids[t, pl.ds(pl.multiple_of(q * 16, 16), 16), :]
                value = (word & 0xFFFF) if table == 0 else lax.shift_right_logical(word, 16)
                local = value - offset
                mine = (local >= 0) & (local < sz.vocab) & (lane_mod < sz.bag)
                code = jnp.where(mine, (local >> 8) * 4 + lane_r4, -1).astype(F32).astype(BF16)
                low = (local & 255).astype(F32).astype(BF16)
                for g in range(16):
                    left = one_where(code[g : g + 1, :] == code_line, FP8)
                    right = one_where(low[g : g + 1, :] == low_line, FP8)
                    found = dot_as(left, right, 1, 1).astype(BF16)
                    line = pl.ds(pl.multiple_of(q * 256 + g * 16, 16), 16)
                    for hh in range(sz.high_parts):
                        counts[table, slot_at, line, hh * LOW : (hh + 1) * LOW] = found[
                            hh * 16 : (hh + 1) * 16, :
                        ]
                return 0

            lax.fori_loop(0, sz.groups // 16, groups_of, 0)
            count_copy(t, table, slot_at).start()
            total = dot_as(counts[table, slot_at], mix[table], 1, 0)
            shape = (block_lines, 4 * width)
            total = jnp.where((iota(shape, 0) // 4) % 4 == iota(shape, 1) // width, total, 0.0)
            half = total[:, :128] + total[:, 128:]
            half = half + pltpu.roll(half, width, 1)
            top = half.astype(BF16)
            rest = (half - top.astype(F32)).astype(BF16)
            both = jnp.where(iota((block_lines, 128), 1) < width, top, rest)
            found = dot_as(spread, both, 1, 0)
            results.append(found + pltpu.roll(found, width, 1))
        joined = jnp.where(iota((sz.rows, 128), 1) < width, results[0], results[1])
        sums[t] = joined.astype(BF16)
        for i in range(1, nb):
            to = batch_peer(i)
            send(
                sums.at[t, pl.ds(pl.multiple_of(to * piece, piece), piece)], pieces.at[t, i - 1],
                rs_s.at[t, i - 1], rs_r.at[t], (to, c),
            ).start()

    def x_at(t, col):
        return x.at[
            pl.ds(pl.multiple_of(t * sz.rows, sz.rows), sz.rows),
            pl.ds(pl.multiple_of(col * 128, 128), 128),
        ]

    def x_piece(t, owner):
        return x.at[
            pl.ds(pl.multiple_of(t * sz.rows + owner * piece, piece), piece),
            pl.ds(pl.multiple_of(c * 128, 128), 128),
        ]

    def reduce_block(t):
        send(pieces.at[t], pieces.at[t], rs_s.at[t, 0], rs_r.at[t], (b, c)).wait_recv()
        total = sums[t, pl.ds(pl.multiple_of(b * piece, piece), piece), :].astype(F32)
        for i in range(nb - 1):
            total = total + pieces[t, i].astype(F32)
        x[
            pl.ds(pl.multiple_of(t * sz.rows + b * piece, piece), piece),
            pl.ds(pl.multiple_of(c * 128, 128), 128),
        ] = (total / sz.bag).astype(BF16)
        for i in range(1, nb):
            send(x_piece(t, b), x_piece(t, b), ag_s.at[t, i - 1], ag_r.at[t], (batch_peer(i), c)).start()

    def cross_block(t):
        send(pieces.at[t], pieces.at[t], ag_s.at[t, 0], ag_r.at[t], (b, c)).wait_recv()
        send(x_at(t, c), x_at(t, c), xx_s.at[t], xx_r.at[t], (b, cx)).start()

    def core_block(t):
        send(x_at(t, cx), x_at(t, cx), xx_s.at[t], xx_r.at[t], (b, cx)).wait_recv()
        send(x_at(t, c), x_at(t, c), co_s.at[t, 0], co_r.at[t, 0], (b, ck)).start()
        send(x_at(t, cx), x_at(t, cx), co_s.at[t, 1], co_r.at[t, 1], (b, ck)).start()

    def full_block(t):
        ckx = lax.rem(ck + 2, nc)
        send(x_at(t, ck), x_at(t, ck), co_s.at[t, 0], co_r.at[t, 0], (b, ck)).wait_recv()
        send(x_at(t, ckx), x_at(t, ckx), co_s.at[t, 1], co_r.at[t, 1], (b, ck)).wait_recv()

    tower_rows = sz.total // 4

    def tower(k):
        at = pl.ds(pl.multiple_of(k * tower_rows, tower_rows), tower_rows)
        pre = dot_as(x[at, :], w1[...], 1, 0) + b_first[...]
        value, slope = gelu_and_slope(pre)
        value = value.astype(BF16)
        acts1[at, :] = value
        slopes1[at, :] = slope.astype(BF16)
        pre = dot_as(value, w2[...], 1, 0) + b_second[...]
        value, slope = gelu_and_slope(pre)
        value = value.astype(BF16)
        acts2[at, :] = value
        slopes2[at, :] = slope.astype(BF16)
        users[at, :] = (dot_as(value, w3[...], 1, 0) + b_third[...]).astype(BF16)

    def step(t, _):
        @pl.when(t < nb)
        def _():
            bag_block(t)

        @pl.when((t >= 1) & (t < nb + 1))
        def _():
            reduce_block(t - 1)

        @pl.when((t >= 2) & (t < nb + 2))
        def _():
            cross_block(t - 2)

        @pl.when((t >= 3) & (t < nb + 3))
        def _():
            core_block(t - 3)

        @pl.when(t >= 4)
        def _():
            full_block(t - 4)

        @pl.when(t >= nb)
        def _():
            tower(t - nb)

        return 0

    lax.fori_loop(0, nb + 4, step, 0)

    out_copies = [(x, x_out), (acts1, act1_out), (slopes1, slope1_out), (acts2, act2_out), (slopes2, slope2_out)]
    out_copies = [pltpu.make_async_copy(s, d, out_sem.at[1 + i]) for i, (s, d) in enumerate(out_copies)]
    for copy in out_copies:
        copy.start()
    user_out[...] = users[pl.ds(pl.multiple_of(b * sz.rows + c * sz.quarter, sz.quarter), sz.quarter), :]

    for i in range(1, nc):
        src = col_from(i)
        send(neg_all.at[src], neg_all.at[src], ne_s.at[i - 1], ne_r.at[i - 1], (b, c)).wait_recv()
        send(pos_all.at[src], pos_all.at[src], pe_s.at[i - 1], pe_r.at[i - 1], (b, c)).wait_recv()
    for i in range(nc):
        e_cols[i * width : (i + 1) * width, 0:cap] = neg_all[i]
        e_cols[i * width : (i + 1) * width, cap:] = pos_all[i]
    e_rows[...] = e_cols[...].T

    quarter_users = jnp.concatenate(
        [
            users[pl.ds(pl.multiple_of(j * sz.rows + c * sz.quarter, sz.quarter), sz.quarter), :]
            for j in range(nb)
        ],
        axis=0,
    )
    logits = dot_as(e_rows[...], quarter_users, 1, 1)
    neg_logits, pos_logits = logits[0:cap], logits[cap:]
    slot_ok = iota((cap, sz.users), 0).astype(F32) < owned_count[0:1, : sz.users]
    pos_here = jnp.zeros((1, sz.users), F32)
    for quarter in range(nc):
        pos_here = jnp.where(c == quarter, pos_high[:, quarter * sz.users : (quarter + 1) * sz.users], pos_here)
    pos_ok = (iota((sz.users, sz.users), 0) == iota((sz.users, sz.users), 1)) & (pos_here >= 0.0)
    neg_logits = jnp.where(slot_ok, neg_logits, NEG_FLOOR)
    pos_masked = jnp.where(pos_ok, pos_logits, NEG_FLOOR)
    peak = jnp.maximum(
        jnp.max(neg_logits, axis=0, keepdims=True), jnp.max(pos_masked, axis=0, keepdims=True)
    )
    mass = jnp.sum(jnp.where(slot_ok, jnp.exp(neg_logits - peak), 0.0), axis=0, keepdims=True) + jnp.sum(
        jnp.where(pos_ok, jnp.exp(pos_masked - peak), 0.0), axis=0, keepdims=True
    )
    pos_value = jnp.sum(jnp.where(pos_ok, pos_logits, 0.0), axis=0, keepdims=True)
    stats[b] = jnp.concatenate([peak, mass, pos_value, jnp.zeros((5, sz.users), F32)], axis=0)
    st_sends = []
    for i in range(1, nb):
        copy = send(stats.at[b], stats.at[b], st_s.at[i - 1], st_r.at[i - 1], (batch_peer(i), c))
        copy.start()
        st_sends.append(copy)
    for i in range(1, nb):
        src = batch_from(i)
        send(stats.at[src], stats.at[src], st_s.at[i - 1], st_r.at[i - 1], (b, c)).wait_recv()
    peaks = [stats[j, 0:1, :] for j in range(nb)]
    top = peaks[0]
    for j in range(1, nb):
        top = jnp.maximum(top, peaks[j])
    full_mass = jnp.zeros((1, sz.users), F32)
    pos_logit = jnp.zeros((1, sz.users), F32)
    for j in range(nb):
        full_mass = full_mass + stats[j, 1:2, :] * jnp.exp(peaks[j] - top)
        pos_logit = pos_logit + stats[j, 2:3, :]
    lse = top + jnp.log(full_mass)
    loss_part = jnp.sum(weight * (lse - pos_logit), axis=1, keepdims=True)
    scale = weight / full_mass
    neg_grad = jnp.where(slot_ok, jnp.exp(neg_logits - top) * scale, 0.0).astype(BF16)
    pos_grad = jnp.where(
        pos_ok, weight * (jnp.exp(pos_logit - top) / full_mass - 1.0), 0.0
    ).astype(BF16)
    probs[0:cap] = neg_grad
    probs[cap:] = pos_grad
    grad_user = dot_as(probs[...], e_rows[...], 0, 0)
    for j in range(nb):
        g_send[j] = grad_user[j * sz.quarter : (j + 1) * sz.quarter].astype(BF16)
    gs_sends = []
    for i in range(1, nb):
        to = batch_peer(i)
        copy = send(g_send.at[to], g_recv.at[i - 1], gs_s.at[i - 1], gs_r.at[i - 1], (to, c))
        copy.start()
        gs_sends.append(copy)
    loss_all[c] = jnp.broadcast_to(loss_part, (8, 128))
    for i in range(1, nc):
        copy = send(loss_all.at[c], loss_all.at[c], lo_s.at[i - 1], lo_r.at[i - 1], (b, col_peer(i)))
        copy.start()
        gs_sends.append(copy)
    rows_grad = dot_as(probs[...], quarter_users, 1, 0)
    rows_grad = rows_grad.T.astype(BF16)
    for i in range(nc):
        rg_send[i] = rows_grad[i * width : (i + 1) * width]
    for i in range(1, nb):
        send(g_send.at[0], g_recv.at[i - 1], gs_s.at[i - 1], gs_r.at[i - 1], (b, c)).wait_recv()
    total = g_send[b].astype(F32)
    for i in range(nb - 1):
        total = total + g_recv[i].astype(F32)
    mine_rows = pl.ds(pl.multiple_of(c * sz.quarter, sz.quarter), sz.quarter)
    gu[b, mine_rows, :] = total.astype(BF16)
    for i in range(1, nb):
        place = gu.at[b, mine_rows]
        copy = send(place, place, ga_s.at[i - 1], ga_r.at[i - 1], (batch_peer(i), c))
        copy.start()
        gs_sends.append(copy)
    for i in range(1, nc):
        to = col_peer(i)
        copy = send(rg_send.at[to], rg_recv.at[c], rg_s.at[i - 1], rg_r.at[i - 1], (b, to))
        copy.start()
        gs_sends.append(copy)
    rg_recv[c] = rg_send[c]
    for i in range(1, nb):
        place = gu.at[batch_from(i), mine_rows]
        send(place, place, ga_s.at[i - 1], ga_r.at[i - 1], (b, c)).wait_recv()

    def gu_at(col):
        return gu.at[:, pl.ds(pl.multiple_of(col * sz.quarter, sz.quarter), sz.quarter), :]

    copy = send(gu_at(c), gu_at(c), gx_s, gx_r, (b, cx))
    copy.start()
    gs_sends.append(copy)
    send(gu_at(cx), gu_at(cx), gx_s, gx_r, (b, cx)).wait_recv()
    for i, col in enumerate((c, cx)):
        copy = send(gu_at(col), gu_at(col), gc_s.at[i], gc_r.at[i], (b, ck))
        copy.start()
        gs_sends.append(copy)
    for i, col in enumerate((ck, lax.rem(ck + 2, nc))):
        send(gu_at(col), gu_at(col), gc_s.at[i], gc_r.at[i], (b, ck)).wait_recv()
    gu_copy = pltpu.make_async_copy(gu, gu_out, out_sem.at[6])
    gu_copy.start()

    loss = loss_all[c] * 1.0
    for i in range(1, nc):
        src = col_from(i)
        send(loss_all.at[src], loss_all.at[src], lo_s.at[i - 1], lo_r.at[i - 1], (b, c)).wait_recv()
        send(rg_recv.at[src], rg_recv.at[src], rg_s.at[i - 1], rg_r.at[i - 1], (b, c)).wait_recv()
    loss = loss_all[0]
    neg_total = rg_recv[0, :, 0:cap].astype(F32)
    for i in range(1, nc):
        loss = loss + loss_all[i]
        neg_total = neg_total + rg_recv[i, :, 0:cap].astype(F32)
    neg_rows_out[...] = neg_total.astype(BF16)
    for i in range(nc):
        pos_rows_out[:, i * sz.users : (i + 1) * sz.users] = rg_recv[i, :, cap:]
    fits = jnp.where(most <= float(cap), 1.0, 0.0)
    line = iota((8, 128), 0)
    small_out[...] = jnp.where(line == 0, loss, jnp.broadcast_to(fits, (8, 128)))

    for copy in ids_sends + e_sends + st_sends + gs_sends:
        copy.wait_send()

    def drain(t, _):
        for i in range(1, nb):
            send(sums.at[t, pl.ds(0, piece)], pieces.at[t, 0], rs_s.at[t, i - 1], rs_r.at[t], (b, c)).wait_send()
            send(x_piece(t, b), x_piece(t, b), ag_s.at[t, i - 1], ag_r.at[t], (b, c)).wait_send()
        send(x_at(t, c), x_at(t, c), xx_s.at[t], xx_r.at[t], (b, cx)).wait_send()
        send(x_at(t, c), x_at(t, c), co_s.at[t, 0], co_r.at[t, 0], (b, ck)).wait_send()
        send(x_at(t, cx), x_at(t, cx), co_s.at[t, 1], co_r.at[t, 1], (b, ck)).wait_send()
        return 0

    lax.fori_loop(0, nb, drain, 0)
    for table in range(2):
        count_copy(nb - 2, table, nb % 2).wait()
        count_copy(nb - 1, table, (nb - 1) % 2).wait()
    buckets_copy.wait()
    gu_copy.wait()
    for copy in out_copies:
        copy.wait()


def front(sz, args):
    nb, nc, total = sz.batch, sz.col, sz.total
    width, embed, cap, users = sz.width, sz.embed, sz.cap, sz.users
    slots = cap + users
    first, second = args["w_second"].shape
    buckets = args["demo_table"].shape[0]
    x_width = nc * 128 + 128
    lines = 4 * sz.rows
    vmem = pl.BlockSpec(memory_space=pltpu.VMEM)
    hbm = pl.BlockSpec(memory_space=pl.ANY)
    dma = pltpu.SemaphoreType.DMA
    count_shape = jax.ShapeDtypeStruct((nb, lines, sz.high_parts * LOW), BF16)

    def shape(dims, kind=BF16):
        return jax.ShapeDtypeStruct(dims, kind)

    outs = [
        (count_shape, hbm), (count_shape, hbm), (shape((total, x_width)), hbm),
        (shape((total, first)), hbm), (shape((total, first)), hbm),
        (shape((total, second)), hbm), (shape((total, second)), hbm),
        (shape((nb, sz.rows, embed)), hbm), (shape((buckets, total)), hbm),
        (shape((width, cap)), vmem), (shape((width, total)), vmem),
        (shape((8, cap), F32), vmem), (shape((8, total), F32), vmem),
        (shape((sz.quarter, embed)), vmem), (shape((8, 128), F32), vmem),
    ]
    scratch = [
        pltpu.VMEM((3, width, sz.vocab), BF16),
        pltpu.VMEM((2, sz.high_parts * LOW, 4 * width), BF16),
        pltpu.VMEM((x_width, first), BF16),
        pltpu.VMEM((first, second), BF16),
        pltpu.VMEM((second, embed), BF16),
        pltpu.VMEM((nb, sz.groups + 8, CHUNK), I32),
        pltpu.VMEM((sz.neg_pad, CHUNK), F32),
        pltpu.VMEM((4, sz.neg_pad, CHUNK), F32),
        pltpu.VMEM((2, 2, lines, sz.high_parts * LOW), BF16),
        pltpu.VMEM((nb, sz.rows, 128), BF16),
        pltpu.VMEM((nb, nb - 1, sz.rows // nb, 128), BF16),
        pltpu.VMEM((total, x_width), BF16),
        pltpu.VMEM((total, first), BF16),
        pltpu.VMEM((total, first), BF16),
        pltpu.VMEM((total, second), BF16),
        pltpu.VMEM((total, second), BF16),
        pltpu.VMEM((total, embed), BF16),
        pltpu.VMEM((buckets, total), BF16),
        pltpu.VMEM((width, cap), BF16),
        pltpu.VMEM((nc, width, cap), BF16),
        pltpu.VMEM((nc, width, users), BF16),
        pltpu.VMEM((nc, width, users), BF16),
        pltpu.VMEM((embed, slots), BF16),
        pltpu.VMEM((slots, embed), BF16),
        pltpu.VMEM((slots, users), BF16),
        pltpu.VMEM((nb, 8, users), F32),
        pltpu.VMEM((nb, sz.quarter, embed), BF16),
        pltpu.VMEM((nb - 1, sz.quarter, embed), BF16),
        pltpu.VMEM((nb, sz.rows, embed), BF16),
        pltpu.VMEM((nc, width, slots), BF16),
        pltpu.VMEM((nc, width, slots), BF16),
        pltpu.VMEM((nc, 8, 128), F32),
        dma((6 + 2 * nc,)), dma((7,)), dma((2, 2)),
        dma((nb - 1,)), dma((nb - 1,)),
        dma((nb, nb - 1)), dma((nb,)), dma((nb, nb - 1)), dma((nb,)),
        dma((nb,)), dma((nb,)), dma((nb, 2)), dma((nb, 2)),
        dma((nc - 1,)), dma((nc - 1,)), dma((nc - 1,)), dma((nc - 1,)),
        dma((nb - 1,)), dma((nb - 1,)), dma((nb - 1,)), dma((nb - 1,)),
        dma((nb - 1,)), dma((nb - 1,)), dma, dma, dma((2,)), dma((2,)),
        dma((nc - 1,)), dma((nc - 1,)), dma((nc - 1,)), dma((nc - 1,)),
    ]
    rows = args["watch_ids"].shape[0]
    extra = jnp.concatenate(
        [
            args["pos_ids"][None, :],
            jnp.broadcast_to(args["valid_counts"][:, None], (1, rows)),
            args["demo_ids"].T,
            jnp.zeros((8 - 2 - args["demo_ids"].shape[1], rows), I32),
        ],
        axis=0,
    )
    pad = sz.neg_pad * CHUNK - sz.negs
    negs = jnp.concatenate([args["neg_ids"], jnp.full((pad,), -1, I32)]).reshape(sz.neg_pad, CHUNK)
    demo_width = args["demo_table"].shape[1]
    demo = jnp.pad(args["demo_table"], ((0, 0), (0, 128 - demo_width)))
    w_demo = jnp.pad(args["w_first"][2 * embed :], ((0, 128 - demo_width), (0, 0)))
    operands = [
        (args["watch_ids"], vmem), (args["search_ids"], vmem), (extra, vmem), (negs, vmem), (demo, vmem),
        (args["b_first"][None, :], vmem), (args["b_second"][None, :], vmem), (args["b_third"][None, :], vmem),
        (w_demo, hbm), (args["watch_table"], hbm), (args["search_table"], hbm), (args["out_table"], hbm),
        (args["w_first"], hbm), (args["w_second"], hbm), (args["w_third"], hbm),
    ]
    return pl.pallas_call(
        functools.partial(front_kernel, sz),
        out_shape=[o for o, _ in outs],
        in_specs=[s for _, s in operands],
        out_specs=[s for _, s in outs],
        scratch_shapes=scratch,
        compiler_params=pltpu.CompilerParams(
            collective_id=0, has_side_effects=True, vmem_limit_bytes=60 * 2**20
        ),
        name="front",
    )(*[o for o, _ in operands])


def back_kernel(
    sz, grads, neg_rows, pos_rows, slots, pos, watch_counts, search_counts,
    watch_out, search_out, table_out, spread_grads, chunk, lines, in_sem, out_sem,
):
    width, cap, total = sz.width, sz.cap, sz.total
    parts, nb = sz.high_parts, sz.batch
    outs = (watch_out, search_out)
    ins = (watch_counts, search_counts)
    depth = 3

    def load(n):
        table, hh = n // parts, n % parts
        source = ins[table].at[:, :, pl.ds(hh * LOW, LOW)]
        return pltpu.make_async_copy(source, chunk.at[n % depth], in_sem.at[n % depth])

    def store(n):
        out = outs[n // parts] if n < 2 * parts else table_out
        hh = n % parts
        return pltpu.make_async_copy(
            lines.at[n % 2], out.at[:, pl.ds(hh * 4 * LOW, 4 * LOW)], out_sem.at[n % 2]
        )

    for n in range(depth):
        load(n).start()

    spread = spread_matrix(sz.rows)
    shape = (4 * width, 4 * sz.rows)
    mask = iota(shape, 0) // width == (iota(shape, 1) // 4) % 4
    for table in range(2):
        for t in range(nb):
            part = grads[t * sz.rows : (t + 1) * sz.rows, table * width : (table + 1) * width]
            wide = jnp.concatenate([part] * 4, axis=1)
            laid = dot_as(wide, spread, 0, 0)
            spread_grads[table, :, t * 4 * sz.rows : (t + 1) * 4 * sz.rows] = jnp.where(
                mask, laid, 0.0
            ).astype(BF16)

    def put(n, found, factor):
        if n >= 2:
            store(n - 2).wait()
        for i in range(4):
            lines[n % 2, :, i * LOW : (i + 1) * LOW] = found[i * width : (i + 1) * width] * factor
        store(n).start()

    for n in range(2 * parts):
        table = n // parts
        load(n).wait()
        stacked = chunk[n % depth].reshape(nb * 4 * sz.rows, LOW)
        found = dot_as(spread_grads[table], stacked, 1, 0)
        if n + depth < 2 * parts:
            load(n + depth).start()
        put(n, found, 1.0 / sz.bag)

    high = jnp.concatenate([slots[0:1, :], pos[0:1, :]], axis=1)
    low = jnp.concatenate([slots[1:2, :], pos[1:2, :]], axis=1)
    values = jnp.concatenate([neg_rows[...], pos_rows[...]], axis=1)
    low_hot = one_where(low.astype(BF16) == iota((LOW, cap + total), 0).astype(BF16), BF16)
    for hh in range(parts):
        left = jnp.concatenate(
            [jnp.where(high == float(hh * 4 + i), values, jnp.zeros((), BF16)) for i in range(4)], axis=0
        )
        put(2 * parts + hh, dot_as(left, low_hot, 1, 1), 1.0)
    store(3 * parts - 2).wait()
    store(3 * parts - 1).wait()


def back(sz, grads, neg_rows, pos_rows, slots, pos, watch_counts, search_counts):
    vmem = pl.BlockSpec(memory_space=pltpu.VMEM)
    hbm = pl.BlockSpec(memory_space=pl.ANY)
    table = jax.ShapeDtypeStruct((sz.width, sz.vocab), F32)
    lines = 4 * sz.rows
    return pl.pallas_call(
        functools.partial(back_kernel, sz),
        out_shape=[table] * 3,
        in_specs=[vmem] * 5 + [hbm] * 2,
        out_specs=[hbm] * 3,
        scratch_shapes=[
            pltpu.VMEM((2, 4 * sz.width, sz.batch * lines), BF16),
            pltpu.VMEM((3, sz.batch, lines, LOW), BF16),
            pltpu.VMEM((2, sz.width, 4 * LOW), F32),
            pltpu.SemaphoreType.DMA((3,)),
            pltpu.SemaphoreType.DMA((2,)),
        ],
        compiler_params=pltpu.CompilerParams(vmem_limit_bytes=56 * 2**20),
        name="back",
    )(grads, neg_rows, pos_rows, slots, pos, watch_counts, search_counts)


def fast_device(sz, *inputs):
    names = (
        "watch_ids", "search_ids", "demo_ids", "pos_ids", "neg_ids", "valid_counts", "watch_table",
        "search_table", "demo_table", "out_table", "w_first", "b_first", "w_second", "b_second",
        "w_third", "b_third",
    )
    args = dict(zip(names, inputs))
    (
        watch_counts, search_counts, x, act1, slope1, act2, slope2, gu, buckets,
        neg_rows, pos_rows, slots, pos, user_vecs, small,
    ) = front(sz, args)

    def finish(*operands):
        nc, width, embed, total = sz.col, sz.width, sz.embed, sz.total
        w_first, w_second, w_third = args["w_first"], args["w_second"], args["w_third"]
        demo_width = args["demo_table"].shape[1]
        start = lax.axis_index("col") * width
        gu_rows = gu.reshape(total, embed)
        grad_second = (contract_cols(gu_rows, w_third) * slope2.astype(F32)).astype(BF16)
        grad_first = (contract_cols(grad_second, w_second) * slope1.astype(F32)).astype(BF16)
        picked = jnp.concatenate(
            [
                lax.dynamic_slice_in_dim(w_first, start, width, 0),
                lax.dynamic_slice_in_dim(w_first, embed + start, width, 0),
                w_first[2 * embed :],
            ],
            axis=0,
        )
        grad_x = contract_cols(grad_first, picked).astype(BF16)
        tables = back(
            sz, grad_x[:, : 2 * width], neg_rows, pos_rows, slots, pos, watch_counts, search_counts
        )
        pairs = x[:, : nc * 128].reshape(total, nc, 2, width).transpose(0, 2, 1, 3)
        joined = jnp.concatenate(
            [pairs.reshape(total, 2 * embed), x[:, nc * 128 : nc * 128 + demo_width]], axis=1
        )
        grad_demo = jnp.dot(buckets, grad_x[:, 2 * width :], preferred_element_type=F32)
        return (
            user_vecs,
            small[0, 0],
            tables[0],
            tables[1],
            tables[2],
            grad_demo,
            contract_rows(joined, grad_first),
            jnp.sum(grad_first.astype(F32), axis=0),
            contract_rows(act1, grad_second),
            jnp.sum(grad_second.astype(F32), axis=0),
            contract_rows(act2, gu_rows),
            jnp.sum(gu_rows.astype(F32), axis=0),
        )

    def general(*operands):
        return per_device(*operands)

    return lax.cond(small[1, 0] > 0.5, finish, general, *inputs)


def fast_sizes(mesh, shapes):
    watch, demo, negs, table, first = shapes
    batch, col = mesh.shape["batch"], mesh.shape["col"]
    rows, width, vocab = watch[0] // batch, table[0] // col, table[1] // batch
    sz = Sizes(batch, col, rows, watch[1], width, vocab, negs[0], table[0])
    good = (
        batch == 8 and col == 4 and rows == 128 and watch[1] <= BAG_PAD and width == 64
        and vocab == 32 * LOW and table[1] <= 65536 and demo[1] <= 4 and first[0] <= 2 * table[0] + 128
        and negs[0] <= 256 * CHUNK
    )
    return sz if good else None


def solution(mesh):
    in_specs = (
        P("batch", None),
        P("batch", None),
        P("batch", None),
        P("batch"),
        P(),
        P("batch"),
        P("col", "batch"),
        P("col", "batch"),
        P(),
        P("col", "batch"),
        P(),
        P(),
        P(),
        P(),
        P(),
        P(),
    )
    out_specs = (
        P(("batch", "col"), None),
        P(),
        P("col", "batch"),
        P("col", "batch"),
        P("col", "batch"),
        P(),
        P(),
        P(),
        P(),
        P(),
        P(),
        P(),
    )

    def whole(*inputs):
        shapes = [inputs[i].shape for i in (0, 2, 4, 6, 10)]
        sz = fast_sizes(mesh, shapes)
        body = per_device if sz is None else functools.partial(fast_device, sz)
        return jax.shard_map(
            body, mesh=mesh, in_specs=in_specs, out_specs=out_specs, check_vma=False
        )(*inputs)

    return whole
```

```python
import functools
import math

import jax
import jax.numpy as jnp
from jax import lax
from jax.experimental import pallas as pl
from jax.experimental.pallas import tpu as pltpu
from jax.sharding import PartitionSpec as P


def contract_rows(left, right):
    return lax.dot_general(
        left, right, (((0,), (0,)), ((), ())), preferred_element_type=jnp.float32
    )


def contract_cols(left, right):
    return lax.dot_general(
        left, right, (((1,), (1,)), ((), ())), preferred_element_type=jnp.float32
    )


def gelu_back(pre_value, grad_value):
    return jax.vjp(jax.nn.gelu, pre_value)[1](grad_value)[0]


class Collectives:
    def gather(self, value, name, axis):
        return lax.all_gather(value, name, axis=axis, tiled=True)

    def scatter_sum(self, value, name, axis):
        return lax.psum_scatter(value, name, scatter_dimension=axis, tiled=True)

    def total(self, values, name):
        return lax.psum(values, name)


class RingCollectives:
    def shift(self, value, name):
        size = lax.axis_size(name)
        return lax.ppermute(value, name, [(i, (i + 1) % size) for i in range(size)])

    def stack(self, value, name):
        size, me = lax.axis_size(name), lax.axis_index(name)
        held = [value]
        for _ in range(size - 1):
            held.append(self.shift(held[-1], name))
        return jnp.take(jnp.stack(held), (me - jnp.arange(size)) % size, axis=0)

    def gather(self, value, name, axis):
        parts = self.stack(value, name)
        return jnp.concatenate([parts[i] for i in range(parts.shape[0])], axis=axis)

    def ring_sum(self, parts, name):
        size, me = lax.axis_size(name), lax.axis_index(name)
        held = jnp.take(parts, (me - 1) % size, axis=0)
        for step in range(1, size):
            held = self.shift(held, name) + jnp.take(parts, (me - 1 - step) % size, axis=0)
        return held

    def scatter_sum(self, value, name, axis):
        size = lax.axis_size(name)
        return self.ring_sum(jnp.stack(jnp.split(value, size, axis=axis)), name)

    def total(self, values, name):
        size = lax.axis_size(name)
        flat = jnp.concatenate([v.reshape(-1) for v in values])
        length = -(-flat.shape[0] // (size * 128)) * 128
        parts = jnp.pad(flat, (0, size * length - flat.shape[0])).reshape(size, length)
        whole = self.stack(self.ring_sum(parts, name), name).reshape(-1)
        out, at = [], 0
        for v in values:
            out.append(whole[at : at + v.size].reshape(v.shape))
            at += v.size
        return tuple(out)


def per_device(
    comm,
    watch_ids,
    search_ids,
    demo_ids,
    pos_ids,
    neg_ids,
    valid_counts,
    watch_table,
    search_table,
    demo_table,
    out_table,
    w_first,
    b_first,
    w_second,
    b_second,
    w_third,
    b_third,
):
    row_count = watch_ids.shape[0]
    bag_size = watch_ids.shape[1]
    col_width = watch_table.shape[0]
    vocab_rows = watch_table.shape[1]
    embed_width = col_width * lax.axis_size("col")
    offset = lax.axis_index("batch") * vocab_rows
    col_slot = lax.axis_index("col")
    quarter = row_count // lax.axis_size("col")
    low_width = math.gcd(vocab_rows, 128)
    high_width = vocab_rows // low_width

    def owned(id_values):
        local_ids = id_values - offset
        return jnp.where((local_ids >= 0) & (local_ids < vocab_rows), local_ids, vocab_rows)

    def bag_counts(id_block):
        local_ids = owned(id_block)
        high_hot = (
            local_ids[:, :, None] // low_width == jnp.arange(high_width)[None, None, :]
        ).astype(jnp.bfloat16)
        low_hot = (
            local_ids[:, :, None] % low_width == jnp.arange(low_width)[None, None, :]
        ).astype(jnp.bfloat16)
        counted = jnp.einsum("rbh,rbl->rhl", high_hot, low_hot, preferred_element_type=jnp.bfloat16)
        return counted.reshape(id_block.shape[0], vocab_rows)

    def single_hot(id_block):
        return (owned(id_block)[:, None] == jnp.arange(vocab_rows)[None, :]).astype(jnp.bfloat16)

    zero_col = jnp.zeros((col_width, 1), jnp.bfloat16)
    padded_out = jnp.concatenate([out_table, zero_col], axis=1)
    all_watch, all_search, all_pos = (
        comm.gather(watch_ids, "batch", 0),
        comm.gather(search_ids, "batch", 0),
        comm.gather(pos_ids, "batch", 0),
    )
    total_rows = all_watch.shape[0]
    block_rows = min(1024, total_rows)
    block_count = total_rows // block_rows
    neg_local = owned(neg_ids)
    neg_part = jnp.take(padded_out, neg_local, axis=1).astype(jnp.float32)

    def flatten_blocks(stacked):
        return stacked.transpose(1, 0, 2).reshape(col_width, total_rows)

    def bag_block(inputs_block):
        watch_block, search_block, pos_block = inputs_block
        watch_part = contract_cols(watch_table, bag_counts(watch_block))
        search_part = contract_cols(search_table, bag_counts(search_block))
        pos_part = contract_cols(out_table, single_hot(pos_block))
        return (watch_part, search_part, pos_part)

    id_blocks = (
        all_watch.reshape(block_count, block_rows, bag_size),
        all_search.reshape(block_count, block_rows, bag_size),
        all_pos.reshape(block_count, block_rows),
    )
    watch_parts, search_parts, pos_parts = lax.map(bag_block, id_blocks)
    watch_sum, search_sum, pos_rows = (
        comm.scatter_sum(flatten_blocks(watch_parts), "batch", 1),
        comm.scatter_sum(flatten_blocks(search_parts), "batch", 1),
        comm.scatter_sum(flatten_blocks(pos_parts), "batch", 1),
    )
    neg_rows, valid_total = comm.total(
        (neg_part, jnp.sum(valid_counts).astype(jnp.float32)), "batch"
    )
    pooled_watch = (watch_sum / bag_size).astype(jnp.bfloat16)
    pooled_search = (search_sum / bag_size).astype(jnp.bfloat16)
    pos_bf = pos_rows.astype(jnp.bfloat16)
    neg_bf = neg_rows.astype(jnp.bfloat16)
    count_here = valid_counts[0]
    full_watch, full_search, full_pos, full_neg = (
        comm.gather(pooled_watch, "col", 0),
        comm.gather(pooled_search, "col", 0),
        comm.gather(pos_bf, "col", 0),
        comm.gather(neg_bf, "col", 0),
    )
    watch_rows = full_watch.T
    search_rows = full_search.T
    pos_full = full_pos.T
    live_rows = jnp.arange(row_count) < count_here
    weight = jnp.where(live_rows, 1.0 / valid_total, 0.0)
    buckets = demo_table.shape[0]
    bucket_counts = jnp.sum(
        (demo_ids[:, :, None] == jnp.arange(buckets)[None, None, :]).astype(jnp.float32), axis=1
    ).astype(jnp.bfloat16)
    demo_vec = jnp.dot(bucket_counts, demo_table, preferred_element_type=jnp.float32)
    joined = jnp.concatenate([watch_rows, search_rows, demo_vec.astype(jnp.bfloat16)], axis=1)
    pre_first = jnp.dot(joined, w_first, preferred_element_type=jnp.float32) + b_first
    act_first = jax.nn.gelu(pre_first).astype(jnp.bfloat16)
    pre_second = jnp.dot(act_first, w_second, preferred_element_type=jnp.float32) + b_second
    act_second = jax.nn.gelu(pre_second).astype(jnp.bfloat16)
    user_block = (
        jnp.dot(act_second, w_third, preferred_element_type=jnp.float32) + b_third
    ).astype(jnp.bfloat16)
    neg_logits = jnp.dot(user_block, full_neg, preferred_element_type=jnp.float32)
    pos_logit = jnp.sum(user_block.astype(jnp.float32) * pos_full.astype(jnp.float32), axis=1)
    row_peak = jnp.maximum(jnp.max(neg_logits, axis=1), pos_logit)
    exp_neg = jnp.exp(neg_logits - row_peak[:, None])
    exp_pos = jnp.exp(pos_logit - row_peak)
    row_total = jnp.sum(exp_neg, axis=1) + exp_pos
    lse = row_peak + jnp.log(row_total)
    loss_here = jnp.sum(weight * (lse - pos_logit))
    grad_neg = (weight[:, None] * exp_neg / row_total[:, None]).astype(jnp.bfloat16)
    grad_pos = (weight * (exp_pos / row_total - 1.0)).astype(jnp.bfloat16)
    grad_user = (
        contract_cols(grad_neg, full_neg)
        + grad_pos.astype(jnp.float32)[:, None] * pos_full.astype(jnp.float32)
    ).astype(jnp.bfloat16)
    neg_row_grad = contract_rows(user_block, grad_neg)
    pos_row_grad = (grad_pos.astype(jnp.float32)[:, None] * user_block.astype(jnp.float32)).astype(
        jnp.bfloat16
    )
    grad_w_third = contract_rows(act_second, grad_user)
    grad_b_third = jnp.sum(grad_user.astype(jnp.float32), axis=0)
    grad_pre_second = gelu_back(pre_second, contract_cols(grad_user, w_third)).astype(jnp.bfloat16)
    grad_w_second = contract_rows(act_first, grad_pre_second)
    grad_b_second = jnp.sum(grad_pre_second.astype(jnp.float32), axis=0)
    grad_pre_first = gelu_back(pre_first, contract_cols(grad_pre_second, w_second)).astype(
        jnp.bfloat16
    )
    grad_w_first = contract_rows(joined, grad_pre_first)
    grad_b_first = jnp.sum(grad_pre_first.astype(jnp.float32), axis=0)
    grad_joined = contract_cols(grad_pre_first, w_first).astype(jnp.bfloat16)
    grad_pw = grad_joined[:, :embed_width]
    grad_ps = grad_joined[:, embed_width : 2 * embed_width]
    grad_demo = contract_rows(bucket_counts, grad_joined[:, 2 * embed_width :])
    col_start = col_slot * col_width
    own_pw = lax.dynamic_slice_in_dim(grad_pw, col_start, col_width, 1).T
    own_ps = lax.dynamic_slice_in_dim(grad_ps, col_start, col_width, 1).T
    own_pos = lax.dynamic_slice_in_dim(pos_row_grad, col_start, col_width, 1).T
    user_vecs = lax.dynamic_slice_in_dim(user_block, col_slot * quarter, quarter, 0)
    all_pw, all_ps, all_dpos = (
        comm.gather(own_pw, "batch", 1),
        comm.gather(own_ps, "batch", 1),
        comm.gather(own_pos, "batch", 1),
    )
    neg_own = lax.dynamic_slice_in_dim(neg_row_grad, col_slot * col_width, col_width, 0)
    sums_out = comm.total(
        (
            grad_w_first,
            grad_b_first,
            grad_w_second,
            grad_b_second,
            grad_w_third,
            grad_b_third,
            grad_demo,
            neg_own,
            loss_here,
        ),
        "batch",
    )
    neg_sum_own = sums_out[7]

    def split_blocks(columns):
        return columns.reshape(col_width, block_count, block_rows).transpose(1, 0, 2)

    def grad_block(running, inputs_block):
        watch_block, search_block, pos_block, block_pw, block_ps, block_pos = inputs_block
        new_watch = running[0] + jnp.dot(
            block_pw, bag_counts(watch_block), preferred_element_type=jnp.float32
        )
        new_search = running[1] + jnp.dot(
            block_ps, bag_counts(search_block), preferred_element_type=jnp.float32
        )
        new_out = running[2] + jnp.dot(
            block_pos, single_hot(pos_block), preferred_element_type=jnp.float32
        )
        return ((new_watch, new_search, new_out), None)

    zeros_table = jnp.zeros((col_width, vocab_rows), jnp.float32)
    (table_watch, table_search, table_out), _ = lax.scan(
        grad_block,
        (zeros_table, zeros_table, zeros_table),
        id_blocks + (split_blocks(all_pw), split_blocks(all_ps), split_blocks(all_dpos)),
    )
    neg_added = (
        jnp.zeros((col_width, vocab_rows + 1), jnp.float32).at[:, neg_local].add(neg_sum_own)
    )
    table_out = table_out + neg_added[:, :vocab_rows]
    return (
        user_vecs,
        sums_out[8],
        table_watch / bag_size,
        table_search / bag_size,
        table_out,
        sums_out[6],
        sums_out[0],
        sums_out[1],
        sums_out[2],
        sums_out[3],
        sums_out[4],
        sums_out[5],
    )


F32, BF16, FP8, I32 = jnp.float32, jnp.bfloat16, jnp.float8_e4m3fn, jnp.int32
MESH = pl.DeviceIdType.MESH
LOW = 256
ROWS_IN_GROUP = 4
BAG_PAD = 64
CHUNK = 256
NEG_FLOOR = -1e30


def dot_as(left, right, left_dim, right_dim):
    return lax.dot_general(
        left, right, (((left_dim,), (right_dim,)), ((), ())), preferred_element_type=F32
    )


def iota(shape, dim):
    return lax.broadcasted_iota(I32, shape, dim)


def one_where(mask, kind):
    return jnp.where(mask, jnp.ones((), BF16), jnp.zeros((), BF16)).astype(kind)


def slot_cap(neg_count, batch):
    mean = neg_count / batch
    return int(math.ceil((mean + 4.5 * math.sqrt(mean)) / CHUNK)) * CHUNK


def gelu(pre):
    bent = jnp.tanh(math.sqrt(2.0 / math.pi) * (pre + 0.044715 * (pre * pre * pre)))
    return 0.5 * pre * (1.0 + bent)


def gelu_slope(pre):
    inner_scale = math.sqrt(2.0 / math.pi)
    square = pre * pre
    bent = jnp.tanh(inner_scale * (pre + 0.044715 * (square * pre)))
    return 0.5 * (1.0 + bent) + 0.5 * pre * (1.0 - bent * bent) * (
        inner_scale * (1.0 + 3.0 * 0.044715 * square)
    )


def spread_matrix(rows):
    shape = (rows, 4 * rows)
    r, m = iota(shape, 0), iota(shape, 1)
    groups = rows // ROWS_IN_GROUP
    return one_where((r % groups == m // 16) & (r // groups == m % ROWS_IN_GROUP), BF16)


class Sizes:
    def __init__(self, batch, col, rows, bag, width, vocab, negs, embed, demo_width):
        self.batch, self.col, self.rows, self.bag = batch, col, rows, bag
        self.width, self.vocab, self.negs, self.embed = width, vocab, negs, embed
        self.demo_width = demo_width
        self.total = batch * rows
        self.quarter = rows // col
        self.users = batch * self.quarter
        self.groups = rows // ROWS_IN_GROUP
        self.high = vocab // LOW
        self.high_parts = self.high // 4
        self.cap = slot_cap(negs, batch)
        self.cap_tiles = self.cap // CHUNK
        self.tiles = self.cap_tiles + col
        self.neg_lines = -(-negs // (CHUNK * 8)) * 8
        self.steps = 4
        self.span = self.total // self.steps
        self.x_width = col * 128 + 128


def front_kernel(
    sz,
    watch_ids, search_ids, demo_ids, pos_ids, neg_ids, demo_table, b_first, b_second, b_third, valid_count,
    watch_table, search_table, out_table, w_first, w_second, w_third,
    counts_out, x_out, act1_out, slope1_out, act2_out, slope2_out, gu_out, buckets_out,
    neg_rows_out, pos_rows_out, slots_out, user_out, loss_out, fits_out,
    tabs, tall, mix, w1_raw, w1, w2, w3, turned, ids, neg_dest, neg_digits, counts, found_sums, sums, pieces, x,
    pre1, pre2, acts1, slopes1, acts2, slopes2, users, buckets, slots, picked, neg_all, pos_all, e_cols,
    e_rows, probs, stats, g_send, g_recv, gu, rg_send, rg_recv, gp_all, loss_all,
    local_sem, out_sem, count_sem, ids_s, ids_r, rs_s, rs_r, ag_s, ag_r, xx_s, xx_r, co_s, co_r,
    ne_s, ne_r, pe_s, pe_r, st_s, st_r, gs_s, gs_r, ga_s, ga_r, gx_s, gx_r, gc_s, gc_r,
    rg_s, rg_r, gp_s, gp_r, lo_s, lo_r,
):
    b, c = lax.axis_index("batch"), lax.axis_index("col")
    nb, nc = sz.batch, sz.col
    offset = b * sz.vocab
    cap, width, embed = sz.cap, sz.width, sz.embed
    cx = lax.rem(c + 2, nc)
    ck = c + 1 - 2 * lax.rem(c, 2)
    ckx = lax.rem(ck + 2, nc)

    def batch_peer(i):
        return lax.rem(b + i, nb)

    def batch_from(i):
        return lax.rem(b + nb - i, nb)

    def col_peer(i):
        return lax.rem(c + i, nc)

    def col_from(i):
        return lax.rem(c + nc - i, nc)

    def send(src, dst, ssem, rsem, to):
        return pltpu.make_async_remote_copy(
            src_ref=src, dst_ref=dst, send_sem=ssem, recv_sem=rsem,
            device_id=to, device_id_type=MESH,
        )

    barrier = pltpu.get_barrier_semaphore()
    for i in range(1, nb):
        pl.semaphore_signal(barrier, inc=1, device_id=(batch_peer(i), c), device_id_type=MESH)
    for i in range(1, nc):
        pl.semaphore_signal(barrier, inc=1, device_id=(b, col_peer(i)), device_id_type=MESH)

    loads = [
        (watch_table, tabs.at[0]), (search_table, tabs.at[1]), (out_table, tabs.at[2]),
        (w_first, w1_raw), (w_second, w2), (w_third, w3),
    ]
    loads = [pltpu.make_async_copy(s, d, local_sem.at[i]) for i, (s, d) in enumerate(loads)]
    for load in loads:
        load.start()

    turned[...] = jnp.zeros((BAG_PAD, 128), I32)
    turned[0 : sz.bag, :] = (watch_ids[...] & 0xFFFF) | (search_ids[...] << 16)
    packed = turned[...].T
    for r4 in range(ROWS_IN_GROUP):
        ids[b, 0 : sz.groups, r4 * BAG_PAD : (r4 + 1) * BAG_PAD] = packed[
            r4 * sz.groups : (r4 + 1) * sz.groups, :
        ]
    ids[b, sz.groups : sz.groups + 8, :] = jnp.zeros((8, CHUNK), I32)
    ids[b, sz.groups : sz.groups + 1, 0:128] = pos_ids[...]
    ids[b, sz.groups + 1 : sz.groups + 2, 0:128] = jnp.full((1, 128), valid_count[0], I32)
    ids[b, sz.groups + 2 : sz.groups + 2 + demo_ids.shape[0], 0:128] = demo_ids[...]

    negs = neg_ids[...]
    lines = sz.neg_lines
    missing = 2 * lines - negs.shape[0]
    second = jnp.concatenate([negs[lines:], jnp.full((missing, 128), -1, I32)], axis=0)
    negs = jnp.concatenate([negs[:lines], second], axis=1)
    neg_local = negs - offset
    own = (neg_local >= 0) & (neg_local < sz.vocab)
    own_bf = one_where(own, BF16)
    upper = one_where(iota((CHUNK, CHUNK), 0) < iota((CHUNK, CHUNK), 1), BF16)
    before = dot_as(own_bf, upper, 1, 0)
    in_row = dot_as(own_bf, jnp.ones((CHUNK, CHUNK), BF16), 1, 0)
    lower = one_where(iota((lines, lines), 1) < iota((lines, lines), 0), BF16)
    rows_before = dot_as(lower, in_row.astype(BF16), 1, 0)
    neg_dest[...] = jnp.where(own, before + rows_before, -1.0)
    owned_count = dot_as(jnp.ones((8, lines), BF16), in_row.astype(BF16), 1, 0)
    most = jnp.zeros((1, 1), F32)
    for shard in range(nb):
        part = negs - shard * sz.vocab
        hits = jnp.where((part >= 0) & (part < sz.vocab), 1.0, 0.0)
        most = jnp.maximum(most, jnp.sum(jnp.sum(hits, axis=1, keepdims=True), axis=0, keepdims=True))
    fits_out[...] = jnp.where(most <= float(cap), 1, 0)
    for digit in range(4):
        neg_digits[digit] = ((neg_local >> (4 * digit)) & 15).astype(F32)

    def compact(k, total):
        place = neg_dest[pl.ds(k, 1), :]
        hot = one_where(place == iota((cap, CHUNK), 0).astype(F32), FP8)
        line = iota((32, CHUNK), 0)
        value = jnp.where(line == 4, 1.0, 0.0)
        for digit in range(4):
            value = jnp.where(line == digit, neg_digits[digit, pl.ds(k, 1), :], value)
        return total + dot_as(value.astype(FP8), hot, 1, 1)

    slot = lax.fori_loop(0, lines, compact, jnp.zeros((32, cap), F32))
    neg_low = slot[0:1] + 16.0 * slot[1:2]
    neg_high = jnp.where(slot[4:5] > 0.5, slot[2:3] + 16.0 * slot[3:4], -1.0)
    slots[...] = jnp.zeros((sz.tiles, 8, CHUNK), F32)
    for k in range(sz.cap_tiles):
        slots[k, 0:1, :] = neg_high[:, k * CHUNK : (k + 1) * CHUNK]
        slots[k, 1:2, :] = neg_low[:, k * CHUNK : (k + 1) * CHUNK]

    for t in range(2):
        loads[t].wait()

    def turn(n, _):
        t, hh = n // sz.high_parts, n % sz.high_parts
        base = pl.multiple_of(hh * 4 * LOW, 4 * LOW)
        stack = jnp.concatenate([tabs[t, :, pl.ds(base + i * LOW, LOW)] for i in range(4)], axis=0)
        mix[t, pl.ds(pl.multiple_of(hh * LOW, LOW), LOW), :] = stack.T
        return 0

    lax.fori_loop(0, 2 * sz.high_parts, turn, 0)

    pl.semaphore_wait(barrier, nb - 1 + nc - 1)
    last_sends = []
    for i in range(1, nb):
        copy = send(ids.at[b], ids.at[b], ids_s.at[i - 1], ids_r.at[i - 1], (batch_peer(i), c))
        copy.start()
        last_sends.append(copy)

    loads[2].wait()

    def stack_up(hh, _):
        for i in range(4):
            tall[pl.ds(pl.multiple_of((hh * 4 + i) * width, width), width), :] = tabs[
                2, :, pl.ds(pl.multiple_of((hh * 4 + i) * LOW, LOW), LOW)
            ]
        return 0

    lax.fori_loop(0, sz.high_parts, stack_up, 0)

    def pick_tile(k, _):
        high, low = slots[k, 0:1, :], slots[k, 1:2, :]
        low_hot = one_where(low.astype(BF16) == iota((LOW, CHUNK), 0).astype(BF16), BF16)
        total = jnp.zeros((width, CHUNK), F32)
        for part in range(4):
            tall_rows = width * sz.high // 4
            got = dot_as(tall[part * tall_rows : (part + 1) * tall_rows, :], low_hot, 1, 0)
            for i in range(sz.high // 4):
                at = float(part * (sz.high // 4) + i)
                total = total + jnp.where(high == at, got[i * width : (i + 1) * width], 0.0)
        picked[k] = total.astype(BF16)
        return 0

    lax.fori_loop(0, sz.cap_tiles, pick_tile, 0)
    neg_part = picked.at[pl.ds(0, sz.cap_tiles)]
    for i in range(1, nc):
        copy = send(neg_part, neg_all.at[c], ne_s.at[i - 1], ne_r.at[i - 1], (b, col_peer(i)))
        copy.start()
        last_sends.append(copy)
    for k in range(sz.cap_tiles):
        neg_all[c, k] = picked[k]

    loads[3].wait()
    w1[nc * 128 :, :] = jnp.zeros((128, w1.shape[1]), BF16)
    for i in range(nc):
        w1[i * 128 : i * 128 + width, :] = w1_raw[i * width : (i + 1) * width, :]
        w1[i * 128 + width : (i + 1) * 128, :] = w1_raw[embed + i * width : embed + (i + 1) * width, :]
    w1[nc * 128 : nc * 128 + sz.demo_width, :] = w1_raw[2 * embed :, :]
    loads[4].wait()
    loads[5].wait()

    for i in range(1, nb):
        src = batch_from(i)
        send(ids.at[src], ids.at[src], ids_s.at[i - 1], ids_r.at[i - 1], (b, c)).wait_recv()

    all_pos = jnp.concatenate([ids[j, sz.groups : sz.groups + 1, 0:128] for j in range(nb)], axis=0)
    valid = jnp.concatenate([ids[j, sz.groups + 1 : sz.groups + 2, 0:128] for j in range(nb)], axis=0)
    pos_local = all_pos - offset
    pos_owned = (pos_local >= 0) & (pos_local < sz.vocab)
    pos_pair = jnp.concatenate(
        [
            jnp.where(pos_owned, pos_local >> 8, 255).astype(F32),
            (pos_local & 255).astype(F32),
        ],
        axis=0,
    ).astype(BF16)
    shape = (nb, CHUNK)
    at_block = iota(shape, 1) // sz.quarter == iota(shape, 0)
    for quarter in range(nc):
        shape = (128, CHUNK)
        pick = one_where(iota(shape, 0) == quarter * sz.quarter + iota(shape, 1) % sz.quarter, BF16)
        wide = dot_as(pos_pair, pick, 1, 0)
        high = jnp.sum(jnp.where(at_block, wide[0:nb], 0.0), axis=0, keepdims=True)
        low = jnp.sum(jnp.where(at_block, wide[nb : 2 * nb], 0.0), axis=0, keepdims=True)
        slots[sz.cap_tiles + quarter, 0:1, :] = jnp.where(high > 254.0, -1.0, high)
        slots[sz.cap_tiles + quarter, 1:2, :] = low
    slots_out[...] = slots[...]
    lax.fori_loop(sz.cap_tiles, sz.tiles, pick_tile, 0)
    pos_all[c] = picked[sz.cap_tiles + c]
    for i in range(1, nc):
        to = col_peer(i)
        copy = send(picked.at[sz.cap_tiles + to], pos_all.at[c], pe_s.at[i - 1], pe_r.at[i - 1], (b, to))
        copy.start()
        last_sends.append(copy)

    valid_wide = jnp.concatenate([valid] * (sz.users // 128), axis=1).astype(F32)
    live_count = jnp.sum(jnp.where(at_block, valid_wide, 0.0), axis=0, keepdims=True)
    valid_total = jnp.sum(valid_wide, axis=0, keepdims=True)
    user_place = c * sz.quarter + iota((1, sz.users), 1) % sz.quarter
    weight = jnp.where(user_place.astype(F32) < live_count, 1.0 / valid_total, 0.0)

    bucket_total = jnp.zeros((buckets.shape[0], sz.total), BF16)
    bucket_line = iota((buckets.shape[0], sz.total), 0).astype(BF16)
    for field in range(demo_ids.shape[0]):
        row = sz.groups + 2 + field
        line = jnp.concatenate([ids[j, row : row + 1, 0:128] for j in range(nb)], axis=1)
        bucket_total = bucket_total + one_where(line.astype(F32).astype(BF16) == bucket_line, BF16)
    buckets[...] = bucket_total
    demo_rows = demo_table[...].astype(F32).T.astype(BF16)
    x[:, nc * 128 :] = jnp.zeros((sz.total, 128), BF16)
    x[:, nc * 128 : nc * 128 + sz.demo_width] = dot_as(bucket_total, demo_rows, 0, 0).astype(BF16)
    buckets_copy = pltpu.make_async_copy(buckets, buckets_out, out_sem.at[0])
    buckets_copy.start()

    spread = spread_matrix(sz.rows)
    span = sz.span
    piece = span // nb
    span_lines = 4 * span
    lane_mod = iota((16, CHUNK), 1) % BAG_PAD
    lane_r4 = iota((16, CHUNK), 1) // BAG_PAD
    blocks = span // sz.rows
    parts_in_block = sz.groups // 16

    def count_copy(t, table, slot_at):
        rows = pl.ds(pl.multiple_of(t * span_lines, span_lines), span_lines)
        return pltpu.make_async_copy(
            counts.at[table, slot_at], counts_out.at[table, :, rows], count_sem.at[table, slot_at]
        )

    def bag_table(t, table):
        slot_at = lax.rem(t, 2)

        @pl.when(t >= 2)
        def _():
            count_copy(t - 2, table, slot_at).wait()

        code_line = iota((4 * sz.high, CHUNK), 0).astype(BF16)
        low_line = iota((LOW, CHUNK), 0).astype(BF16)

        def groups_of(q, _):
            block = t * blocks + q // parts_in_block
            word = ids[block, pl.ds(pl.multiple_of((q % parts_in_block) * 16, 16), 16), :]
            value = lax.shift_right_logical(word, 16 * table) & 0xFFFF
            local = value - offset
            mine = (local >= 0) & (local < sz.vocab) & (lane_mod < sz.bag)
            code = jnp.where(mine, (local >> 8) * 4 + lane_r4, -1).astype(F32).astype(BF16)
            low = (local & 255).astype(F32).astype(BF16)
            for g in range(16):
                left = one_where(code[g : g + 1, :] == code_line, FP8)
                right = one_where(low[g : g + 1, :] == low_line, FP8)
                found = dot_as(left, right, 1, 1).astype(BF16)
                line = pl.ds(pl.multiple_of(q * 256 + g * 16, 16), 16)
                for hh in range(sz.high_parts):
                    counts[table, slot_at, hh, line, :] = found[hh * 16 : (hh + 1) * 16, :]
            return 0

        lax.fori_loop(0, blocks * parts_in_block, groups_of, 0)
        count_copy(t, table, slot_at).start()
        left = jnp.concatenate([counts[table, slot_at, hh] for hh in range(sz.high_parts)], axis=1)
        total = dot_as(left, mix[table], 1, 0)
        shape = (span_lines, 4 * width)
        total = jnp.where((iota(shape, 0) // 4) % 4 == iota(shape, 1) // width, total, 0.0)
        half = (total[:, :128] + total[:, 128:]).astype(BF16)
        for k in range(blocks):
            found = dot_as(spread, half[k * 4 * sz.rows : (k + 1) * 4 * sz.rows], 1, 0)
            found_sums[table, k * sz.rows : (k + 1) * sz.rows, :] = found + pltpu.roll(found, width, 1)

    def bag_step(t):
        def one_table(table, _):
            bag_table(t, table)
            return 0

        lax.fori_loop(0, 2, one_table, 0)
        joined = jnp.where(iota((span, 128), 1) < width, found_sums[0], found_sums[1])
        sums[t] = joined.astype(BF16)
        for i in range(1, nb):
            to = batch_peer(i)
            send(
                sums.at[t, pl.ds(pl.multiple_of(to * piece, piece), piece)], pieces.at[t, i - 1],
                rs_s.at[t, i - 1], rs_r.at[t], (to, c),
            ).start()

    def x_at(t, col):
        return x.at[
            pl.ds(pl.multiple_of(t * span, span), span), pl.ds(pl.multiple_of(col * 128, 128), 128)
        ]

    def x_piece(t, owner):
        return x.at[
            pl.ds(pl.multiple_of(t * span + owner * piece, piece), piece),
            pl.ds(pl.multiple_of(c * 128, 128), 128),
        ]

    def reduce_step(t):
        send(pieces.at[t], pieces.at[t], rs_s.at[t, 0], rs_r.at[t], (b, c)).wait_recv()
        total = sums[t, pl.ds(pl.multiple_of(b * piece, piece), piece), :].astype(F32)
        for i in range(nb - 1):
            total = total + pieces[t, i].astype(F32)
        x[
            pl.ds(pl.multiple_of(t * span + b * piece, piece), piece),
            pl.ds(pl.multiple_of(c * 128, 128), 128),
        ] = (total / sz.bag).astype(BF16)
        for i in range(1, nb):
            send(x_piece(t, b), x_piece(t, b), ag_s.at[t, i - 1], ag_r.at[t], (batch_peer(i), c)).start()

    def cross_step(t):
        send(pieces.at[t], pieces.at[t], ag_s.at[t, 0], ag_r.at[t], (b, c)).wait_recv()
        send(x_at(t, c), x_at(t, c), xx_s.at[t], xx_r.at[t], (b, cx)).start()

    def core_step(t):
        send(x_at(t, cx), x_at(t, cx), xx_s.at[t], xx_r.at[t], (b, cx)).wait_recv()
        send(x_at(t, c), x_at(t, c), co_s.at[t, 0], co_r.at[t, 0], (b, ck)).start()
        send(x_at(t, cx), x_at(t, cx), co_s.at[t, 1], co_r.at[t, 1], (b, ck)).start()

    def full_step(t):
        send(x_at(t, ck), x_at(t, ck), co_s.at[t, 0], co_r.at[t, 0], (b, ck)).wait_recv()
        send(x_at(t, ckx), x_at(t, ckx), co_s.at[t, 1], co_r.at[t, 1], (b, ck)).wait_recv()

    def tower(k):
        at = pl.ds(pl.multiple_of(k * span, span), span)
        pre = dot_as(x[at, :], w1[...], 1, 0) + b_first[...]
        pre1[at, :] = pre
        value = gelu(pre).astype(BF16)
        acts1[at, :] = value
        pre = dot_as(value, w2[...], 1, 0) + b_second[...]
        pre2[at, :] = pre
        value = gelu(pre).astype(BF16)
        acts2[at, :] = value
        users[at, :] = (dot_as(value, w3[...], 1, 0) + b_third[...]).astype(BF16)

    def slopes(k):
        at = pl.ds(pl.multiple_of(k * span, span), span)
        slopes1[at, :] = gelu_slope(pre1[at, :]).astype(BF16)
        slopes2[at, :] = gelu_slope(pre2[at, :]).astype(BF16)

    def step(t, _):
        @pl.when(t < sz.steps)
        def _():
            bag_step(t)

        @pl.when((t >= 1) & (t < sz.steps + 1))
        def _():
            reduce_step(t - 1)

        @pl.when((t >= 2) & (t < sz.steps + 2))
        def _():
            cross_step(t - 2)

        @pl.when((t >= 3) & (t < sz.steps + 3))
        def _():
            core_step(t - 3)

        @pl.when(t >= 4)
        def _():
            full_step(t - 4)

        @pl.when(t >= sz.steps)
        def _():
            tower(t - sz.steps)

        return 0

    lax.fori_loop(0, sz.steps + 4, step, 0)

    out_copies = [(x, x_out), (acts1, act1_out), (acts2, act2_out), (slopes1, slope1_out), (slopes2, slope2_out)]
    out_copies = [pltpu.make_async_copy(s, d, out_sem.at[1 + i]) for i, (s, d) in enumerate(out_copies)]
    for copy in out_copies[:3]:
        copy.start()
    user_out[...] = users[pl.ds(pl.multiple_of(b * sz.rows + c * sz.quarter, sz.quarter), sz.quarter), :]

    for i in range(1, nc):
        src = col_from(i)
        send(neg_all.at[src], neg_all.at[src], ne_s.at[i - 1], ne_r.at[i - 1], (b, c)).wait_recv()
        send(pos_all.at[src], pos_all.at[src], pe_s.at[i - 1], pe_r.at[i - 1], (b, c)).wait_recv()
    for i in range(nc):
        for k in range(sz.cap_tiles):
            e_cols[i * width : (i + 1) * width, k * CHUNK : (k + 1) * CHUNK] = neg_all[i, k]
        e_cols[i * width : (i + 1) * width, cap:] = pos_all[i]
    e_rows[...] = e_cols[...].T

    def users_of(quarter):
        return jnp.concatenate(
            [
                users[pl.ds(pl.multiple_of(j * sz.rows + quarter * sz.quarter, sz.quarter), sz.quarter), :]
                for j in range(nb)
            ],
            axis=0,
        )

    quarter_users = users_of(c)
    logits = dot_as(e_rows[...], quarter_users, 1, 1)
    neg_logits, pos_logits = logits[0:cap], logits[cap:]
    slot_ok = iota((cap, sz.users), 0).astype(F32) < owned_count[0:1, : sz.users]
    pos_here = slots[sz.cap_tiles + c, 0:1, :]
    pos_ok = (iota((sz.users, sz.users), 0) == iota((sz.users, sz.users), 1)) & (pos_here >= 0.0)
    neg_logits = jnp.where(slot_ok, neg_logits, NEG_FLOOR)
    pos_masked = jnp.where(pos_ok, pos_logits, NEG_FLOOR)
    peak = jnp.maximum(
        jnp.max(neg_logits, axis=0, keepdims=True), jnp.max(pos_masked, axis=0, keepdims=True)
    )
    mass = jnp.sum(jnp.where(slot_ok, jnp.exp(neg_logits - peak), 0.0), axis=0, keepdims=True) + jnp.sum(
        jnp.where(pos_ok, jnp.exp(pos_masked - peak), 0.0), axis=0, keepdims=True
    )
    pos_value = jnp.sum(jnp.where(pos_ok, pos_logits, 0.0), axis=0, keepdims=True)
    stats[b] = jnp.concatenate([peak, mass, pos_value, jnp.zeros((5, sz.users), F32)], axis=0)
    for i in range(1, nb):
        copy = send(stats.at[b], stats.at[b], st_s.at[i - 1], st_r.at[i - 1], (batch_peer(i), c))
        copy.start()
        last_sends.append(copy)

    def some_slopes(k, _):
        slopes(k)
        return 0

    lax.fori_loop(0, sz.steps // 2, some_slopes, 0)
    for i in range(1, nb):
        src = batch_from(i)
        send(stats.at[src], stats.at[src], st_s.at[i - 1], st_r.at[i - 1], (b, c)).wait_recv()
    peaks = [stats[j, 0:1, :] for j in range(nb)]
    top = peaks[0]
    for j in range(1, nb):
        top = jnp.maximum(top, peaks[j])
    full_mass = jnp.zeros((1, sz.users), F32)
    pos_logit = jnp.zeros((1, sz.users), F32)
    for j in range(nb):
        full_mass = full_mass + stats[j, 1:2, :] * jnp.exp(peaks[j] - top)
        pos_logit = pos_logit + stats[j, 2:3, :]
    lse = top + jnp.log(full_mass)
    loss_part = jnp.sum(weight * (lse - pos_logit), axis=1, keepdims=True)
    scale = weight / full_mass
    probs[0:cap] = jnp.where(slot_ok, jnp.exp(neg_logits - top) * scale, 0.0).astype(BF16)
    pos_grad = weight * (jnp.exp(pos_logit - top) / full_mass - 1.0)
    probs[cap:] = jnp.where(pos_ok, pos_grad, 0.0).astype(BF16)
    grad_user = dot_as(probs[...], e_rows[...], 0, 0)
    for j in range(nb):
        g_send[j] = grad_user[j * sz.quarter : (j + 1) * sz.quarter].astype(BF16)
    for i in range(1, nb):
        to = batch_peer(i)
        copy = send(g_send.at[to], g_recv.at[i - 1], gs_s.at[i - 1], gs_r.at[i - 1], (to, c))
        copy.start()
        last_sends.append(copy)
    rows_grad = dot_as(probs[0:cap, :], quarter_users, 1, 0)
    rows_grad = rows_grad.T.astype(BF16)
    for i in range(nc):
        rg_send[i] = rows_grad[i * width : (i + 1) * width]
    gp_all[c] = jnp.broadcast_to(jnp.where(pos_here >= 0.0, pos_grad, 0.0), (8, sz.users))
    loss_all[c] = jnp.broadcast_to(loss_part, (8, 128))
    for i in range(1, nc):
        to = col_peer(i)
        for copy in (
            send(rg_send.at[to], rg_recv.at[c], rg_s.at[i - 1], rg_r.at[i - 1], (b, to)),
            send(gp_all.at[c], gp_all.at[c], gp_s.at[i - 1], gp_r.at[i - 1], (b, to)),
            send(loss_all.at[c], loss_all.at[c], lo_s.at[i - 1], lo_r.at[i - 1], (b, to)),
        ):
            copy.start()
            last_sends.append(copy)
    rg_recv[c] = rg_send[c]
    lax.fori_loop(sz.steps // 2, sz.steps, some_slopes, 0)
    for copy in out_copies[3:]:
        copy.start()
    for i in range(1, nb):
        send(g_send.at[0], g_recv.at[i - 1], gs_s.at[i - 1], gs_r.at[i - 1], (b, c)).wait_recv()
    total = g_send[b].astype(F32)
    for i in range(nb - 1):
        total = total + g_recv[i].astype(F32)

    def gu_at(block, col):
        return gu.at[block, pl.ds(pl.multiple_of(col * sz.quarter, sz.quarter), sz.quarter), :]

    def gu_all(col):
        return gu.at[:, pl.ds(pl.multiple_of(col * sz.quarter, sz.quarter), sz.quarter), :]

    gu[b, pl.ds(pl.multiple_of(c * sz.quarter, sz.quarter), sz.quarter), :] = total.astype(BF16)
    for i in range(1, nb):
        copy = send(gu_at(b, c), gu_at(b, c), ga_s.at[i - 1], ga_r.at[i - 1], (batch_peer(i), c))
        copy.start()
        last_sends.append(copy)
    for i in range(nb):
        src = batch_from(i)
        if i > 0:
            send(gu_at(src, c), gu_at(src, c), ga_s.at[i - 1], ga_r.at[i - 1], (b, c)).wait_recv()
        copy = send(gu_at(src, c), gu_at(src, c), gx_s.at[i], gx_r.at[i], (b, cx))
        copy.start()
        last_sends.append(copy)
    copy = send(gu_all(c), gu_all(c), gc_s.at[0], gc_r.at[0], (b, ck))
    copy.start()
    last_sends.append(copy)

    pick_own = one_where(iota((width, embed), 1) == c * width + iota((width, embed), 0), BF16)
    for i in range(1, nc):
        src = col_from(i)
        send(gp_all.at[src], gp_all.at[src], gp_s.at[i - 1], gp_r.at[i - 1], (b, c)).wait_recv()
    for quarter in range(nc):
        own_part = dot_as(pick_own, users_of(quarter), 1, 1)
        grad = gp_all[quarter, 0:1, :].astype(BF16).astype(F32)
        mine = slots[sz.cap_tiles + quarter, 0:1, :] >= 0.0
        pos_rows_out[:, quarter * sz.users : (quarter + 1) * sz.users] = jnp.where(
            mine, grad * own_part, 0.0
        ).astype(BF16)

    for i in range(nb):
        src = batch_from(i)
        send(gu_at(src, cx), gu_at(src, cx), gx_s.at[i], gx_r.at[i], (b, cx)).wait_recv()
    copy = send(gu_all(cx), gu_all(cx), gc_s.at[1], gc_r.at[1], (b, ck))
    copy.start()
    last_sends.append(copy)

    for i in range(1, nc):
        src = col_from(i)
        send(loss_all.at[src], loss_all.at[src], lo_s.at[i - 1], lo_r.at[i - 1], (b, c)).wait_recv()
        send(rg_recv.at[src], rg_recv.at[src], rg_s.at[i - 1], rg_r.at[i - 1], (b, c)).wait_recv()
    loss = loss_all[0]
    neg_total = rg_recv[0].astype(F32)
    for i in range(1, nc):
        loss = loss + loss_all[i]
        neg_total = neg_total + rg_recv[i].astype(F32)
    neg_rows_out[...] = neg_total.astype(BF16)
    loss_out[...] = loss[0:1, 0:1]

    for i, col in enumerate((ck, ckx)):
        send(gu_all(col), gu_all(col), gc_s.at[i], gc_r.at[i], (b, ck)).wait_recv()
    gu_copy = pltpu.make_async_copy(gu, gu_out, out_sem.at[6])
    gu_copy.start()

    for copy in last_sends:
        copy.wait_send()

    def drain(t, _):
        for i in range(1, nb):
            send(sums.at[t, pl.ds(0, piece)], pieces.at[t, 0], rs_s.at[t, i - 1], rs_r.at[t], (b, c)).wait_send()
            send(x_piece(t, b), x_piece(t, b), ag_s.at[t, i - 1], ag_r.at[t], (b, c)).wait_send()
        send(x_at(t, c), x_at(t, c), xx_s.at[t], xx_r.at[t], (b, cx)).wait_send()
        send(x_at(t, c), x_at(t, c), co_s.at[t, 0], co_r.at[t, 0], (b, ck)).wait_send()
        send(x_at(t, cx), x_at(t, cx), co_s.at[t, 1], co_r.at[t, 1], (b, ck)).wait_send()
        return 0

    lax.fori_loop(0, sz.steps, drain, 0)
    for table in range(2):
        for t in (sz.steps - 2, sz.steps - 1):
            count_copy(t, table, t % 2).wait()
    buckets_copy.wait()
    gu_copy.wait()
    for copy in out_copies:
        copy.wait()


def front(sz, args):
    nb, nc, total = sz.batch, sz.col, sz.total
    width, embed, cap, users = sz.width, sz.embed, sz.cap, sz.users
    slots = cap + users
    first, second = args["w_second"].shape
    buckets = args["demo_table"].shape[0]
    x_width = sz.x_width
    span_lines = 4 * sz.span
    vmem = pl.BlockSpec(memory_space=pltpu.VMEM)
    smem = pl.BlockSpec(memory_space=pltpu.SMEM)
    hbm = pl.BlockSpec(memory_space=pl.ANY)
    dma = pltpu.SemaphoreType.DMA

    def shape(dims, kind=BF16):
        return jax.ShapeDtypeStruct(dims, kind)

    outs = [
        (shape((2, sz.high_parts, 4 * total, LOW)), hbm), (shape((total, x_width)), hbm),
        (shape((total, first)), hbm), (shape((total, first)), hbm),
        (shape((total, second)), hbm), (shape((total, second)), hbm),
        (shape((nb, sz.rows, embed)), hbm), (shape((buckets, total)), hbm),
        (shape((width, cap)), vmem), (shape((width, total)), vmem),
        (shape((sz.tiles, 8, CHUNK), F32), vmem),
        (shape((sz.quarter, embed)), vmem), (shape((1, 1), F32), vmem), (shape((1, 1), I32), vmem),
    ]
    scratch = [
        pltpu.VMEM((3, width, sz.vocab), BF16),
        pltpu.VMEM((sz.high * width, LOW), BF16),
        pltpu.VMEM((2, sz.high_parts * LOW, 4 * width), BF16),
        pltpu.VMEM(args["w_first"].shape, BF16),
        pltpu.VMEM((x_width, first), BF16),
        pltpu.VMEM((first, second), BF16),
        pltpu.VMEM((second, embed), BF16),
        pltpu.VMEM((BAG_PAD, 128), I32),
        pltpu.VMEM((nb, sz.groups + 8, CHUNK), I32),
        pltpu.VMEM((sz.neg_lines, CHUNK), F32),
        pltpu.VMEM((4, sz.neg_lines, CHUNK), F32),
        pltpu.VMEM((2, 2, sz.high_parts, span_lines, LOW), BF16),
        pltpu.VMEM((2, sz.span, 128), F32),
        pltpu.VMEM((sz.steps, sz.span, 128), BF16),
        pltpu.VMEM((sz.steps, nb - 1, sz.span // nb, 128), BF16),
        pltpu.VMEM((total, x_width), BF16),
        pltpu.VMEM((total, first), F32),
        pltpu.VMEM((total, second), F32),
        pltpu.VMEM((total, first), BF16),
        pltpu.VMEM((total, first), BF16),
        pltpu.VMEM((total, second), BF16),
        pltpu.VMEM((total, second), BF16),
        pltpu.VMEM((total, embed), BF16),
        pltpu.VMEM((buckets, total), BF16),
        pltpu.VMEM((sz.tiles, 8, CHUNK), F32),
        pltpu.VMEM((sz.tiles, width, CHUNK), BF16),
        pltpu.VMEM((nc, sz.cap_tiles, width, CHUNK), BF16),
        pltpu.VMEM((nc, width, users), BF16),
        pltpu.VMEM((embed, slots), BF16),
        pltpu.VMEM((slots, embed), BF16),
        pltpu.VMEM((slots, users), BF16),
        pltpu.VMEM((nb, 8, users), F32),
        pltpu.VMEM((nb, sz.quarter, embed), BF16),
        pltpu.VMEM((nb - 1, sz.quarter, embed), BF16),
        pltpu.VMEM((nb, sz.rows, embed), BF16),
        pltpu.VMEM((nc, width, cap), BF16),
        pltpu.VMEM((nc, width, cap), BF16),
        pltpu.VMEM((nc, 8, users), F32),
        pltpu.VMEM((nc, 8, 128), F32),
        dma((6,)), dma((7,)), dma((2, 2)),
        dma((nb - 1,)), dma((nb - 1,)),
        dma((sz.steps, nb - 1)), dma((sz.steps,)), dma((sz.steps, nb - 1)), dma((sz.steps,)),
        dma((sz.steps,)), dma((sz.steps,)), dma((sz.steps, 2)), dma((sz.steps, 2)),
        dma((nc - 1,)), dma((nc - 1,)), dma((nc - 1,)), dma((nc - 1,)),
        dma((nb - 1,)), dma((nb - 1,)), dma((nb - 1,)), dma((nb - 1,)),
        dma((nb - 1,)), dma((nb - 1,)), dma((nb,)), dma((nb,)), dma((2,)), dma((2,)),
        dma((nc - 1,)), dma((nc - 1,)), dma((nc - 1,)), dma((nc - 1,)), dma((nc - 1,)), dma((nc - 1,)),
    ]
    operands = [
        (args["watch_ids"].T, vmem), (args["search_ids"].T, vmem), (args["demo_ids"].T, vmem),
        (args["pos_ids"].reshape(1, -1), vmem), (args["neg_ids"].reshape(-1, 128), vmem),
        (args["demo_table"].T, vmem), (args["b_first"].reshape(1, -1), vmem),
        (args["b_second"].reshape(1, -1), vmem), (args["b_third"].reshape(1, -1), vmem),
        (args["valid_counts"], smem),
        (args["watch_table"], hbm), (args["search_table"], hbm), (args["out_table"], hbm),
        (args["w_first"], hbm), (args["w_second"], hbm), (args["w_third"], hbm),
    ]
    return pl.pallas_call(
        functools.partial(front_kernel, sz),
        out_shape=[o for o, _ in outs],
        in_specs=[s for _, s in operands],
        out_specs=[s for _, s in outs],
        scratch_shapes=scratch,
        compiler_params=pltpu.CompilerParams(
            collective_id=0, has_side_effects=True, vmem_limit_bytes=63 * 2**20
        ),
        name="front",
    )(*[o for o, _ in operands])


def back_kernel(
    sz, neg_rows, pos_rows, slots, counts, x_in, act1_in, slope1_in, act2_in, slope2_in, gu_in,
    buckets_in, w_first, w_second, w_third,
    watch_out, search_out, table_out, gw1_out, gw2_out, gw3_out, demo_out, gb1_out, gb2_out, gb3_out,
    x, act1, slope1, act2, slope2, gu, buckets, w1, w1_own, w2, w3, gps, gpf, gx, spread_grads, ring,
    lines, low_rows, gw1, gw2, gw3, in_sem, ring_sem, line_sem, out_sem,
):
    width, cap, total, nb = sz.width, sz.cap, sz.total, sz.batch
    parts, nc, embed = sz.high_parts, sz.col, sz.embed
    c = lax.axis_index("col")
    depth = ring.shape[0]
    names = [
        (gu_in, gu), (w_third, w3), (slope2_in, slope2), (w_second, w2), (slope1_in, slope1),
        (w_first, w1), (act2_in, act2), (act1_in, act1), (x_in, x), (buckets_in, buckets),
    ]
    loads = [pltpu.make_async_copy(s, d, in_sem.at[i]) for i, (s, d) in enumerate(names)]
    for load in loads:
        load.start()

    def ring_load(n):
        return pltpu.make_async_copy(
            counts.at[lax.rem(n, 2), n // 2], ring.at[lax.rem(n, depth)], ring_sem.at[lax.rem(n, depth)]
        )

    for n in range(depth):
        ring_load(n).start()

    loads[5].wait()
    w1_own[...] = jnp.zeros(w1_own.shape, BF16)
    w1_own[0:width, :] = w1[pl.ds(pl.multiple_of(c * width, width), width), :]
    w1_own[width : 2 * width, :] = w1[pl.ds(pl.multiple_of(embed + c * width, width), width), :]
    w1_own[2 * width : 2 * width + sz.demo_width, :] = w1[2 * embed :, :]
    for load in loads[:5]:
        load.wait()
    half_blocks = nb // 2
    half = half_blocks * sz.rows

    def down(k, _):
        at = pl.ds(pl.multiple_of(k * half, half), half)
        top = gu[pl.ds(k * half_blocks, half_blocks)].reshape(half, embed)
        second = (dot_as(top, w3[...], 1, 1) * slope2[at, :].astype(F32)).astype(BF16)
        gps[at, :] = second
        first = (dot_as(second, w2[...], 1, 1) * slope1[at, :].astype(F32)).astype(BF16)
        gpf[at, :] = first
        gx[at, :] = dot_as(first, w1_own[...], 1, 1).astype(BF16)
        return 0

    lax.fori_loop(0, 2, down, 0)

    spread = spread_matrix(sz.rows)
    shape = (4 * width, 4 * sz.rows)
    mask = iota(shape, 0) // width == (iota(shape, 1) // 4) % 4

    def lay(t, _):
        rows = gx[pl.ds(pl.multiple_of(t * sz.rows, sz.rows), sz.rows), 0:128]
        at = pl.ds(pl.multiple_of(t * 4 * sz.rows, 4 * sz.rows), 4 * sz.rows)
        for table in range(2):
            part = rows[:, table * width : (table + 1) * width]
            wide = jnp.concatenate([part] * 4, axis=1)
            laid = dot_as(wide, spread, 0, 0)
            spread_grads[table, :, at] = jnp.where(mask, laid, 0.0).astype(BF16)
        return 0

    lax.fori_loop(0, nb, lay, 0)

    for load in loads[6:]:
        load.wait()
    gu_rows = gu[...].reshape(total, embed)
    gw3[...] = dot_as(act2[...], gu_rows, 0, 0)
    gw2[...] = dot_as(act1[...], gps[...], 0, 0)
    gw1[...] = dot_as(x[...], gpf[...], 0, 0)
    stores = [(gw3, gw3_out), (gw2, gw2_out)]
    for i in range(nc):
        stores.append((gw1.at[pl.ds(i * 128, width)], gw1_out.at[pl.ds(i * width, width)]))
        stores.append((gw1.at[pl.ds(i * 128 + width, width)], gw1_out.at[pl.ds(embed + i * width, width)]))
    stores.append((gw1.at[pl.ds(nc * 128, sz.demo_width)], gw1_out.at[pl.ds(2 * embed, sz.demo_width)]))
    stores = [pltpu.make_async_copy(s, d, out_sem.at[i]) for i, (s, d) in enumerate(stores)]
    for store in stores:
        store.start()
    demo = dot_as(buckets[...], gx[:, 128:256], 1, 0)
    demo_out[...] = demo.T[0 : sz.demo_width, :]
    gb1_out[...] = jnp.sum(gpf[...].astype(F32), axis=0, keepdims=True)
    gb2_out[...] = jnp.sum(gps[...].astype(F32), axis=0, keepdims=True)
    gb3_out[...] = jnp.sum(gu_rows.astype(F32), axis=0, keepdims=True)

    def line_store(out, slot, hh):
        at = pl.ds(pl.multiple_of(hh * 4 * LOW, 4 * LOW), 4 * LOW)
        return pltpu.make_async_copy(lines.at[slot], out.at[:, at], line_sem.at[slot])

    def put(slot, found, factor):
        for i in range(4):
            lines[slot, :, i * LOW : (i + 1) * LOW] = found[i * width : (i + 1) * width] * factor

    def bags(hh, _):
        for table, out in enumerate((watch_out, search_out)):
            n = hh * 2 + table
            slot = table * 2 + lax.rem(hh, 2)
            ring_load(n).wait()
            found = dot_as(spread_grads[table], ring[lax.rem(n, depth)], 1, 0)

            @pl.when(n + depth < 2 * parts)
            def _():
                ring_load(n + depth).start()

            @pl.when(hh >= 2)
            def _():
                line_store(out, slot, hh - 2).wait()

            put(slot, found, 1.0 / sz.bag)
            line_store(out, slot, hh).start()
        return 0

    lax.fori_loop(0, parts, bags, 0)

    for k in range(sz.tiles):
        low = slots[k, 1:2, :].astype(BF16)
        hot = one_where(low == iota((LOW, CHUNK), 0).astype(BF16), BF16)
        low_rows[k * CHUNK : (k + 1) * CHUNK, :] = hot.T
    high = jnp.concatenate([slots[k, 0:1, :] for k in range(sz.tiles)], axis=1).astype(BF16)
    values = jnp.concatenate([neg_rows[...], pos_rows[...]], axis=1)

    def scatter(n, _):
        left = []
        for i in range(8):
            at = (n * 8 + i).astype(F32).astype(BF16)
            left.append(jnp.where(high == at, values, jnp.zeros((), BF16)))
        found = dot_as(jnp.concatenate(left, axis=0), low_rows[...], 1, 0)
        for j in range(2):

            @pl.when(n >= 1)
            def _():
                line_store(table_out, 4 + j, (n - 1) * 2 + j).wait()

            put(4 + j, found[j * 4 * width : (j + 1) * 4 * width], 1.0)
            line_store(table_out, 4 + j, n * 2 + j).start()
        return 0

    lax.fori_loop(0, parts // 2, scatter, 0)
    for table, out in enumerate((watch_out, search_out)):
        for hh in (parts - 2, parts - 1):
            line_store(out, table * 2 + hh % 2, hh).wait()
    for j in range(2):
        line_store(table_out, 4 + j, parts - 2 + j).wait()
    for store in stores:
        store.wait()


def back(sz, args, kept):
    vmem = pl.BlockSpec(memory_space=pltpu.VMEM)
    hbm = pl.BlockSpec(memory_space=pl.ANY)
    total, nb = sz.total, sz.batch
    first, second = args["w_second"].shape
    embed, buckets = sz.embed, args["demo_table"].shape[0]
    dma = pltpu.SemaphoreType.DMA

    def shape(dims, kind=F32):
        return jax.ShapeDtypeStruct(dims, kind)

    table = shape((sz.width, sz.vocab))
    outs = [(table, hbm)] * 3 + [
        (shape((args["w_first"].shape)), hbm), (shape((first, second)), hbm), (shape((second, embed)), hbm),
        (shape((sz.demo_width, buckets)), vmem), (shape((1, first)), vmem), (shape((1, second)), vmem),
        (shape((1, embed)), vmem),
    ]
    slots = sz.tiles * CHUNK
    return pl.pallas_call(
        functools.partial(back_kernel, sz),
        out_shape=[o for o, _ in outs],
        in_specs=[vmem] * 3 + [hbm] * 11,
        out_specs=[s for _, s in outs],
        scratch_shapes=[
            pltpu.VMEM((total, sz.x_width), BF16), pltpu.VMEM((total, first), BF16),
            pltpu.VMEM((total, first), BF16), pltpu.VMEM((total, second), BF16),
            pltpu.VMEM((total, second), BF16), pltpu.VMEM((nb, sz.rows, embed), BF16),
            pltpu.VMEM((buckets, total), BF16), pltpu.VMEM(args["w_first"].shape, BF16),
            pltpu.VMEM((256, first), BF16), pltpu.VMEM((first, second), BF16),
            pltpu.VMEM((second, embed), BF16), pltpu.VMEM((total, second), BF16),
            pltpu.VMEM((total, first), BF16), pltpu.VMEM((total, 256), BF16),
            pltpu.VMEM((2, 4 * sz.width, 4 * total), BF16), pltpu.VMEM((4, 4 * total, LOW), BF16),
            pltpu.VMEM((6, sz.width, 4 * LOW), F32), pltpu.VMEM((slots, LOW), BF16),
            pltpu.VMEM((sz.x_width, first), F32), pltpu.VMEM((first, second), F32),
            pltpu.VMEM((second, embed), F32),
            dma((10,)), dma((4,)), dma((6,)), dma((3 + 2 * sz.col,)),
        ],
        compiler_params=pltpu.CompilerParams(vmem_limit_bytes=62 * 2**20),
        name="back",
    )(*kept, args["w_first"], args["w_second"], args["w_third"])


def fast_device(sz, *inputs):
    names = (
        "watch_ids", "search_ids", "demo_ids", "pos_ids", "neg_ids", "valid_counts", "watch_table",
        "search_table", "demo_table", "out_table", "w_first", "b_first", "w_second", "b_second",
        "w_third", "b_third",
    )
    args = dict(zip(names, inputs))
    (
        counts, x, act1, slope1, act2, slope2, gu, buckets, neg_rows, pos_rows, slots, user_vecs, loss, fits,
    ) = front(sz, args)

    def finish(*operands):
        kept = (neg_rows, pos_rows, slots, counts, x, act1, slope1, act2, slope2, gu, buckets)
        watch, search, table, gw1, gw2, gw3, demo, gb1, gb2, gb3 = back(sz, args, kept)
        return (
            user_vecs, loss.reshape(()), watch, search, table, demo.T, gw1, gb1.reshape(-1),
            gw2, gb2.reshape(-1), gw3, gb3.reshape(-1),
        )

    def general(*operands):
        return per_device(RingCollectives(), *operands)

    return lax.cond(fits.reshape(()) > 0, finish, general, *inputs)


def fast_sizes(mesh, shapes):
    watch, demo, negs, table, first = shapes
    batch, col = mesh.shape["batch"], mesh.shape["col"]
    rows, width, vocab = watch[0] // batch, table[0] // col, table[1] // batch
    demo_width = first[0] - 2 * table[0]
    sz = Sizes(batch, col, rows, watch[1], width, vocab, negs[0], table[0], demo_width)
    good = (
        batch == 8 and col == 4 and rows == 128 and watch[1] <= BAG_PAD and width == 64
        and vocab == 32 * LOW and table[1] <= 65536 and demo[1] <= 4 and demo_width <= 128
        and negs[0] % 128 == 0 and negs[0] <= 256 * CHUNK
    )
    return sz if good else None


def solution(mesh):
    in_specs = (
        P("batch", None),
        P("batch", None),
        P("batch", None),
        P("batch"),
        P(),
        P("batch"),
        P("col", "batch"),
        P("col", "batch"),
        P(),
        P("col", "batch"),
        P(),
        P(),
        P(),
        P(),
        P(),
        P(),
    )
    out_specs = (
        P(("batch", "col"), None),
        P(),
        P("col", "batch"),
        P("col", "batch"),
        P("col", "batch"),
        P(),
        P(),
        P(),
        P(),
        P(),
        P(),
        P(),
    )
    def whole(*inputs):
        shapes = [inputs[i].shape for i in (0, 2, 4, 6, 10)]
        sz = fast_sizes(mesh, shapes)
        if sz is None:
            body = functools.partial(per_device, Collectives())
        else:
            body = functools.partial(fast_device, sz)
        return jax.shard_map(
            body, mesh=mesh, in_specs=in_specs, out_specs=out_specs, check_vma=False
        )(*inputs)

    return whole
```

```python
import functools
import math

import jax
import jax.numpy as jnp
from jax import lax
from jax.experimental import pallas as pl
from jax.experimental.pallas import tpu as pltpu
from jax.sharding import PartitionSpec as P


def contract_rows(left, right):
    return lax.dot_general(
        left, right, (((0,), (0,)), ((), ())), preferred_element_type=jnp.float32
    )


def contract_cols(left, right):
    return lax.dot_general(
        left, right, (((1,), (1,)), ((), ())), preferred_element_type=jnp.float32
    )


def gelu_back(pre_value, grad_value):
    return jax.vjp(jax.nn.gelu, pre_value)[1](grad_value)[0]


class Collectives:
    def gather(self, value, name, axis):
        return lax.all_gather(value, name, axis=axis, tiled=True)

    def scatter_sum(self, value, name, axis):
        return lax.psum_scatter(value, name, scatter_dimension=axis, tiled=True)

    def total(self, values, name):
        return lax.psum(values, name)


class RingCollectives:
    def shift(self, value, name):
        size = lax.axis_size(name)
        return lax.ppermute(value, name, [(i, (i + 1) % size) for i in range(size)])

    def stack(self, value, name):
        size, me = lax.axis_size(name), lax.axis_index(name)
        held = [value]
        for _ in range(size - 1):
            held.append(self.shift(held[-1], name))
        return jnp.take(jnp.stack(held), (me - jnp.arange(size)) % size, axis=0)

    def gather(self, value, name, axis):
        parts = self.stack(value, name)
        return jnp.concatenate([parts[i] for i in range(parts.shape[0])], axis=axis)

    def ring_sum(self, parts, name):
        size, me = lax.axis_size(name), lax.axis_index(name)
        held = jnp.take(parts, (me - 1) % size, axis=0)
        for step in range(1, size):
            held = self.shift(held, name) + jnp.take(parts, (me - 1 - step) % size, axis=0)
        return held

    def scatter_sum(self, value, name, axis):
        size = lax.axis_size(name)
        return self.ring_sum(jnp.stack(jnp.split(value, size, axis=axis)), name)

    def total(self, values, name):
        size = lax.axis_size(name)
        flat = jnp.concatenate([v.reshape(-1) for v in values])
        length = -(-flat.shape[0] // (size * 128)) * 128
        parts = jnp.pad(flat, (0, size * length - flat.shape[0])).reshape(size, length)
        whole = self.stack(self.ring_sum(parts, name), name).reshape(-1)
        out, at = [], 0
        for v in values:
            out.append(whole[at : at + v.size].reshape(v.shape))
            at += v.size
        return tuple(out)


def per_device(
    comm,
    watch_ids,
    search_ids,
    demo_ids,
    pos_ids,
    neg_ids,
    valid_counts,
    watch_table,
    search_table,
    demo_table,
    out_table,
    w_first,
    b_first,
    w_second,
    b_second,
    w_third,
    b_third,
):
    row_count = watch_ids.shape[0]
    bag_size = watch_ids.shape[1]
    col_width = watch_table.shape[0]
    vocab_rows = watch_table.shape[1]
    embed_width = col_width * lax.axis_size("col")
    offset = lax.axis_index("batch") * vocab_rows
    col_slot = lax.axis_index("col")
    quarter = row_count // lax.axis_size("col")
    low_width = math.gcd(vocab_rows, 128)
    high_width = vocab_rows // low_width

    def owned(id_values):
        local_ids = id_values - offset
        return jnp.where((local_ids >= 0) & (local_ids < vocab_rows), local_ids, vocab_rows)

    def bag_counts(id_block):
        local_ids = owned(id_block)
        high_hot = (
            local_ids[:, :, None] // low_width == jnp.arange(high_width)[None, None, :]
        ).astype(jnp.bfloat16)
        low_hot = (
            local_ids[:, :, None] % low_width == jnp.arange(low_width)[None, None, :]
        ).astype(jnp.bfloat16)
        counted = jnp.einsum("rbh,rbl->rhl", high_hot, low_hot, preferred_element_type=jnp.bfloat16)
        return counted.reshape(id_block.shape[0], vocab_rows)

    def single_hot(id_block):
        return (owned(id_block)[:, None] == jnp.arange(vocab_rows)[None, :]).astype(jnp.bfloat16)

    zero_col = jnp.zeros((col_width, 1), jnp.bfloat16)
    padded_out = jnp.concatenate([out_table, zero_col], axis=1)
    all_watch, all_search, all_pos = (
        comm.gather(watch_ids, "batch", 0),
        comm.gather(search_ids, "batch", 0),
        comm.gather(pos_ids, "batch", 0),
    )
    total_rows = all_watch.shape[0]
    block_rows = min(1024, total_rows)
    block_count = total_rows // block_rows
    neg_local = owned(neg_ids)
    neg_part = jnp.take(padded_out, neg_local, axis=1).astype(jnp.float32)

    def flatten_blocks(stacked):
        return stacked.transpose(1, 0, 2).reshape(col_width, total_rows)

    def bag_block(inputs_block):
        watch_block, search_block, pos_block = inputs_block
        watch_part = contract_cols(watch_table, bag_counts(watch_block))
        search_part = contract_cols(search_table, bag_counts(search_block))
        pos_part = contract_cols(out_table, single_hot(pos_block))
        return (watch_part, search_part, pos_part)

    id_blocks = (
        all_watch.reshape(block_count, block_rows, bag_size),
        all_search.reshape(block_count, block_rows, bag_size),
        all_pos.reshape(block_count, block_rows),
    )
    watch_parts, search_parts, pos_parts = lax.map(bag_block, id_blocks)
    watch_sum, search_sum, pos_rows = (
        comm.scatter_sum(flatten_blocks(watch_parts), "batch", 1),
        comm.scatter_sum(flatten_blocks(search_parts), "batch", 1),
        comm.scatter_sum(flatten_blocks(pos_parts), "batch", 1),
    )
    neg_rows, valid_total = comm.total(
        (neg_part, jnp.sum(valid_counts).astype(jnp.float32)), "batch"
    )
    pooled_watch = (watch_sum / bag_size).astype(jnp.bfloat16)
    pooled_search = (search_sum / bag_size).astype(jnp.bfloat16)
    pos_bf = pos_rows.astype(jnp.bfloat16)
    neg_bf = neg_rows.astype(jnp.bfloat16)
    count_here = valid_counts[0]
    full_watch, full_search, full_pos, full_neg = (
        comm.gather(pooled_watch, "col", 0),
        comm.gather(pooled_search, "col", 0),
        comm.gather(pos_bf, "col", 0),
        comm.gather(neg_bf, "col", 0),
    )
    watch_rows = full_watch.T
    search_rows = full_search.T
    pos_full = full_pos.T
    live_rows = jnp.arange(row_count) < count_here
    weight = jnp.where(live_rows, 1.0 / valid_total, 0.0)
    buckets = demo_table.shape[0]
    bucket_counts = jnp.sum(
        (demo_ids[:, :, None] == jnp.arange(buckets)[None, None, :]).astype(jnp.float32), axis=1
    ).astype(jnp.bfloat16)
    demo_vec = jnp.dot(bucket_counts, demo_table, preferred_element_type=jnp.float32)
    joined = jnp.concatenate([watch_rows, search_rows, demo_vec.astype(jnp.bfloat16)], axis=1)
    pre_first = jnp.dot(joined, w_first, preferred_element_type=jnp.float32) + b_first
    act_first = jax.nn.gelu(pre_first).astype(jnp.bfloat16)
    pre_second = jnp.dot(act_first, w_second, preferred_element_type=jnp.float32) + b_second
    act_second = jax.nn.gelu(pre_second).astype(jnp.bfloat16)
    user_block = (
        jnp.dot(act_second, w_third, preferred_element_type=jnp.float32) + b_third
    ).astype(jnp.bfloat16)
    neg_logits = jnp.dot(user_block, full_neg, preferred_element_type=jnp.float32)
    pos_logit = jnp.sum(user_block.astype(jnp.float32) * pos_full.astype(jnp.float32), axis=1)
    row_peak = jnp.maximum(jnp.max(neg_logits, axis=1), pos_logit)
    exp_neg = jnp.exp(neg_logits - row_peak[:, None])
    exp_pos = jnp.exp(pos_logit - row_peak)
    row_total = jnp.sum(exp_neg, axis=1) + exp_pos
    lse = row_peak + jnp.log(row_total)
    loss_here = jnp.sum(weight * (lse - pos_logit))
    grad_neg = (weight[:, None] * exp_neg / row_total[:, None]).astype(jnp.bfloat16)
    grad_pos = (weight * (exp_pos / row_total - 1.0)).astype(jnp.bfloat16)
    grad_user = (
        contract_cols(grad_neg, full_neg)
        + grad_pos.astype(jnp.float32)[:, None] * pos_full.astype(jnp.float32)
    ).astype(jnp.bfloat16)
    neg_row_grad = contract_rows(user_block, grad_neg)
    pos_row_grad = (grad_pos.astype(jnp.float32)[:, None] * user_block.astype(jnp.float32)).astype(
        jnp.bfloat16
    )
    grad_w_third = contract_rows(act_second, grad_user)
    grad_b_third = jnp.sum(grad_user.astype(jnp.float32), axis=0)
    grad_pre_second = gelu_back(pre_second, contract_cols(grad_user, w_third)).astype(jnp.bfloat16)
    grad_w_second = contract_rows(act_first, grad_pre_second)
    grad_b_second = jnp.sum(grad_pre_second.astype(jnp.float32), axis=0)
    grad_pre_first = gelu_back(pre_first, contract_cols(grad_pre_second, w_second)).astype(
        jnp.bfloat16
    )
    grad_w_first = contract_rows(joined, grad_pre_first)
    grad_b_first = jnp.sum(grad_pre_first.astype(jnp.float32), axis=0)
    grad_joined = contract_cols(grad_pre_first, w_first).astype(jnp.bfloat16)
    grad_pw = grad_joined[:, :embed_width]
    grad_ps = grad_joined[:, embed_width : 2 * embed_width]
    grad_demo = contract_rows(bucket_counts, grad_joined[:, 2 * embed_width :])
    col_start = col_slot * col_width
    own_pw = lax.dynamic_slice_in_dim(grad_pw, col_start, col_width, 1).T
    own_ps = lax.dynamic_slice_in_dim(grad_ps, col_start, col_width, 1).T
    own_pos = lax.dynamic_slice_in_dim(pos_row_grad, col_start, col_width, 1).T
    user_vecs = lax.dynamic_slice_in_dim(user_block, col_slot * quarter, quarter, 0)
    all_pw, all_ps, all_dpos = (
        comm.gather(own_pw, "batch", 1),
        comm.gather(own_ps, "batch", 1),
        comm.gather(own_pos, "batch", 1),
    )
    neg_own = lax.dynamic_slice_in_dim(neg_row_grad, col_slot * col_width, col_width, 0)
    sums_out = comm.total(
        (
            grad_w_first,
            grad_b_first,
            grad_w_second,
            grad_b_second,
            grad_w_third,
            grad_b_third,
            grad_demo,
            neg_own,
            loss_here,
        ),
        "batch",
    )
    neg_sum_own = sums_out[7]

    def split_blocks(columns):
        return columns.reshape(col_width, block_count, block_rows).transpose(1, 0, 2)

    def grad_block(running, inputs_block):
        watch_block, search_block, pos_block, block_pw, block_ps, block_pos = inputs_block
        new_watch = running[0] + jnp.dot(
            block_pw, bag_counts(watch_block), preferred_element_type=jnp.float32
        )
        new_search = running[1] + jnp.dot(
            block_ps, bag_counts(search_block), preferred_element_type=jnp.float32
        )
        new_out = running[2] + jnp.dot(
            block_pos, single_hot(pos_block), preferred_element_type=jnp.float32
        )
        return ((new_watch, new_search, new_out), None)

    zeros_table = jnp.zeros((col_width, vocab_rows), jnp.float32)
    (table_watch, table_search, table_out), _ = lax.scan(
        grad_block,
        (zeros_table, zeros_table, zeros_table),
        id_blocks + (split_blocks(all_pw), split_blocks(all_ps), split_blocks(all_dpos)),
    )
    neg_added = (
        jnp.zeros((col_width, vocab_rows + 1), jnp.float32).at[:, neg_local].add(neg_sum_own)
    )
    table_out = table_out + neg_added[:, :vocab_rows]
    return (
        user_vecs,
        sums_out[8],
        table_watch / bag_size,
        table_search / bag_size,
        table_out,
        sums_out[6],
        sums_out[0],
        sums_out[1],
        sums_out[2],
        sums_out[3],
        sums_out[4],
        sums_out[5],
    )


F32, BF16, FP8, I32 = jnp.float32, jnp.bfloat16, jnp.float8_e4m3fn, jnp.int32
MESH = pl.DeviceIdType.MESH
LOW = 256
ROWS_IN_GROUP = 4
BAG_PAD = 64
CHUNK = 256
NEG_FLOOR = -1e30


def dot_as(left, right, left_dim, right_dim):
    return lax.dot_general(
        left, right, (((left_dim,), (right_dim,)), ((), ())), preferred_element_type=F32
    )


def iota(shape, dim):
    return lax.broadcasted_iota(I32, shape, dim)


def one_where(mask, kind):
    return jnp.where(mask, jnp.ones((), BF16), jnp.zeros((), BF16)).astype(kind)


def slot_cap(neg_count, batch):
    mean = neg_count / batch
    return int(math.ceil((mean + 4.5 * math.sqrt(mean)) / CHUNK)) * CHUNK


def gelu(pre):
    bent = jnp.tanh(math.sqrt(2.0 / math.pi) * (pre + 0.044715 * (pre * pre * pre)))
    return 0.5 * pre * (1.0 + bent)


def gelu_slope(pre):
    inner_scale = math.sqrt(2.0 / math.pi)
    square = pre * pre
    bent = jnp.tanh(inner_scale * (pre + 0.044715 * (square * pre)))
    return 0.5 * (1.0 + bent) + 0.5 * pre * (1.0 - bent * bent) * (
        inner_scale * (1.0 + 3.0 * 0.044715 * square)
    )


class Sizes:
    def __init__(self, batch, col, rows, bag, width, vocab, negs, embed, demo_width):
        self.batch, self.col, self.rows, self.bag = batch, col, rows, bag
        self.width, self.vocab, self.negs, self.embed = width, vocab, negs, embed
        self.demo_width = demo_width
        self.total = batch * rows
        self.quarter = rows // col
        self.users = batch * self.quarter
        self.groups = rows // ROWS_IN_GROUP
        self.high = vocab // LOW
        self.high_parts = self.high // 4
        self.cap = slot_cap(negs, batch)
        self.cap_tiles = self.cap // CHUNK
        self.tiles = self.cap_tiles + col
        self.neg_lines = -(-negs // (CHUNK * 8)) * 8
        self.steps = 4
        self.span = self.total // self.steps
        self.x_width = col * 128 + 128


def front_kernel(
    sz,
    watch_ids, search_ids, demo_ids, pos_ids, neg_ids, demo_table, b_first, b_second, b_third, valid_count,
    watch_table, search_table, out_table, w_first, w_second, w_third,
    counts_out, x_out, act1_out, act2_out, gu_out, gps_out, gpf_out, gx_out, buckets_out,
    neg_rows_out, pos_rows_out, slots_out, user_out, loss_out, fits_out,
    tabs, tall, mix, w1_raw, w1, w1_own, w2, w3, turned, upright, lines_own, ids, side, neg_dest, neg_digits, counts, found_sums, sums, pieces, x,
    pre1, pre2, acts1, slopes1, acts2, slopes2, users, buckets, slots, picked, neg_all, pos_all, e_cols,
    e_rows, probs, stats, g_send, g_recv, gu, gps, gpf, gx, rg_send, rg_recv, gp_all, loss_all,
    local_sem, out_sem, down_sem, count_sem, ids_s, ids_r, sd_s, sd_r, ic_s, ic_r, rs_s, rs_r, ag_s, ag_r, xx_s, xx_r, co_s, co_r,
    ne_s, ne_r, pe_s, pe_r, st_s, st_r, gs_s, gs_r, ga_s, ga_r, gx_s, gx_r, gc_s, gc_r,
    rg_s, rg_r, gp_s, gp_r, lo_s, lo_r,
):
    b, c = lax.axis_index("batch"), lax.axis_index("col")
    nb, nc = sz.batch, sz.col
    offset = b * sz.vocab
    cap, width, embed = sz.cap, sz.width, sz.embed
    cx = lax.rem(c + 2, nc)
    ck = c + 1 - 2 * lax.rem(c, 2)
    ckx = lax.rem(ck + 2, nc)

    def batch_peer(i):
        return lax.rem(b + i, nb)

    def batch_from(i):
        return lax.rem(b + nb - i, nb)

    def col_peer(i):
        return lax.rem(c + i, nc)

    def col_from(i):
        return lax.rem(c + nc - i, nc)

    def send(src, dst, ssem, rsem, to):
        return pltpu.make_async_remote_copy(
            src_ref=src, dst_ref=dst, send_sem=ssem, recv_sem=rsem,
            device_id=to, device_id_type=MESH,
        )

    barrier = pltpu.get_barrier_semaphore()
    for i in range(1, nb):
        pl.semaphore_signal(barrier, inc=1, device_id=(batch_peer(i), c), device_id_type=MESH)
    for i in range(1, nc):
        pl.semaphore_signal(barrier, inc=1, device_id=(b, col_peer(i)), device_id_type=MESH)

    loads = [
        (watch_table, tabs.at[0]), (search_table, tabs.at[1]), (out_table, tabs.at[2]),
        (w_first, w1_raw), (w_second, w2), (w_third, w3),
    ]
    loads = [pltpu.make_async_copy(s, d, local_sem.at[i]) for i, (s, d) in enumerate(loads)]
    for load in loads:
        load.start()

    turned[...] = jnp.zeros((BAG_PAD, 128), I32)
    turned[0 : sz.bag, :] = (watch_ids[...] & 0xFFFF) | (search_ids[...] << 16)
    upright[...] = turned[...].T
    for r4 in range(ROWS_IN_GROUP):
        lines_own[:, r4 * BAG_PAD : (r4 + 1) * BAG_PAD] = upright[
            pl.ds(r4, sz.groups, stride=ROWS_IN_GROUP), :
        ]
    share = sz.groups // nc

    def share_of(col):
        return pl.ds(pl.multiple_of(col * share, share), share)

    ids[b, share_of(c), :] = lines_own[share_of(c), :]
    side[b] = jnp.zeros((8, 128), I32)
    side[b, 0:1, :] = pos_ids[...]
    side[b, 1:2, :] = jnp.full((1, 128), valid_count[0], I32)
    side[b, 2 : 2 + demo_ids.shape[0], :] = demo_ids[...]

    pl.semaphore_wait(barrier, nb - 1 + nc - 1)
    last_sends = []
    for i in range(1, nb):
        place = ids.at[b, share_of(c)]
        copy = send(place, place, ids_s.at[i - 1], ids_r.at[i - 1], (batch_peer(i), c))
        copy.start()
        last_sends.append(copy)

    for i in range(1, nb):
        copy = send(side.at[b], side.at[b], sd_s.at[i - 1], sd_r.at[i - 1], (batch_peer(i), c))
        copy.start()
        last_sends.append(copy)

    negs = neg_ids[...]
    lines = sz.neg_lines
    missing = 2 * lines - negs.shape[0]
    second = jnp.concatenate([negs[lines:], jnp.full((missing, 128), -1, I32)], axis=0)
    negs = jnp.concatenate([negs[:lines], second], axis=1)
    neg_local = negs - offset
    own = (neg_local >= 0) & (neg_local < sz.vocab)
    own_bf = one_where(own, BF16)
    upper = one_where(iota((CHUNK, CHUNK), 0) < iota((CHUNK, CHUNK), 1), BF16)
    before = dot_as(own_bf, upper, 1, 0)
    in_row = dot_as(own_bf, jnp.ones((CHUNK, CHUNK), BF16), 1, 0)
    lower = one_where(iota((lines, lines), 1) < iota((lines, lines), 0), BF16)
    rows_before = dot_as(lower, in_row.astype(BF16), 1, 0)
    neg_dest[...] = jnp.where(own, before + rows_before, -1.0)
    owned_count = dot_as(jnp.ones((8, lines), BF16), in_row.astype(BF16), 1, 0)
    most = jnp.zeros((1, 1), F32)
    for shard in range(nb):
        part = negs - shard * sz.vocab
        hits = jnp.where((part >= 0) & (part < sz.vocab), 1.0, 0.0)
        most = jnp.maximum(most, jnp.sum(jnp.sum(hits, axis=1, keepdims=True), axis=0, keepdims=True))
    fits_out[...] = jnp.where(most <= float(cap), 1, 0)
    for digit in range(4):
        neg_digits[digit] = ((neg_local >> (4 * digit)) & 15).astype(F32)

    def compact(k, total):
        place = neg_dest[pl.ds(k, 1), :]
        hot = one_where(place == iota((cap, CHUNK), 0).astype(F32), FP8)
        line = iota((32, CHUNK), 0)
        value = jnp.where(line == 4, 1.0, 0.0)
        for digit in range(4):
            value = jnp.where(line == digit, neg_digits[digit, pl.ds(k, 1), :], value)
        return total + dot_as(value.astype(FP8), hot, 1, 1)

    slot = lax.fori_loop(0, lines, compact, jnp.zeros((32, cap), F32))
    neg_low = slot[0:1] + 16.0 * slot[1:2]
    neg_high = jnp.where(slot[4:5] > 0.5, slot[2:3] + 16.0 * slot[3:4], -1.0)
    slots[...] = jnp.zeros((sz.tiles, 8, CHUNK), F32)
    for k in range(sz.cap_tiles):
        slots[k, 0:1, :] = neg_high[:, k * CHUNK : (k + 1) * CHUNK]
        slots[k, 1:2, :] = neg_low[:, k * CHUNK : (k + 1) * CHUNK]

    for i in range(1, nb):
        place = ids.at[batch_from(i), share_of(c)]
        send(place, place, ids_s.at[i - 1], ids_r.at[i - 1], (b, c)).wait_recv()
    for i in range(1, nc):
        place = ids.at[:, share_of(c)]
        copy = send(place, place, ic_s.at[i - 1], ic_r.at[i - 1], (b, col_peer(i)))
        copy.start()
        last_sends.append(copy)
    for t in range(2):
        loads[t].wait()

    def turn(n, _):
        t, hh = n // sz.high_parts, n % sz.high_parts
        base = pl.multiple_of(hh * 4 * LOW, 4 * LOW)
        stack = jnp.concatenate([tabs[t, :, pl.ds(base + i * LOW, LOW)] for i in range(4)], axis=0)
        mix[t, pl.ds(pl.multiple_of(hh * LOW, LOW), LOW), :] = stack.T
        return 0

    lax.fori_loop(0, 2 * sz.high_parts, turn, 0)

    loads[2].wait()

    def stack_up(hh, _):
        for i in range(4):
            tall[pl.ds(pl.multiple_of((hh * 4 + i) * width, width), width), :] = tabs[
                2, :, pl.ds(pl.multiple_of((hh * 4 + i) * LOW, LOW), LOW)
            ]
        return 0

    lax.fori_loop(0, sz.high_parts, stack_up, 0)

    def pick_tile(k, _):
        high, low = slots[k, 0:1, :], slots[k, 1:2, :]
        low_hot = one_where(low.astype(BF16) == iota((LOW, CHUNK), 0).astype(BF16), BF16)
        total = jnp.zeros((width, CHUNK), F32)
        for part in range(4):
            tall_rows = width * sz.high // 4
            got = dot_as(tall[part * tall_rows : (part + 1) * tall_rows, :], low_hot, 1, 0)
            for i in range(sz.high // 4):
                at = float(part * (sz.high // 4) + i)
                total = total + jnp.where(high == at, got[i * width : (i + 1) * width], 0.0)
        picked[k] = total.astype(BF16)
        return 0

    lax.fori_loop(0, sz.cap_tiles, pick_tile, 0)
    neg_part = picked.at[pl.ds(0, sz.cap_tiles)]
    for i in range(1, nc):
        copy = send(neg_part, neg_all.at[c], ne_s.at[i - 1], ne_r.at[i - 1], (b, col_peer(i)))
        copy.start()
        last_sends.append(copy)
    for k in range(sz.cap_tiles):
        neg_all[c, k] = picked[k]

    loads[3].wait()
    w1[nc * 128 :, :] = jnp.zeros((128, w1.shape[1]), BF16)
    for i in range(nc):
        w1[i * 128 : i * 128 + width, :] = w1_raw[i * width : (i + 1) * width, :]
        w1[i * 128 + width : (i + 1) * 128, :] = w1_raw[embed + i * width : embed + (i + 1) * width, :]
    w1[nc * 128 : nc * 128 + sz.demo_width, :] = w1_raw[2 * embed :, :]
    loads[4].wait()
    loads[5].wait()

    w1_own[...] = jnp.zeros(w1_own.shape, BF16)
    w1_own[0 : 2 * width, :] = w1[pl.ds(pl.multiple_of(c * 128, 128), 128), :]
    w1_own[2 * width : 2 * width + sz.demo_width, :] = w1_raw[2 * embed :, :]
    for i in range(1, nc):
        place = ids.at[:, share_of(col_from(i))]
        send(place, place, ic_s.at[i - 1], ic_r.at[i - 1], (b, c)).wait_recv()

    users_shape = (nb, CHUNK)
    at_block = iota(users_shape, 1) // sz.quarter == iota(users_shape, 0)

    def demo_part():
        for i in range(1, nb):
            place = side.at[batch_from(i)]
            send(place, place, sd_s.at[i - 1], sd_r.at[i - 1], (b, c)).wait_recv()
        bucket_total = jnp.zeros((buckets.shape[0], sz.total), BF16)
        bucket_line = iota((buckets.shape[0], sz.total), 0).astype(BF16)
        for field in range(demo_ids.shape[0]):
            line = jnp.concatenate([side[j, 2 + field : 3 + field, :] for j in range(nb)], axis=1)
            bucket_total = bucket_total + one_where(line.astype(F32).astype(BF16) == bucket_line, BF16)
        buckets[...] = bucket_total
        demo_rows = demo_table[...].astype(F32).T.astype(BF16)
        x[:, nc * 128 :] = jnp.zeros((sz.total, 128), BF16)
        x[:, nc * 128 : nc * 128 + sz.demo_width] = dot_as(bucket_total, demo_rows, 0, 0).astype(BF16)

    def pos_part():
        all_pos = jnp.concatenate([side[j, 0:1, :] for j in range(nb)], axis=0)
        pos_local = all_pos - offset
        pos_owned = (pos_local >= 0) & (pos_local < sz.vocab)
        pos_pair = jnp.concatenate(
            [
                jnp.where(pos_owned, pos_local >> 8, 255).astype(F32),
                (pos_local & 255).astype(F32),
            ],
            axis=0,
        ).astype(BF16)
        for quarter in range(nc):
            shape = (128, CHUNK)
            pick = one_where(iota(shape, 0) == quarter * sz.quarter + iota(shape, 1) % sz.quarter, BF16)
            wide = dot_as(pos_pair, pick, 1, 0)
            high = jnp.sum(jnp.where(at_block, wide[0:nb], 0.0), axis=0, keepdims=True)
            low = jnp.sum(jnp.where(at_block, wide[nb : 2 * nb], 0.0), axis=0, keepdims=True)
            slots[sz.cap_tiles + quarter, 0:1, :] = jnp.where(high > 254.0, -1.0, high)
            slots[sz.cap_tiles + quarter, 1:2, :] = low
        slots_out[...] = slots[...]
        lax.fori_loop(sz.cap_tiles, sz.tiles, pick_tile, 0)
        pos_all[c] = picked[sz.cap_tiles + c]
        for i in range(1, nc):
            pos_send(i).start()

    def pos_send(i):
        to = col_peer(i)
        return send(picked.at[sz.cap_tiles + to], pos_all.at[c], pe_s.at[i - 1], pe_r.at[i - 1], (b, to))

    span = sz.span
    piece = span // nb
    lane_mod = iota((16, CHUNK), 1) % BAG_PAD
    lane_r4 = iota((16, CHUNK), 1) // BAG_PAD
    blocks = span // sz.rows
    parts_in_block = sz.groups // 16

    def count_copy(t, table, slot_at):
        rows = pl.ds(pl.multiple_of(t * span, span), span)
        return pltpu.make_async_copy(
            counts.at[table, slot_at], counts_out.at[table, :, :, rows], count_sem.at[table, slot_at]
        )

    def bag_table(t, table):
        slot_at = lax.rem(t, 2)

        @pl.when(t >= 2)
        def _():
            count_copy(t - 2, table, slot_at).wait()

        code_line = iota((4 * sz.high, CHUNK), 0).astype(BF16)
        low_line = iota((LOW, CHUNK), 0).astype(BF16)

        def groups_of(q, _):
            block = t * blocks + q // parts_in_block
            word = ids[block, pl.ds(pl.multiple_of((q % parts_in_block) * 16, 16), 16), :]
            value = lax.shift_right_logical(word, 16 * table) & 0xFFFF
            local = value - offset
            mine = (local >= 0) & (local < sz.vocab) & (lane_mod < sz.bag)
            code = jnp.where(mine, (local >> 8) * 4 + lane_r4, -1).astype(F32).astype(BF16)
            low = (local & 255).astype(F32).astype(BF16)
            low_half = iota((sz.high // 2, 8, LOW), 1) < 4
            for quad in range(4):
                pairs = []
                for pair in range(2):
                    found = []
                    for g in (quad * 4 + pair * 2, quad * 4 + pair * 2 + 1):
                        left = one_where(code[g : g + 1, :] == code_line, FP8)
                        right = one_where(low[g : g + 1, :] == low_line, FP8)
                        found.append(dot_as(left, right, 1, 1).reshape(sz.high // 2, 8, LOW))
                    even = jnp.where(low_half, found[0], pltpu.roll(found[1], 4, 1))
                    odd = jnp.where(low_half, pltpu.roll(found[0], 4, 1), found[1])
                    pairs.append((even, odd))
                line = pl.ds(pl.multiple_of(q * 64 + quad * 16, 16), 16)
                for part in range(sz.high):
                    both = [pairs[k][part % 2][part // 2] for k in range(2)]
                    counts[table, slot_at, part // 4, part % 4, line, :] = jnp.concatenate(
                        both, axis=0
                    ).astype(BF16)
            return 0

        lax.fori_loop(0, blocks * parts_in_block, groups_of, 0)
        count_copy(t, table, slot_at).start()
        left = jnp.concatenate(
            [counts[table, slot_at, hh].reshape(4 * span, LOW) for hh in range(sz.high_parts)], axis=1
        )
        total = dot_as(left, mix[table], 1, 0)
        left_side = iota((span, 128), 1) < width
        first = jnp.where(left_side, total[0:span, 0:128], total[span : 2 * span, 0:128])
        second = jnp.where(left_side, total[2 * span : 3 * span, 128:], total[3 * span :, 128:])
        both = first + second
        found_sums[table] = both + pltpu.roll(both, width, 1)

    def bag_sums(t):
        joined = jnp.where(iota((span, 128), 1) < width, found_sums[0], found_sums[1])
        sums[t] = joined.astype(BF16)
        for i in range(1, nb):
            to = batch_peer(i)
            send(
                sums.at[t, pl.ds(pl.multiple_of(to * piece, piece), piece)], pieces.at[t, i - 1],
                rs_s.at[t, i - 1], rs_r.at[t], (to, c),
            ).start()

    def x_at(t, col):
        return x.at[
            pl.ds(pl.multiple_of(t * span, span), span), pl.ds(pl.multiple_of(col * 128, 128), 128)
        ]

    def x_piece(t, owner):
        return x.at[
            pl.ds(pl.multiple_of(t * span + owner * piece, piece), piece),
            pl.ds(pl.multiple_of(c * 128, 128), 128),
        ]

    def reduce_step(t):
        send(pieces.at[t], pieces.at[t], rs_s.at[t, 0], rs_r.at[t], (b, c)).wait_recv()
        total = sums[t, pl.ds(pl.multiple_of(b * piece, piece), piece), :].astype(F32)
        for i in range(nb - 1):
            total = total + pieces[t, i].astype(F32)
        x[
            pl.ds(pl.multiple_of(t * span + b * piece, piece), piece),
            pl.ds(pl.multiple_of(c * 128, 128), 128),
        ] = (total / sz.bag).astype(BF16)
        for i in range(1, nb):
            send(x_piece(t, b), x_piece(t, b), ag_s.at[t, i - 1], ag_r.at[t], (batch_peer(i), c)).start()

    def cross_step(t):
        send(pieces.at[t], pieces.at[t], ag_s.at[t, 0], ag_r.at[t], (b, c)).wait_recv()
        send(x_at(t, c), x_at(t, c), xx_s.at[t], xx_r.at[t], (b, cx)).start()

    def core_step(t):
        send(x_at(t, cx), x_at(t, cx), xx_s.at[t], xx_r.at[t], (b, cx)).wait_recv()
        send(x_at(t, c), x_at(t, c), co_s.at[t, 0], co_r.at[t, 0], (b, ck)).start()
        send(x_at(t, cx), x_at(t, cx), co_s.at[t, 1], co_r.at[t, 1], (b, ck)).start()

    def full_step(t):
        send(x_at(t, ck), x_at(t, ck), co_s.at[t, 0], co_r.at[t, 0], (b, ck)).wait_recv()
        send(x_at(t, ckx), x_at(t, ckx), co_s.at[t, 1], co_r.at[t, 1], (b, ck)).wait_recv()

    def tower(k):
        at = pl.ds(pl.multiple_of(k * span, span), span)
        pre = dot_as(x[at, :], w1[...], 1, 0) + b_first[...]
        pre1[at, :] = pre
        value = gelu(pre).astype(BF16)
        acts1[at, :] = value
        pre = dot_as(value, w2[...], 1, 0) + b_second[...]
        pre2[at, :] = pre
        value = gelu(pre).astype(BF16)
        acts2[at, :] = value
        users[at, :] = (dot_as(value, w3[...], 1, 0) + b_third[...]).astype(BF16)

    def slopes(k):
        at = pl.ds(pl.multiple_of(k * span, span), span)
        slopes1[at, :] = gelu_slope(pre1[at, :]).astype(BF16)
        slopes2[at, :] = gelu_slope(pre2[at, :]).astype(BF16)

    bag_ticks = 2 * sz.steps
    last = sz.steps - 1

    def tick(n, _):
        half = n // 2
        odd = lax.rem(n, 2) == 1

        @pl.when(n < bag_ticks)
        def _():
            bag_table(half, lax.rem(n, 2))

        @pl.when((n < bag_ticks) & odd)
        def _():
            bag_sums(half)

        @pl.when(n == bag_ticks)
        def _():
            demo_part()

        @pl.when(n == bag_ticks + 1)
        def _():
            pos_part()

        @pl.when(odd & (n >= 5))
        def _():
            full_step((n - 5) // 2)

        done = jnp.where(n <= bag_ticks, 0, jnp.where(n <= bag_ticks + 2, 1, last))
        ready = jnp.where(
            n < bag_ticks, 0, jnp.where(n <= bag_ticks + 1, 1, jnp.where(n == bag_ticks + 2, last, sz.steps))
        )

        def some_tower(k, _):
            tower(k)
            return 0

        lax.fori_loop(done, ready, some_tower, 0)

        @pl.when((~odd) & (n >= 2) & (n <= bag_ticks))
        def _():
            reduce_step(half - 1)

        @pl.when(odd & (n >= 3) & (n <= bag_ticks + 1))
        def _():
            cross_step((n - 3) // 2)

        @pl.when((~odd) & (n >= 4) & (n <= bag_ticks + 2))
        def _():
            core_step(half - 2)

        return 0

    lax.fori_loop(0, bag_ticks + 4, tick, 0)

    valid = jnp.concatenate([side[j, 1:2, :] for j in range(nb)], axis=0)
    valid_wide = jnp.concatenate([valid] * (sz.users // 128), axis=1).astype(F32)
    live_count = jnp.sum(jnp.where(at_block, valid_wide, 0.0), axis=0, keepdims=True)
    valid_total = jnp.sum(valid_wide, axis=0, keepdims=True)
    user_place = c * sz.quarter + iota((1, sz.users), 1) % sz.quarter
    weight = jnp.where(user_place.astype(F32) < live_count, 1.0 / valid_total, 0.0)

    out_copies = [(x, x_out), (acts1, act1_out), (acts2, act2_out), (buckets, buckets_out)]
    out_copies = [pltpu.make_async_copy(s, d, out_sem.at[i]) for i, (s, d) in enumerate(out_copies)]
    for copy in out_copies:
        copy.start()
    user_out[...] = users[pl.ds(pl.multiple_of(b * sz.rows + c * sz.quarter, sz.quarter), sz.quarter), :]

    for i in range(1, nc):
        src = col_from(i)
        send(neg_all.at[src], neg_all.at[src], ne_s.at[i - 1], ne_r.at[i - 1], (b, c)).wait_recv()
        send(pos_all.at[src], pos_all.at[src], pe_s.at[i - 1], pe_r.at[i - 1], (b, c)).wait_recv()
    for i in range(nc):
        for k in range(sz.cap_tiles):
            e_cols[i * width : (i + 1) * width, k * CHUNK : (k + 1) * CHUNK] = neg_all[i, k]
        e_cols[i * width : (i + 1) * width, cap:] = pos_all[i]
    e_rows[...] = e_cols[...].T

    def users_of(quarter):
        return jnp.concatenate(
            [
                users[pl.ds(pl.multiple_of(j * sz.rows + quarter * sz.quarter, sz.quarter), sz.quarter), :]
                for j in range(nb)
            ],
            axis=0,
        )

    quarter_users = users_of(c)
    logits = dot_as(e_rows[...], quarter_users, 1, 1)
    neg_logits, pos_logits = logits[0:cap], logits[cap:]
    slot_ok = iota((cap, sz.users), 0).astype(F32) < owned_count[0:1, : sz.users]
    pos_here = slots[sz.cap_tiles + c, 0:1, :]
    pos_ok = (iota((sz.users, sz.users), 0) == iota((sz.users, sz.users), 1)) & (pos_here >= 0.0)
    neg_logits = jnp.where(slot_ok, neg_logits, NEG_FLOOR)
    pos_masked = jnp.where(pos_ok, pos_logits, NEG_FLOOR)
    peak = jnp.maximum(
        jnp.max(neg_logits, axis=0, keepdims=True), jnp.max(pos_masked, axis=0, keepdims=True)
    )
    mass = jnp.sum(jnp.where(slot_ok, jnp.exp(neg_logits - peak), 0.0), axis=0, keepdims=True) + jnp.sum(
        jnp.where(pos_ok, jnp.exp(pos_masked - peak), 0.0), axis=0, keepdims=True
    )
    pos_value = jnp.sum(jnp.where(pos_ok, pos_logits, 0.0), axis=0, keepdims=True)
    stats[b] = jnp.concatenate([peak, mass, pos_value, jnp.zeros((5, sz.users), F32)], axis=0)
    for i in range(1, nb):
        copy = send(stats.at[b], stats.at[b], st_s.at[i - 1], st_r.at[i - 1], (batch_peer(i), c))
        copy.start()
        last_sends.append(copy)

    def some_slopes(k, _):
        slopes(k)
        return 0

    lax.fori_loop(0, sz.steps // 2, some_slopes, 0)
    for i in range(1, nb):
        src = batch_from(i)
        send(stats.at[src], stats.at[src], st_s.at[i - 1], st_r.at[i - 1], (b, c)).wait_recv()
    peaks = [stats[j, 0:1, :] for j in range(nb)]
    top = peaks[0]
    for j in range(1, nb):
        top = jnp.maximum(top, peaks[j])
    full_mass = jnp.zeros((1, sz.users), F32)
    pos_logit = jnp.zeros((1, sz.users), F32)
    for j in range(nb):
        full_mass = full_mass + stats[j, 1:2, :] * jnp.exp(peaks[j] - top)
        pos_logit = pos_logit + stats[j, 2:3, :]
    lse = top + jnp.log(full_mass)
    loss_part = jnp.sum(weight * (lse - pos_logit), axis=1, keepdims=True)
    scale = weight / full_mass
    probs[0:cap] = jnp.where(slot_ok, jnp.exp(neg_logits - top) * scale, 0.0).astype(BF16)
    pos_grad = weight * (jnp.exp(pos_logit - top) / full_mass - 1.0)
    probs[cap:] = jnp.where(pos_ok, pos_grad, 0.0).astype(BF16)
    grad_user = dot_as(probs[...], e_rows[...], 0, 0)
    for j in range(nb):
        g_send[j] = grad_user[j * sz.quarter : (j + 1) * sz.quarter].astype(BF16)
    for i in range(1, nb):
        to = batch_peer(i)
        copy = send(g_send.at[to], g_recv.at[i - 1], gs_s.at[i - 1], gs_r.at[i - 1], (to, c))
        copy.start()
        last_sends.append(copy)
    rows_grad = dot_as(probs[0:cap, :], quarter_users, 1, 0)
    rows_grad = rows_grad.T.astype(BF16)
    for i in range(nc):
        rg_send[i] = rows_grad[i * width : (i + 1) * width]
    gp_all[c] = jnp.broadcast_to(jnp.where(pos_here >= 0.0, pos_grad, 0.0), (8, sz.users))
    loss_all[c] = jnp.broadcast_to(loss_part, (8, 128))
    for i in range(1, nc):
        to = col_peer(i)
        for copy in (
            send(rg_send.at[to], rg_recv.at[c], rg_s.at[i - 1], rg_r.at[i - 1], (b, to)),
            send(gp_all.at[c], gp_all.at[c], gp_s.at[i - 1], gp_r.at[i - 1], (b, to)),
            send(loss_all.at[c], loss_all.at[c], lo_s.at[i - 1], lo_r.at[i - 1], (b, to)),
        ):
            copy.start()
            last_sends.append(copy)
    rg_recv[c] = rg_send[c]
    lax.fori_loop(sz.steps // 2, sz.steps, some_slopes, 0)
    for i in range(1, nb):
        send(g_send.at[0], g_recv.at[i - 1], gs_s.at[i - 1], gs_r.at[i - 1], (b, c)).wait_recv()
    total = g_send[b].astype(F32)
    for i in range(nb - 1):
        total = total + g_recv[i].astype(F32)

    def gu_at(block, col):
        return gu.at[block, pl.ds(pl.multiple_of(col * sz.quarter, sz.quarter), sz.quarter), :]

    def gu_all(col):
        return gu.at[:, pl.ds(pl.multiple_of(col * sz.quarter, sz.quarter), sz.quarter), :]

    gu[b, pl.ds(pl.multiple_of(c * sz.quarter, sz.quarter), sz.quarter), :] = total.astype(BF16)
    for i in range(1, nb):
        copy = send(gu_at(b, c), gu_at(b, c), ga_s.at[i - 1], ga_r.at[i - 1], (batch_peer(i), c))
        copy.start()
        last_sends.append(copy)
    for i in range(nb):
        src = batch_from(i)
        if i > 0:
            send(gu_at(src, c), gu_at(src, c), ga_s.at[i - 1], ga_r.at[i - 1], (b, c)).wait_recv()
        copy = send(gu_at(src, c), gu_at(src, c), gx_s.at[i], gx_r.at[i], (b, cx))
        copy.start()
        last_sends.append(copy)
    copy = send(gu_all(c), gu_all(c), gc_s.at[0], gc_r.at[0], (b, ck))
    copy.start()
    last_sends.append(copy)

    def rows_at(ref, col):
        return ref.at[:, pl.ds(pl.multiple_of(col * sz.quarter, sz.quarter), sz.quarter), :]

    def down_copies(col, i):
        return [
            pltpu.make_async_copy(rows_at(kept, col), rows_at(out, col), down_sem.at[i, k])
            for k, (kept, out) in enumerate(((gps, gps_out), (gpf, gpf_out), (gx, gx_out)))
        ]

    def down(i, col):
        def spread_out(ref, value):
            for j in range(nb):
                ref[j, pl.ds(pl.multiple_of(col * sz.quarter, sz.quarter), sz.quarter), :] = value[
                    j * sz.quarter : (j + 1) * sz.quarter
                ]

        def gathered(ref):
            return jnp.concatenate(
                [
                    ref[pl.ds(pl.multiple_of(j * sz.rows + col * sz.quarter, sz.quarter), sz.quarter), :]
                    for j in range(nb)
                ],
                axis=0,
            )

        top = jnp.concatenate(
            [gu[j, pl.ds(pl.multiple_of(col * sz.quarter, sz.quarter), sz.quarter), :] for j in range(nb)],
            axis=0,
        )
        second = (dot_as(top, w3[...], 1, 1) * gathered(slopes2).astype(F32)).astype(BF16)
        spread_out(gps, second)
        first = (dot_as(second, w2[...], 1, 1) * gathered(slopes1).astype(F32)).astype(BF16)
        spread_out(gpf, first)
        spread_out(gx, dot_as(first, w1_own[...], 1, 1).astype(BF16))
        for copy in down_copies(col, i):
            copy.start()

    def quarter_down(i, _):
        flip = jnp.where(i == 0, c, jnp.where(i == 1, cx, jnp.where(i == 2, ck, ckx)))

        @pl.when(i == 1)
        def _():
            for k in range(nb):
                src = batch_from(k)
                send(gu_at(src, cx), gu_at(src, cx), gx_s.at[k], gx_r.at[k], (b, cx)).wait_recv()
            send(gu_all(cx), gu_all(cx), gc_s.at[1], gc_r.at[1], (b, ck)).start()

        @pl.when(i == 2)
        def _():
            send(gu_all(ck), gu_all(ck), gc_s.at[0], gc_r.at[0], (b, ck)).wait_recv()

        @pl.when(i == 3)
        def _():
            send(gu_all(ckx), gu_all(ckx), gc_s.at[1], gc_r.at[1], (b, ck)).wait_recv()

        down(i, flip)
        return 0

    lax.fori_loop(0, nc, quarter_down, 0)
    gu_copy = pltpu.make_async_copy(gu, gu_out, out_sem.at[4])
    gu_copy.start()

    pick_own = one_where(iota((width, embed), 1) == c * width + iota((width, embed), 0), BF16)
    for i in range(1, nc):
        src = col_from(i)
        send(gp_all.at[src], gp_all.at[src], gp_s.at[i - 1], gp_r.at[i - 1], (b, c)).wait_recv()
    for quarter in range(nc):
        own_part = dot_as(pick_own, users_of(quarter), 1, 1)
        grad = gp_all[quarter, 0:1, :].astype(BF16).astype(F32)
        mine = slots[sz.cap_tiles + quarter, 0:1, :] >= 0.0
        pos_rows_out[:, quarter * sz.users : (quarter + 1) * sz.users] = jnp.where(
            mine, grad * own_part, 0.0
        ).astype(BF16)

    for i in range(1, nc):
        src = col_from(i)
        send(loss_all.at[src], loss_all.at[src], lo_s.at[i - 1], lo_r.at[i - 1], (b, c)).wait_recv()
        send(rg_recv.at[src], rg_recv.at[src], rg_s.at[i - 1], rg_r.at[i - 1], (b, c)).wait_recv()
    loss = loss_all[0]
    neg_total = rg_recv[0].astype(F32)
    for i in range(1, nc):
        loss = loss + loss_all[i]
        neg_total = neg_total + rg_recv[i].astype(F32)
    neg_rows_out[...] = neg_total.astype(BF16)
    loss_out[...] = loss[0:1, 0:1]

    last_sends.append(send(gu_all(cx), gu_all(cx), gc_s.at[1], gc_r.at[1], (b, ck)))
    for i in range(1, nc):
        last_sends.append(pos_send(i))
    for copy in last_sends:
        copy.wait_send()

    def drain(t, _):
        for i in range(1, nb):
            send(sums.at[t, pl.ds(0, piece)], pieces.at[t, 0], rs_s.at[t, i - 1], rs_r.at[t], (b, c)).wait_send()
            send(x_piece(t, b), x_piece(t, b), ag_s.at[t, i - 1], ag_r.at[t], (b, c)).wait_send()
        send(x_at(t, c), x_at(t, c), xx_s.at[t], xx_r.at[t], (b, cx)).wait_send()
        send(x_at(t, c), x_at(t, c), co_s.at[t, 0], co_r.at[t, 0], (b, ck)).wait_send()
        send(x_at(t, cx), x_at(t, cx), co_s.at[t, 1], co_r.at[t, 1], (b, ck)).wait_send()
        return 0

    lax.fori_loop(0, sz.steps, drain, 0)
    for table in range(2):
        for t in (sz.steps - 2, sz.steps - 1):
            count_copy(t, table, t % 2).wait()
    gu_copy.wait()
    for copy in out_copies:
        copy.wait()
    for i, col in enumerate((c, cx, ck, ckx)):
        for copy in down_copies(col, i):
            copy.wait()


def front(sz, args):
    nb, nc, total = sz.batch, sz.col, sz.total
    width, embed, cap, users = sz.width, sz.embed, sz.cap, sz.users
    slots = cap + users
    first, second = args["w_second"].shape
    buckets = args["demo_table"].shape[0]
    x_width = sz.x_width
    vmem = pl.BlockSpec(memory_space=pltpu.VMEM)
    smem = pl.BlockSpec(memory_space=pltpu.SMEM)
    hbm = pl.BlockSpec(memory_space=pl.ANY)
    dma = pltpu.SemaphoreType.DMA

    def shape(dims, kind=BF16):
        return jax.ShapeDtypeStruct(dims, kind)

    outs = [
        (shape((2, sz.high_parts, 4, total, LOW)), hbm), (shape((total, x_width)), hbm),
        (shape((total, first)), hbm), (shape((total, second)), hbm), (shape((nb, sz.rows, embed)), hbm),
        (shape((nb, sz.rows, second)), hbm), (shape((nb, sz.rows, first)), hbm),
        (shape((nb, sz.rows, 256)), hbm), (shape((buckets, total)), hbm),
        (shape((width, cap)), vmem), (shape((width, total)), vmem),
        (shape((sz.tiles, 8, CHUNK), F32), vmem),
        (shape((sz.quarter, embed)), vmem), (shape((1, 1), F32), vmem), (shape((1, 1), I32), vmem),
    ]
    scratch = [
        pltpu.VMEM((3, width, sz.vocab), BF16),
        pltpu.VMEM((sz.high * width, LOW), BF16),
        pltpu.VMEM((2, sz.high_parts * LOW, 4 * width), BF16),
        pltpu.VMEM(args["w_first"].shape, BF16),
        pltpu.VMEM((x_width, first), BF16),
        pltpu.VMEM((256, first), BF16),
        pltpu.VMEM((first, second), BF16),
        pltpu.VMEM((second, embed), BF16),
        pltpu.VMEM((BAG_PAD, 128), I32),
        pltpu.VMEM((sz.rows, BAG_PAD), I32),
        pltpu.VMEM((sz.groups, CHUNK), I32),
        pltpu.VMEM((nb, sz.groups, CHUNK), I32),
        pltpu.VMEM((nb, 8, 128), I32),
        pltpu.VMEM((sz.neg_lines, CHUNK), F32),
        pltpu.VMEM((4, sz.neg_lines, CHUNK), F32),
        pltpu.VMEM((2, 2, sz.high_parts, 4, sz.span, LOW), BF16),
        pltpu.VMEM((2, sz.span, 128), F32),
        pltpu.VMEM((sz.steps, sz.span, 128), BF16),
        pltpu.VMEM((sz.steps, nb - 1, sz.span // nb, 128), BF16),
        pltpu.VMEM((total, x_width), BF16),
        pltpu.VMEM((total, first), F32),
        pltpu.VMEM((total, second), F32),
        pltpu.VMEM((total, first), BF16),
        pltpu.VMEM((total, first), BF16),
        pltpu.VMEM((total, second), BF16),
        pltpu.VMEM((total, second), BF16),
        pltpu.VMEM((total, embed), BF16),
        pltpu.VMEM((buckets, total), BF16),
        pltpu.VMEM((sz.tiles, 8, CHUNK), F32),
        pltpu.VMEM((sz.tiles, width, CHUNK), BF16),
        pltpu.VMEM((nc, sz.cap_tiles, width, CHUNK), BF16),
        pltpu.VMEM((nc, width, users), BF16),
        pltpu.VMEM((embed, slots), BF16),
        pltpu.VMEM((slots, embed), BF16),
        pltpu.VMEM((slots, users), BF16),
        pltpu.VMEM((nb, 8, users), F32),
        pltpu.VMEM((nb, sz.quarter, embed), BF16),
        pltpu.VMEM((nb - 1, sz.quarter, embed), BF16),
        pltpu.VMEM((nb, sz.rows, embed), BF16),
        pltpu.VMEM((nb, sz.rows, second), BF16),
        pltpu.VMEM((nb, sz.rows, first), BF16),
        pltpu.VMEM((nb, sz.rows, 256), BF16),
        pltpu.VMEM((nc, width, cap), BF16),
        pltpu.VMEM((nc, width, cap), BF16),
        pltpu.VMEM((nc, 8, users), F32),
        pltpu.VMEM((nc, 8, 128), F32),
        dma((6,)), dma((5,)), dma((nc, 3)), dma((2, 2)),
        dma((nb - 1,)), dma((nb - 1,)), dma((nb - 1,)), dma((nb - 1,)), dma((nc - 1,)), dma((nc - 1,)),
        dma((sz.steps, nb - 1)), dma((sz.steps,)), dma((sz.steps, nb - 1)), dma((sz.steps,)),
        dma((sz.steps,)), dma((sz.steps,)), dma((sz.steps, 2)), dma((sz.steps, 2)),
        dma((nc - 1,)), dma((nc - 1,)), dma((nc - 1,)), dma((nc - 1,)),
        dma((nb - 1,)), dma((nb - 1,)), dma((nb - 1,)), dma((nb - 1,)),
        dma((nb - 1,)), dma((nb - 1,)), dma((nb,)), dma((nb,)), dma((2,)), dma((2,)),
        dma((nc - 1,)), dma((nc - 1,)), dma((nc - 1,)), dma((nc - 1,)), dma((nc - 1,)), dma((nc - 1,)),
    ]
    operands = [
        (args["watch_ids"].T, vmem), (args["search_ids"].T, vmem), (args["demo_ids"].T, vmem),
        (args["pos_ids"].reshape(1, -1), vmem), (args["neg_ids"].reshape(-1, 128), vmem),
        (args["demo_table"].T, vmem), (args["b_first"].reshape(1, -1), vmem),
        (args["b_second"].reshape(1, -1), vmem), (args["b_third"].reshape(1, -1), vmem),
        (args["valid_counts"], smem),
        (args["watch_table"], hbm), (args["search_table"], hbm), (args["out_table"], hbm),
        (args["w_first"], hbm), (args["w_second"], hbm), (args["w_third"], hbm),
    ]
    return pl.pallas_call(
        functools.partial(front_kernel, sz),
        out_shape=[o for o, _ in outs],
        in_specs=[s for _, s in operands],
        out_specs=[s for _, s in outs],
        scratch_shapes=scratch,
        compiler_params=pltpu.CompilerParams(
            collective_id=0, has_side_effects=True, vmem_limit_bytes=63 * 2**20
        ),
        name="front",
    )(*[o for o, _ in operands])


def back_kernel(
    sz, neg_rows, pos_rows, slots, counts, x_in, act1_in, act2_in, gu_in, gps_in, gpf_in, gx_in, buckets_in,
    watch_out, search_out, table_out, gw1_out, gw2_out, gw3_out, demo_out, gb1_out, gb2_out, gb3_out,
    x, act1, act2, gu, gps, gpf, gx, buckets, grads, ring,
    lines, low_rows, gw1, gw2, gw3, in_sem, ring_sem, line_sem, out_sem,
):
    width, cap, total, nb = sz.width, sz.cap, sz.total, sz.batch
    parts, nc, embed = sz.high_parts, sz.col, sz.embed
    depth = ring.shape[0]
    names = [
        (gx_in, gx), (act2_in, act2), (gu_in, gu), (act1_in, act1), (gps_in, gps), (x_in, x), (gpf_in, gpf),
        (buckets_in, buckets),
    ]
    loads = [pltpu.make_async_copy(s, d, in_sem.at[i]) for i, (s, d) in enumerate(names)]
    loads[0].start()

    def ring_load(n):
        return pltpu.make_async_copy(
            counts.at[lax.rem(n, 2), n // 2], ring.at[lax.rem(n, depth)], ring_sem.at[lax.rem(n, depth)]
        )

    for n in range(depth):
        ring_load(n).start()
    for load in loads[1:]:
        load.start()
    loads[0].wait()

    grads[...] = gx[...].reshape(total, gx.shape[2])[:, 0:128].T

    def line_store(out, slot, hh):
        at = pl.ds(pl.multiple_of(hh * 4 * LOW, 4 * LOW), 4 * LOW)
        return pltpu.make_async_copy(lines.at[slot], out.at[:, at], line_sem.at[slot])

    def put(slot, found, factor):
        for i in range(4):
            lines[slot, :, i * LOW : (i + 1) * LOW] = found[i] * factor

    for k in range(sz.tiles):
        low = slots[k, 1:2, :].astype(BF16)
        hot = one_where(low == iota((LOW, CHUNK), 0).astype(BF16), BF16)
        low_rows[k * CHUNK : (k + 1) * CHUNK, :] = hot.T
    high = jnp.concatenate([slots[k, 0:1, :] for k in range(sz.tiles)], axis=1).astype(BF16)
    values = jnp.concatenate([neg_rows[...], pos_rows[...]], axis=1)

    def scatter(n, _):
        left = []
        for i in range(8):
            at = (n * 8 + i).astype(F32).astype(BF16)
            left.append(jnp.where(high == at, values, jnp.zeros((), BF16)))
        found = dot_as(jnp.concatenate(left, axis=0), low_rows[...], 1, 0)
        for j in range(2):

            @pl.when(n >= 1)
            def _():
                line_store(table_out, 4 + j, (n - 1) * 2 + j).wait()

            put(4 + j, [found[(j * 4 + i) * width : (j * 4 + i + 1) * width] for i in range(4)], 1.0)
            line_store(table_out, 4 + j, n * 2 + j).start()
        return 0

    lax.fori_loop(0, parts // 2, scatter, 0)
    def bags(hh, _):
        for table, out in enumerate((watch_out, search_out)):
            n = hh * 2 + table
            slot = table * 2 + lax.rem(hh, 2)
            ring_load(n).wait()
            own = grads[table * width : (table + 1) * width, :]
            found = [dot_as(own, ring[lax.rem(n, depth), i], 1, 0) for i in range(4)]

            @pl.when(n + depth < 2 * parts)
            def _():
                ring_load(n + depth).start()

            @pl.when(hh >= 2)
            def _():
                line_store(out, slot, hh - 2).wait()

            put(slot, found, 1.0 / sz.bag)
            line_store(out, slot, hh).start()
        return 0

    lax.fori_loop(0, parts, bags, 0)

    for load in loads[1:]:
        load.wait()
    gu_rows = gu[...].reshape(total, embed)
    second = gps[...].reshape(total, gps.shape[2])
    first = gpf[...].reshape(total, gpf.shape[2])
    demo_grad = gx[...].reshape(total, 256)[:, 128:]
    gw3[...] = dot_as(act2[...], gu_rows, 0, 0)
    gw2[...] = dot_as(act1[...], second, 0, 0)
    gw1[...] = dot_as(x[...], first, 0, 0)
    stores = [(gw3, gw3_out), (gw2, gw2_out)]
    for i in range(nc):
        stores.append((gw1.at[pl.ds(i * 128, width)], gw1_out.at[pl.ds(i * width, width)]))
        stores.append((gw1.at[pl.ds(i * 128 + width, width)], gw1_out.at[pl.ds(embed + i * width, width)]))
    stores.append((gw1.at[pl.ds(nc * 128, sz.demo_width)], gw1_out.at[pl.ds(2 * embed, sz.demo_width)]))
    stores = [pltpu.make_async_copy(s, d, out_sem.at[i]) for i, (s, d) in enumerate(stores)]
    for store in stores:
        store.start()
    demo = dot_as(buckets[...], demo_grad, 1, 0)
    demo_out[...] = demo.T[0 : sz.demo_width, :]
    gb1_out[...] = jnp.sum(first.astype(F32), axis=0, keepdims=True)
    gb2_out[...] = jnp.sum(second.astype(F32), axis=0, keepdims=True)
    gb3_out[...] = jnp.sum(gu_rows.astype(F32), axis=0, keepdims=True)

    for table, out in enumerate((watch_out, search_out)):
        for hh in (parts - 2, parts - 1):
            line_store(out, table * 2 + hh % 2, hh).wait()
    for j in range(2):
        line_store(table_out, 4 + j, parts - 2 + j).wait()
    for store in stores:
        store.wait()


def back(sz, args, kept):
    vmem = pl.BlockSpec(memory_space=pltpu.VMEM)
    hbm = pl.BlockSpec(memory_space=pl.ANY)
    total, nb = sz.total, sz.batch
    first, second = args["w_second"].shape
    embed, buckets = sz.embed, args["demo_table"].shape[0]
    dma = pltpu.SemaphoreType.DMA

    def shape(dims, kind=F32):
        return jax.ShapeDtypeStruct(dims, kind)

    table = shape((sz.width, sz.vocab))
    outs = [(table, hbm)] * 3 + [
        (shape((args["w_first"].shape)), hbm), (shape((first, second)), hbm), (shape((second, embed)), hbm),
        (shape((sz.demo_width, buckets)), vmem), (shape((1, first)), vmem), (shape((1, second)), vmem),
        (shape((1, embed)), vmem),
    ]
    slots = sz.tiles * CHUNK
    return pl.pallas_call(
        functools.partial(back_kernel, sz),
        out_shape=[o for o, _ in outs],
        in_specs=[vmem] * 3 + [hbm] * 9,
        out_specs=[s for _, s in outs],
        scratch_shapes=[
            pltpu.VMEM((total, sz.x_width), BF16), pltpu.VMEM((total, first), BF16),
            pltpu.VMEM((total, second), BF16), pltpu.VMEM((nb, sz.rows, embed), BF16),
            pltpu.VMEM((nb, sz.rows, second), BF16), pltpu.VMEM((nb, sz.rows, first), BF16),
            pltpu.VMEM((nb, sz.rows, 256), BF16), pltpu.VMEM((buckets, total), BF16),
            pltpu.VMEM((128, total), BF16), pltpu.VMEM((8, 4, total, LOW), BF16),
            pltpu.VMEM((6, sz.width, 4 * LOW), F32), pltpu.VMEM((slots, LOW), BF16),
            pltpu.VMEM((sz.x_width, first), F32), pltpu.VMEM((first, second), F32),
            pltpu.VMEM((second, embed), F32),
            dma((8,)), dma((8,)), dma((6,)), dma((3 + 2 * sz.col,)),
        ],
        compiler_params=pltpu.CompilerParams(vmem_limit_bytes=62 * 2**20),
        name="back",
    )(*kept)


def fast_device(sz, *inputs):
    names = (
        "watch_ids", "search_ids", "demo_ids", "pos_ids", "neg_ids", "valid_counts", "watch_table",
        "search_table", "demo_table", "out_table", "w_first", "b_first", "w_second", "b_second",
        "w_third", "b_third",
    )
    args = dict(zip(names, inputs))
    (
        counts, x, act1, act2, gu, gps, gpf, gx, buckets, neg_rows, pos_rows, slots, user_vecs, loss, fits,
    ) = front(sz, args)

    def finish(*operands):
        kept = (neg_rows, pos_rows, slots, counts, x, act1, act2, gu, gps, gpf, gx, buckets)
        watch, search, table, gw1, gw2, gw3, demo, gb1, gb2, gb3 = back(sz, args, kept)
        return (
            user_vecs, loss.reshape(()), watch, search, table, demo.T, gw1, gb1.reshape(-1),
            gw2, gb2.reshape(-1), gw3, gb3.reshape(-1),
        )

    def general(*operands):
        return per_device(RingCollectives(), *operands)

    return lax.cond(fits.reshape(()) > 0, finish, general, *inputs)


def fast_sizes(mesh, shapes):
    watch, demo, negs, table, first = shapes
    batch, col = mesh.shape["batch"], mesh.shape["col"]
    rows, width, vocab = watch[0] // batch, table[0] // col, table[1] // batch
    demo_width = first[0] - 2 * table[0]
    sz = Sizes(batch, col, rows, watch[1], width, vocab, negs[0], table[0], demo_width)
    good = (
        batch == 8 and col == 4 and rows == 128 and watch[1] <= BAG_PAD and width == 64
        and vocab == 32 * LOW and table[1] <= 65536 and demo[1] <= 4 and demo_width <= 128
        and negs[0] % 128 == 0 and negs[0] <= 256 * CHUNK
    )
    return sz if good else None


def solution(mesh):
    in_specs = (
        P("batch", None),
        P("batch", None),
        P("batch", None),
        P("batch"),
        P(),
        P("batch"),
        P("col", "batch"),
        P("col", "batch"),
        P(),
        P("col", "batch"),
        P(),
        P(),
        P(),
        P(),
        P(),
        P(),
    )
    out_specs = (
        P(("batch", "col"), None),
        P(),
        P("col", "batch"),
        P("col", "batch"),
        P("col", "batch"),
        P(),
        P(),
        P(),
        P(),
        P(),
        P(),
        P(),
    )
    def whole(*inputs):
        shapes = [inputs[i].shape for i in (0, 2, 4, 6, 10)]
        sz = fast_sizes(mesh, shapes)
        if sz is None:
            body = functools.partial(per_device, Collectives())
        else:
            body = functools.partial(fast_device, sz)
        return jax.shard_map(
            body, mesh=mesh, in_specs=in_specs, out_specs=out_specs, check_vma=False
        )(*inputs)

    return whole
```

```python
import functools
import math

import jax
import jax.numpy as jnp
from jax import lax
from jax.experimental import pallas as pl
from jax.experimental.pallas import tpu as pltpu
from jax.sharding import PartitionSpec as P


def contract_rows(left, right):
    return lax.dot_general(
        left, right, (((0,), (0,)), ((), ())), preferred_element_type=jnp.float32
    )


def contract_cols(left, right):
    return lax.dot_general(
        left, right, (((1,), (1,)), ((), ())), preferred_element_type=jnp.float32
    )


def gelu_back(pre_value, grad_value):
    return jax.vjp(jax.nn.gelu, pre_value)[1](grad_value)[0]


class Collectives:
    def gather(self, value, name, axis):
        return lax.all_gather(value, name, axis=axis, tiled=True)

    def scatter_sum(self, value, name, axis):
        return lax.psum_scatter(value, name, scatter_dimension=axis, tiled=True)

    def total(self, values, name):
        return lax.psum(values, name)


class RingCollectives:
    def shift(self, value, name):
        size = lax.axis_size(name)
        return lax.ppermute(value, name, [(i, (i + 1) % size) for i in range(size)])

    def stack(self, value, name):
        size, me = lax.axis_size(name), lax.axis_index(name)
        held = [value]
        for _ in range(size - 1):
            held.append(self.shift(held[-1], name))
        return jnp.take(jnp.stack(held), (me - jnp.arange(size)) % size, axis=0)

    def gather(self, value, name, axis):
        parts = self.stack(value, name)
        return jnp.concatenate([parts[i] for i in range(parts.shape[0])], axis=axis)

    def ring_sum(self, parts, name):
        size, me = lax.axis_size(name), lax.axis_index(name)
        held = jnp.take(parts, (me - 1) % size, axis=0)
        for step in range(1, size):
            held = self.shift(held, name) + jnp.take(parts, (me - 1 - step) % size, axis=0)
        return held

    def scatter_sum(self, value, name, axis):
        size = lax.axis_size(name)
        return self.ring_sum(jnp.stack(jnp.split(value, size, axis=axis)), name)

    def total(self, values, name):
        size = lax.axis_size(name)
        flat = jnp.concatenate([v.reshape(-1) for v in values])
        length = -(-flat.shape[0] // (size * 128)) * 128
        parts = jnp.pad(flat, (0, size * length - flat.shape[0])).reshape(size, length)
        whole = self.stack(self.ring_sum(parts, name), name).reshape(-1)
        out, at = [], 0
        for v in values:
            out.append(whole[at : at + v.size].reshape(v.shape))
            at += v.size
        return tuple(out)


def per_device(
    comm,
    watch_ids,
    search_ids,
    demo_ids,
    pos_ids,
    neg_ids,
    valid_counts,
    watch_table,
    search_table,
    demo_table,
    out_table,
    w_first,
    b_first,
    w_second,
    b_second,
    w_third,
    b_third,
):
    row_count = watch_ids.shape[0]
    bag_size = watch_ids.shape[1]
    col_width = watch_table.shape[0]
    vocab_rows = watch_table.shape[1]
    embed_width = col_width * lax.axis_size("col")
    offset = lax.axis_index("batch") * vocab_rows
    col_slot = lax.axis_index("col")
    quarter = row_count // lax.axis_size("col")
    low_width = math.gcd(vocab_rows, 128)
    high_width = vocab_rows // low_width

    def owned(id_values):
        local_ids = id_values - offset
        return jnp.where((local_ids >= 0) & (local_ids < vocab_rows), local_ids, vocab_rows)

    def bag_counts(id_block):
        local_ids = owned(id_block)
        high_hot = (
            local_ids[:, :, None] // low_width == jnp.arange(high_width)[None, None, :]
        ).astype(jnp.bfloat16)
        low_hot = (
            local_ids[:, :, None] % low_width == jnp.arange(low_width)[None, None, :]
        ).astype(jnp.bfloat16)
        counted = jnp.einsum("rbh,rbl->rhl", high_hot, low_hot, preferred_element_type=jnp.bfloat16)
        return counted.reshape(id_block.shape[0], vocab_rows)

    def single_hot(id_block):
        return (owned(id_block)[:, None] == jnp.arange(vocab_rows)[None, :]).astype(jnp.bfloat16)

    zero_col = jnp.zeros((col_width, 1), jnp.bfloat16)
    padded_out = jnp.concatenate([out_table, zero_col], axis=1)
    all_watch, all_search, all_pos = (
        comm.gather(watch_ids, "batch", 0),
        comm.gather(search_ids, "batch", 0),
        comm.gather(pos_ids, "batch", 0),
    )
    total_rows = all_watch.shape[0]
    block_rows = min(1024, total_rows)
    block_count = total_rows // block_rows
    neg_local = owned(neg_ids)
    neg_part = jnp.take(padded_out, neg_local, axis=1).astype(jnp.float32)

    def flatten_blocks(stacked):
        return stacked.transpose(1, 0, 2).reshape(col_width, total_rows)

    def bag_block(inputs_block):
        watch_block, search_block, pos_block = inputs_block
        watch_part = contract_cols(watch_table, bag_counts(watch_block))
        search_part = contract_cols(search_table, bag_counts(search_block))
        pos_part = contract_cols(out_table, single_hot(pos_block))
        return (watch_part, search_part, pos_part)

    id_blocks = (
        all_watch.reshape(block_count, block_rows, bag_size),
        all_search.reshape(block_count, block_rows, bag_size),
        all_pos.reshape(block_count, block_rows),
    )
    watch_parts, search_parts, pos_parts = lax.map(bag_block, id_blocks)
    watch_sum, search_sum, pos_rows = (
        comm.scatter_sum(flatten_blocks(watch_parts), "batch", 1),
        comm.scatter_sum(flatten_blocks(search_parts), "batch", 1),
        comm.scatter_sum(flatten_blocks(pos_parts), "batch", 1),
    )
    neg_rows, valid_total = comm.total(
        (neg_part, jnp.sum(valid_counts).astype(jnp.float32)), "batch"
    )
    pooled_watch = (watch_sum / bag_size).astype(jnp.bfloat16)
    pooled_search = (search_sum / bag_size).astype(jnp.bfloat16)
    pos_bf = pos_rows.astype(jnp.bfloat16)
    neg_bf = neg_rows.astype(jnp.bfloat16)
    count_here = valid_counts[0]
    full_watch, full_search, full_pos, full_neg = (
        comm.gather(pooled_watch, "col", 0),
        comm.gather(pooled_search, "col", 0),
        comm.gather(pos_bf, "col", 0),
        comm.gather(neg_bf, "col", 0),
    )
    watch_rows = full_watch.T
    search_rows = full_search.T
    pos_full = full_pos.T
    live_rows = jnp.arange(row_count) < count_here
    weight = jnp.where(live_rows, 1.0 / valid_total, 0.0)
    buckets = demo_table.shape[0]
    bucket_counts = jnp.sum(
        (demo_ids[:, :, None] == jnp.arange(buckets)[None, None, :]).astype(jnp.float32), axis=1
    ).astype(jnp.bfloat16)
    demo_vec = jnp.dot(bucket_counts, demo_table, preferred_element_type=jnp.float32)
    joined = jnp.concatenate([watch_rows, search_rows, demo_vec.astype(jnp.bfloat16)], axis=1)
    pre_first = jnp.dot(joined, w_first, preferred_element_type=jnp.float32) + b_first
    act_first = jax.nn.gelu(pre_first).astype(jnp.bfloat16)
    pre_second = jnp.dot(act_first, w_second, preferred_element_type=jnp.float32) + b_second
    act_second = jax.nn.gelu(pre_second).astype(jnp.bfloat16)
    user_block = (
        jnp.dot(act_second, w_third, preferred_element_type=jnp.float32) + b_third
    ).astype(jnp.bfloat16)
    neg_logits = jnp.dot(user_block, full_neg, preferred_element_type=jnp.float32)
    pos_logit = jnp.sum(user_block.astype(jnp.float32) * pos_full.astype(jnp.float32), axis=1)
    row_peak = jnp.maximum(jnp.max(neg_logits, axis=1), pos_logit)
    exp_neg = jnp.exp(neg_logits - row_peak[:, None])
    exp_pos = jnp.exp(pos_logit - row_peak)
    row_total = jnp.sum(exp_neg, axis=1) + exp_pos
    lse = row_peak + jnp.log(row_total)
    loss_here = jnp.sum(weight * (lse - pos_logit))
    grad_neg = (weight[:, None] * exp_neg / row_total[:, None]).astype(jnp.bfloat16)
    grad_pos = (weight * (exp_pos / row_total - 1.0)).astype(jnp.bfloat16)
    grad_user = (
        contract_cols(grad_neg, full_neg)
        + grad_pos.astype(jnp.float32)[:, None] * pos_full.astype(jnp.float32)
    ).astype(jnp.bfloat16)
    neg_row_grad = contract_rows(user_block, grad_neg)
    pos_row_grad = (grad_pos.astype(jnp.float32)[:, None] * user_block.astype(jnp.float32)).astype(
        jnp.bfloat16
    )
    grad_w_third = contract_rows(act_second, grad_user)
    grad_b_third = jnp.sum(grad_user.astype(jnp.float32), axis=0)
    grad_pre_second = gelu_back(pre_second, contract_cols(grad_user, w_third)).astype(jnp.bfloat16)
    grad_w_second = contract_rows(act_first, grad_pre_second)
    grad_b_second = jnp.sum(grad_pre_second.astype(jnp.float32), axis=0)
    grad_pre_first = gelu_back(pre_first, contract_cols(grad_pre_second, w_second)).astype(
        jnp.bfloat16
    )
    grad_w_first = contract_rows(joined, grad_pre_first)
    grad_b_first = jnp.sum(grad_pre_first.astype(jnp.float32), axis=0)
    grad_joined = contract_cols(grad_pre_first, w_first).astype(jnp.bfloat16)
    grad_pw = grad_joined[:, :embed_width]
    grad_ps = grad_joined[:, embed_width : 2 * embed_width]
    grad_demo = contract_rows(bucket_counts, grad_joined[:, 2 * embed_width :])
    col_start = col_slot * col_width
    own_pw = lax.dynamic_slice_in_dim(grad_pw, col_start, col_width, 1).T
    own_ps = lax.dynamic_slice_in_dim(grad_ps, col_start, col_width, 1).T
    own_pos = lax.dynamic_slice_in_dim(pos_row_grad, col_start, col_width, 1).T
    user_vecs = lax.dynamic_slice_in_dim(user_block, col_slot * quarter, quarter, 0)
    all_pw, all_ps, all_dpos = (
        comm.gather(own_pw, "batch", 1),
        comm.gather(own_ps, "batch", 1),
        comm.gather(own_pos, "batch", 1),
    )
    neg_own = lax.dynamic_slice_in_dim(neg_row_grad, col_slot * col_width, col_width, 0)
    sums_out = comm.total(
        (
            grad_w_first,
            grad_b_first,
            grad_w_second,
            grad_b_second,
            grad_w_third,
            grad_b_third,
            grad_demo,
            neg_own,
            loss_here,
        ),
        "batch",
    )
    neg_sum_own = sums_out[7]

    def split_blocks(columns):
        return columns.reshape(col_width, block_count, block_rows).transpose(1, 0, 2)

    def grad_block(running, inputs_block):
        watch_block, search_block, pos_block, block_pw, block_ps, block_pos = inputs_block
        new_watch = running[0] + jnp.dot(
            block_pw, bag_counts(watch_block), preferred_element_type=jnp.float32
        )
        new_search = running[1] + jnp.dot(
            block_ps, bag_counts(search_block), preferred_element_type=jnp.float32
        )
        new_out = running[2] + jnp.dot(
            block_pos, single_hot(pos_block), preferred_element_type=jnp.float32
        )
        return ((new_watch, new_search, new_out), None)

    zeros_table = jnp.zeros((col_width, vocab_rows), jnp.float32)
    (table_watch, table_search, table_out), _ = lax.scan(
        grad_block,
        (zeros_table, zeros_table, zeros_table),
        id_blocks + (split_blocks(all_pw), split_blocks(all_ps), split_blocks(all_dpos)),
    )
    neg_added = (
        jnp.zeros((col_width, vocab_rows + 1), jnp.float32).at[:, neg_local].add(neg_sum_own)
    )
    table_out = table_out + neg_added[:, :vocab_rows]
    return (
        user_vecs,
        sums_out[8],
        table_watch / bag_size,
        table_search / bag_size,
        table_out,
        sums_out[6],
        sums_out[0],
        sums_out[1],
        sums_out[2],
        sums_out[3],
        sums_out[4],
        sums_out[5],
    )


F32, BF16, FP8, I32 = jnp.float32, jnp.bfloat16, jnp.float8_e4m3fn, jnp.int32
MESH = pl.DeviceIdType.MESH
LOW = 256
ROWS_IN_GROUP = 4
BAG_PAD = 64
CHUNK = 256
NEG_FLOOR = -1e30


def dot_as(left, right, left_dim, right_dim):
    return lax.dot_general(
        left, right, (((left_dim,), (right_dim,)), ((), ())), preferred_element_type=F32
    )


def iota(shape, dim):
    return lax.broadcasted_iota(I32, shape, dim)


def one_where(mask, kind):
    return jnp.where(mask, jnp.ones((), BF16), jnp.zeros((), BF16)).astype(kind)


def slot_cap(neg_count, batch):
    mean = neg_count / batch
    return int(math.ceil((mean + 4.5 * math.sqrt(mean)) / CHUNK)) * CHUNK


def gelu(pre):
    bent = jnp.tanh(math.sqrt(2.0 / math.pi) * (pre + 0.044715 * (pre * pre * pre)))
    return 0.5 * pre * (1.0 + bent)


def gelu_slope(pre):
    inner_scale = math.sqrt(2.0 / math.pi)
    square = pre * pre
    bent = jnp.tanh(inner_scale * (pre + 0.044715 * (square * pre)))
    return 0.5 * (1.0 + bent) + 0.5 * pre * (1.0 - bent * bent) * (
        inner_scale * (1.0 + 3.0 * 0.044715 * square)
    )


def flip_rows(value):
    rows, lanes = value.shape
    return pltpu.roll(value.reshape(rows // 8, 8, lanes), 4, 1).reshape(rows, lanes)


def x_place(col):
    return ((col % 2) * 2 + col // 2) * 128


def scattered(n, high, values, low_rows):
    left = []
    for i in range(8):
        at = (n * 8 + i).astype(F32).astype(BF16)
        left.append(jnp.where(high == at, values, jnp.zeros((), BF16)))
    return dot_as(jnp.concatenate(left, axis=0), low_rows, 1, 0)


class Sizes:
    def __init__(self, batch, col, rows, bag, width, vocab, negs, embed, demo_width):
        self.batch, self.col, self.rows, self.bag = batch, col, rows, bag
        self.width, self.vocab, self.negs, self.embed = width, vocab, negs, embed
        self.demo_width = demo_width
        self.total = batch * rows
        self.quarter = rows // col
        self.users = batch * self.quarter
        self.groups = rows // ROWS_IN_GROUP
        self.high = vocab // LOW
        self.high_parts = self.high // 4
        self.cap = slot_cap(negs, batch)
        self.cap_tiles = self.cap // CHUNK
        self.tiles = self.cap_tiles + col
        self.neg_lines = -(-negs // (CHUNK * 8)) * 8
        self.steps = 4
        self.span = self.total // self.steps
        self.x_width = col * 128 + 128


def front_kernel(
    sz,
    watch_ids, search_ids, demo_ids, pos_ids, neg_ids, demo_table, b_first, b_second, b_third, valid_count,
    watch_table, search_table, out_table, w_first, w_second, w_third,
    counts_out, x_out, act1_out, act2_out, gu_out, gps_out, gpf_out, gx_out, buckets_out,
    neg_rows_out, pos_table_out, slots_out, user_out, loss_out, fits_out,
    tabs, tall, mix, w1_raw, w1, w1_own, w2, w3, turned, upright, lines_own, ids, side, neg_dest, neg_digits, counts, found_sums, sums, pieces, x,
    pre1, pre2, acts1, slopes1, acts2, slopes2, users, buckets, slots, picked, neg_all, pos_all, e_cols,
    e_rows, low_rows, pos_table, probs, stats, factors, home, g_send, g_recv, gu, gps, gpf, gx, rg_send, rg_recv, gp_all, loss_all,
    local_sem, out_sem, down_sem, count_sem, ids_s, ids_r, sd_s, sd_r, ic_s, ic_r, rs_s, rs_r, ag_s, ag_r, xx_s, xx_r, co_s, co_r,
    ne_s, ne_r, pe_s, pe_r, ho_s, ho_r, st_s, st_r, gs_s, gs_r, ga_s, ga_r, gx_s, gx_r, gc_s, gc_r,
    rg_s, rg_r, gp_s, gp_r, lo_s, lo_r,
):
    b, c = lax.axis_index("batch"), lax.axis_index("col")
    nb, nc = sz.batch, sz.col
    offset = b * sz.vocab
    cap, width, embed = sz.cap, sz.width, sz.embed
    cx = lax.rem(c + 2, nc)
    ck = c + 1 - 2 * lax.rem(c, 2)
    ckx = lax.rem(ck + 2, nc)

    def batch_peer(i):
        return lax.rem(b + i, nb)

    def batch_from(i):
        return lax.rem(b + nb - i, nb)

    def col_peer(i):
        return lax.rem(c + i, nc)

    def col_from(i):
        return lax.rem(c + nc - i, nc)

    def send(src, dst, ssem, rsem, to):
        return pltpu.make_async_remote_copy(
            src_ref=src, dst_ref=dst, send_sem=ssem, recv_sem=rsem,
            device_id=to, device_id_type=MESH,
        )

    barrier = pltpu.get_barrier_semaphore()
    for i in range(1, nb):
        pl.semaphore_signal(barrier, inc=1, device_id=(batch_peer(i), c), device_id_type=MESH)
    for i in range(1, nc):
        pl.semaphore_signal(barrier, inc=1, device_id=(b, col_peer(i)), device_id_type=MESH)

    loads = [
        (watch_table, tabs.at[0]), (search_table, tabs.at[1]), (out_table, tabs.at[2]),
        (w_first, w1_raw), (w_second, w2), (w_third, w3),
    ]
    loads = [pltpu.make_async_copy(s, d, local_sem.at[i]) for i, (s, d) in enumerate(loads)]
    for load in loads:
        load.start()

    turned[...] = jnp.zeros((BAG_PAD, 128), I32)
    turned[0 : sz.bag, :] = (watch_ids[...] & 0xFFFF) | (search_ids[...] << 16)
    upright[...] = turned[...].T
    for r4 in range(ROWS_IN_GROUP):
        lines_own[:, r4 * BAG_PAD : (r4 + 1) * BAG_PAD] = upright[
            pl.ds(r4, sz.groups, stride=ROWS_IN_GROUP), :
        ]
    share = sz.groups // nc

    def share_of(col):
        return pl.ds(pl.multiple_of(col * share, share), share)

    ids[b, share_of(c), :] = lines_own[share_of(c), :]
    side[b] = jnp.zeros((8, 128), I32)
    side[b, 0:1, :] = pos_ids[...]
    side[b, 1:2, :] = jnp.full((1, 128), valid_count[0], I32)
    side[b, 2 : 2 + demo_ids.shape[0], :] = demo_ids[...]

    pl.semaphore_wait(barrier, nb - 1 + nc - 1)
    last_sends = []
    for i in range(1, nb):
        place = ids.at[b, share_of(c)]
        copy = send(place, place, ids_s.at[i - 1], ids_r.at[i - 1], (batch_peer(i), c))
        copy.start()
        last_sends.append(copy)

    for i in range(1, nb):
        copy = send(side.at[b], side.at[b], sd_s.at[i - 1], sd_r.at[i - 1], (batch_peer(i), c))
        copy.start()
        last_sends.append(copy)

    negs = neg_ids[...]
    lines = sz.neg_lines
    missing = 2 * lines - negs.shape[0]
    second = jnp.concatenate([negs[lines:], jnp.full((missing, 128), -1, I32)], axis=0)
    negs = jnp.concatenate([negs[:lines], second], axis=1)
    neg_local = negs - offset
    own = (neg_local >= 0) & (neg_local < sz.vocab)
    own_bf = one_where(own, BF16)
    upper = one_where(iota((CHUNK, CHUNK), 0) < iota((CHUNK, CHUNK), 1), BF16)
    before = dot_as(own_bf, upper, 1, 0)
    in_row = dot_as(own_bf, jnp.ones((CHUNK, CHUNK), BF16), 1, 0)
    lower = one_where(iota((lines, lines), 1) < iota((lines, lines), 0), BF16)
    rows_before = dot_as(lower, in_row.astype(BF16), 1, 0)
    neg_dest[...] = jnp.where(own, before + rows_before, -1.0)
    owned_count = dot_as(jnp.ones((8, lines), BF16), in_row.astype(BF16), 1, 0)
    most = jnp.zeros((1, 1), F32)
    for shard in range(nb):
        part = negs - shard * sz.vocab
        hits = jnp.where((part >= 0) & (part < sz.vocab), 1.0, 0.0)
        most = jnp.maximum(most, jnp.sum(jnp.sum(hits, axis=1, keepdims=True), axis=0, keepdims=True))
    fits_out[...] = jnp.where(most <= float(cap), 1, 0)
    for digit in range(4):
        neg_digits[digit] = ((neg_local >> (4 * digit)) & 15).astype(F32)

    def compact(k, total):
        place = neg_dest[pl.ds(k, 1), :]
        hot = one_where(place == iota((cap, CHUNK), 0).astype(F32), FP8)
        line = iota((32, CHUNK), 0)
        value = jnp.where(line == 4, 1.0, 0.0)
        for digit in range(4):
            value = jnp.where(line == digit, neg_digits[digit, pl.ds(k, 1), :], value)
        return total + dot_as(value.astype(FP8), hot, 1, 1)

    slot = lax.fori_loop(0, lines, compact, jnp.zeros((32, cap), F32))
    neg_low = slot[0:1] + 16.0 * slot[1:2]
    neg_high = jnp.where(slot[4:5] > 0.5, slot[2:3] + 16.0 * slot[3:4], -1.0)
    slots[...] = jnp.zeros((sz.tiles, 8, CHUNK), F32)
    for k in range(sz.cap_tiles):
        slots[k, 0:1, :] = neg_high[:, k * CHUNK : (k + 1) * CHUNK]
        slots[k, 1:2, :] = neg_low[:, k * CHUNK : (k + 1) * CHUNK]

    for i in range(1, nb):
        place = ids.at[batch_from(i), share_of(c)]
        send(place, place, ids_s.at[i - 1], ids_r.at[i - 1], (b, c)).wait_recv()
    for i in range(1, nc):
        place = ids.at[:, share_of(c)]
        copy = send(place, place, ic_s.at[i - 1], ic_r.at[i - 1], (b, col_peer(i)))
        copy.start()
        last_sends.append(copy)
    for t in range(2):
        loads[t].wait()

    def turn(n, _):
        t, hh = n // sz.high_parts, n % sz.high_parts
        base = pl.multiple_of(hh * 4 * LOW, 4 * LOW)
        stack = jnp.concatenate([tabs[t, :, pl.ds(base + i * LOW, LOW)] for i in range(4)], axis=0)
        mix[t, pl.ds(pl.multiple_of(hh * LOW, LOW), LOW), :] = stack.T
        return 0

    lax.fori_loop(0, 2 * sz.high_parts, turn, 0)

    loads[2].wait()

    def stack_up(hh, _):
        for i in range(4):
            tall[pl.ds(pl.multiple_of((hh * 4 + i) * width, width), width), :] = tabs[
                2, :, pl.ds(pl.multiple_of((hh * 4 + i) * LOW, LOW), LOW)
            ]
        return 0

    lax.fori_loop(0, sz.high_parts, stack_up, 0)

    def pick_tile(k, _):
        high, low = slots[k, 0:1, :], slots[k, 1:2, :]
        low_hot = one_where(low.astype(BF16) == iota((LOW, CHUNK), 0).astype(BF16), BF16)
        total = jnp.zeros((width, CHUNK), F32)
        for part in range(4):
            tall_rows = width * sz.high // 4
            got = dot_as(tall[part * tall_rows : (part + 1) * tall_rows, :], low_hot, 1, 0)
            for i in range(sz.high // 4):
                at = float(part * (sz.high // 4) + i)
                total = total + jnp.where(high == at, got[i * width : (i + 1) * width], 0.0)
        picked[k] = total.astype(BF16)
        return 0

    lax.fori_loop(0, sz.cap_tiles, pick_tile, 0)
    neg_part = picked.at[pl.ds(0, sz.cap_tiles)]
    for i in range(1, nc):
        copy = send(neg_part, neg_all.at[c], ne_s.at[i - 1], ne_r.at[i - 1], (b, col_peer(i)))
        copy.start()
        last_sends.append(copy)
    for k in range(sz.cap_tiles):
        neg_all[c, k] = picked[k]

    loads[3].wait()
    w1[nc * 128 :, :] = jnp.zeros((128, w1.shape[1]), BF16)
    for i in range(nc):
        at = x_place(i)
        w1[at : at + width, :] = w1_raw[i * width : (i + 1) * width, :]
        w1[at + width : at + 128, :] = w1_raw[embed + i * width : embed + (i + 1) * width, :]
    w1[nc * 128 : nc * 128 + sz.demo_width, :] = w1_raw[2 * embed :, :]
    loads[4].wait()
    loads[5].wait()

    w1_own[...] = jnp.zeros(w1_own.shape, BF16)
    w1_own[0 : 2 * width, :] = w1[pl.ds(pl.multiple_of((lax.rem(c, 2) * 2 + c // 2) * 128, 128), 128), :]
    w1_own[2 * width : 2 * width + sz.demo_width, :] = w1_raw[2 * embed :, :]
    for i in range(1, nc):
        place = ids.at[:, share_of(col_from(i))]
        send(place, place, ic_s.at[i - 1], ic_r.at[i - 1], (b, c)).wait_recv()

    users_shape = (nb, CHUNK)
    at_block = iota(users_shape, 1) // sz.quarter == iota(users_shape, 0)

    def demo_part():
        for i in range(1, nb):
            place = side.at[batch_from(i)]
            send(place, place, sd_s.at[i - 1], sd_r.at[i - 1], (b, c)).wait_recv()
        bucket_total = jnp.zeros((buckets.shape[0], sz.total), BF16)
        bucket_line = iota((buckets.shape[0], sz.total), 0).astype(BF16)
        for field in range(demo_ids.shape[0]):
            line = jnp.concatenate([side[j, 2 + field : 3 + field, :] for j in range(nb)], axis=1)
            bucket_total = bucket_total + one_where(line.astype(F32).astype(BF16) == bucket_line, BF16)
        buckets[...] = bucket_total
        demo_rows = demo_table[...].astype(F32).T.astype(BF16)
        x[:, nc * 128 :] = jnp.zeros((sz.total, 128), BF16)
        x[:, nc * 128 : nc * 128 + sz.demo_width] = dot_as(bucket_total, demo_rows, 0, 0).astype(BF16)

    def pos_part():
        all_pos = jnp.concatenate([side[j, 0:1, :] for j in range(nb)], axis=0)
        pos_local = all_pos - offset
        pos_owned = (pos_local >= 0) & (pos_local < sz.vocab)
        pos_pair = jnp.concatenate(
            [
                jnp.where(pos_owned, pos_local >> 8, 255).astype(F32),
                (pos_local & 255).astype(F32),
            ],
            axis=0,
        ).astype(BF16)
        for quarter in range(nc):
            shape = (128, CHUNK)
            pick = one_where(iota(shape, 0) == quarter * sz.quarter + iota(shape, 1) % sz.quarter, BF16)
            wide = dot_as(pos_pair, pick, 1, 0)
            high = jnp.sum(jnp.where(at_block, wide[0:nb], 0.0), axis=0, keepdims=True)
            low = jnp.sum(jnp.where(at_block, wide[nb : 2 * nb], 0.0), axis=0, keepdims=True)
            slots[sz.cap_tiles + quarter, 0:1, :] = jnp.where(high > 254.0, -1.0, high)
            slots[sz.cap_tiles + quarter, 1:2, :] = low
        slots_out[...] = slots[...]
        lax.fori_loop(sz.cap_tiles, sz.tiles, pick_tile, 0)
        pos_all[c] = picked[sz.cap_tiles + c]
        for i in range(1, nc):
            pos_send(i).start()

    def slot_rows():
        for i in range(1, nc):
            src = col_from(i)
            send(neg_all.at[src], neg_all.at[src], ne_s.at[i - 1], ne_r.at[i - 1], (b, c)).wait_recv()
            send(pos_all.at[src], pos_all.at[src], pe_s.at[i - 1], pe_r.at[i - 1], (b, c)).wait_recv()
        for i in range(nc):
            for k in range(sz.cap_tiles):
                e_cols[i * width : (i + 1) * width, k * CHUNK : (k + 1) * CHUNK] = neg_all[i, k]
            e_cols[i * width : (i + 1) * width, cap:] = pos_all[i]
        e_rows[...] = e_cols[...].T
        for i in range(1, nb):
            home_send(i).start()

    def home_send(i):
        to = batch_peer(i)
        rows = e_rows.at[pl.ds(pl.multiple_of(cap + to * sz.quarter, sz.quarter), sz.quarter)]
        return send(rows, home.at[i - 1], ho_s.at[i - 1], ho_r.at[i - 1], (to, c))

    def pos_send(i):
        to = col_peer(i)
        return send(picked.at[sz.cap_tiles + to], pos_all.at[c], pe_s.at[i - 1], pe_r.at[i - 1], (b, to))

    span = sz.span
    piece = span // nb
    lane_mod = iota((16, CHUNK), 1) % BAG_PAD
    lane_r4 = iota((16, CHUNK), 1) // BAG_PAD
    odd_group = iota((16, CHUNK), 0) & 1
    blocks = span // sz.rows
    parts_in_block = sz.groups // 16

    def count_copy(t, table, slot_at):
        rows = pl.ds(pl.multiple_of(t * span, span), span)
        return pltpu.make_async_copy(
            counts.at[table, slot_at], counts_out.at[table, :, :, rows], count_sem.at[table, slot_at]
        )

    def bag_table(t, table):
        slot_at = lax.rem(t, 2)

        @pl.when(t >= 2)
        def _():
            count_copy(t - 2, table, slot_at).wait()

        code_line = iota((4 * sz.high, CHUNK), 0).astype(BF16)
        low_line = iota((LOW, CHUNK), 0).astype(BF16)

        def groups_of(q, _):
            block = t * blocks + q // parts_in_block
            word = ids[block, pl.ds(pl.multiple_of((q % parts_in_block) * 16, 16), 16), :]
            value = lax.shift_right_logical(word, 16 * table) & 0xFFFF
            local = value - offset
            mine = (local >= 0) & (local < sz.vocab) & (lane_mod < sz.bag)
            code = jnp.where(mine, ((local >> 8) ^ odd_group) * 4 + lane_r4, -1).astype(F32).astype(BF16)
            low = (local & 255).astype(F32).astype(BF16)
            low_half = iota((sz.high // 2, 8, LOW), 1) < 4
            for quad in range(4):
                pairs = []
                for pair in range(2):
                    found = []
                    for g in (quad * 4 + pair * 2, quad * 4 + pair * 2 + 1):
                        left = one_where(code[g : g + 1, :] == code_line, FP8)
                        right = one_where(low[g : g + 1, :] == low_line, FP8)
                        found.append(dot_as(left, right, 1, 1).reshape(sz.high // 2, 8, LOW))
                    even = jnp.where(low_half, found[0], found[1])
                    odd = jnp.where(low_half, found[1], found[0])
                    pairs.append((even, odd))
                line = pl.ds(pl.multiple_of(q * 64 + quad * 16, 16), 16)
                for part in range(sz.high):
                    both = [pairs[k][part % 2][part // 2] for k in range(2)]
                    counts[table, slot_at, part // 4, part % 4, line, :] = jnp.concatenate(
                        both, axis=0
                    ).astype(BF16)
            return 0

        lax.fori_loop(0, blocks * parts_in_block, groups_of, 0)
        count_copy(t, table, slot_at).start()
        left = jnp.concatenate(
            [counts[table, slot_at, hh].reshape(4 * span, LOW) for hh in range(sz.high_parts)], axis=1
        )
        total = dot_as(left, mix[table], 1, 0)
        left_side = iota((span, 128), 1) < width
        first = jnp.where(left_side, total[0:span, 0:128], flip_rows(total[span : 2 * span, 0:128]))
        second = jnp.where(left_side, total[2 * span : 3 * span, 128:], flip_rows(total[3 * span :, 128:]))
        both = first + second
        found_sums[table] = both + pltpu.roll(both, width, 1)

    def bag_sums(t):
        joined = jnp.where(iota((span, 128), 1) < width, found_sums[0], found_sums[1])
        sums[t] = joined.astype(BF16)
        for i in range(1, nb):
            to = batch_peer(i)
            send(
                sums.at[t, pl.ds(pl.multiple_of(to * piece, piece), piece)], pieces.at[t, i - 1],
                rs_s.at[t, i - 1], rs_r.at[t], (to, c),
            ).start()

    def lanes_of(col):
        return pl.ds(pl.multiple_of((lax.rem(col, 2) * 2 + col // 2) * 128, 128), 128)

    def x_at(t, col):
        return x.at[pl.ds(pl.multiple_of(t * span, span), span), lanes_of(col)]

    def x_pair(t, col):
        return x.at[
            pl.ds(pl.multiple_of(t * span, span), span),
            pl.ds(pl.multiple_of(lax.rem(col, 2) * 256, 256), 256),
        ]

    def x_piece(t, owner):
        return x.at[
            pl.ds(pl.multiple_of(t * span + owner * piece, piece), piece), lanes_of(c)
        ]

    def reduce_step(t):
        send(pieces.at[t], pieces.at[t], rs_s.at[t, 0], rs_r.at[t], (b, c)).wait_recv()
        total = sums[t, pl.ds(pl.multiple_of(b * piece, piece), piece), :].astype(F32)
        for i in range(nb - 1):
            total = total + pieces[t, i].astype(F32)
        x[
            pl.ds(pl.multiple_of(t * span + b * piece, piece), piece), lanes_of(c)
        ] = (total / sz.bag).astype(BF16)
        for i in range(1, nb):
            send(x_piece(t, b), x_piece(t, b), ag_s.at[t, i - 1], ag_r.at[t], (batch_peer(i), c)).start()

    def cross_step(t):
        send(pieces.at[t], pieces.at[t], ag_s.at[t, 0], ag_r.at[t], (b, c)).wait_recv()
        send(x_at(t, c), x_at(t, c), xx_s.at[t], xx_r.at[t], (b, cx)).start()

    def core_step(t):
        send(x_at(t, cx), x_at(t, cx), xx_s.at[t], xx_r.at[t], (b, cx)).wait_recv()
        send(x_pair(t, c), x_pair(t, c), co_s.at[t], co_r.at[t], (b, ck)).start()

    def full_step(t):
        send(x_pair(t, ck), x_pair(t, ck), co_s.at[t], co_r.at[t], (b, ck)).wait_recv()

    def tower(k):
        at = pl.ds(pl.multiple_of(k * span, span), span)
        pre = dot_as(x[at, :], w1[...], 1, 0) + b_first[...]
        pre1[at, :] = pre
        value = gelu(pre).astype(BF16)
        acts1[at, :] = value
        pre = dot_as(value, w2[...], 1, 0) + b_second[...]
        pre2[at, :] = pre
        value = gelu(pre).astype(BF16)
        acts2[at, :] = value
        users[at, :] = (dot_as(value, w3[...], 1, 0) + b_third[...]).astype(BF16)

    def slopes(k):
        at = pl.ds(pl.multiple_of(k * span, span), span)
        slopes1[at, :] = gelu_slope(pre1[at, :]).astype(BF16)
        slopes2[at, :] = gelu_slope(pre2[at, :]).astype(BF16)

    bag_ticks = 2 * sz.steps
    last = sz.steps - 1

    def tick(n, _):
        half = n // 2
        odd = lax.rem(n, 2) == 1

        @pl.when(n < bag_ticks)
        def _():
            bag_table(half, lax.rem(n, 2))

        @pl.when((n < bag_ticks) & odd)
        def _():
            bag_sums(half)

        @pl.when(n == bag_ticks)
        def _():
            demo_part()

        @pl.when(n == bag_ticks + 1)
        def _():
            pos_part()

        @pl.when(n == bag_ticks + 3)
        def _():
            slot_rows()

        @pl.when(odd & (n >= 5))
        def _():
            full_step((n - 5) // 2)

        done = jnp.where(n <= bag_ticks, 0, jnp.where(n <= bag_ticks + 2, 1, last))
        ready = jnp.where(
            n < bag_ticks, 0, jnp.where(n <= bag_ticks + 1, 1, jnp.where(n == bag_ticks + 2, last, sz.steps))
        )

        def some_tower(k, _):
            tower(k)
            return 0

        lax.fori_loop(done, ready, some_tower, 0)

        @pl.when((~odd) & (n >= 2) & (n <= bag_ticks))
        def _():
            reduce_step(half - 1)

        @pl.when(odd & (n >= 3) & (n <= bag_ticks + 1))
        def _():
            cross_step((n - 3) // 2)

        @pl.when((~odd) & (n >= 4) & (n <= bag_ticks + 2))
        def _():
            core_step(half - 2)

        return 0

    lax.fori_loop(0, bag_ticks + 4, tick, 0)

    valid = jnp.concatenate([side[j, 1:2, :] for j in range(nb)], axis=0)
    valid_wide = jnp.concatenate([valid] * (sz.users // 128), axis=1).astype(F32)
    live_count = jnp.sum(jnp.where(at_block, valid_wide, 0.0), axis=0, keepdims=True)
    valid_total = jnp.sum(valid_wide, axis=0, keepdims=True)
    user_place = c * sz.quarter + iota((1, sz.users), 1) % sz.quarter
    weight = jnp.where(user_place.astype(F32) < live_count, 1.0 / valid_total, 0.0)

    out_copies = [(x, x_out), (acts1, act1_out), (acts2, act2_out), (buckets, buckets_out)]
    out_copies = [pltpu.make_async_copy(s, d, out_sem.at[i]) for i, (s, d) in enumerate(out_copies)]
    for copy in out_copies:
        copy.start()
    user_out[...] = users[pl.ds(pl.multiple_of(b * sz.rows + c * sz.quarter, sz.quarter), sz.quarter), :]

    def users_of(quarter):
        return jnp.concatenate(
            [
                users[pl.ds(pl.multiple_of(j * sz.rows + quarter * sz.quarter, sz.quarter), sz.quarter), :]
                for j in range(nb)
            ],
            axis=0,
        )

    quarter_users = users_of(c)
    logits = dot_as(e_rows[...], quarter_users, 1, 1)
    neg_logits, pos_logits = logits[0:cap], logits[cap:]
    slot_ok = iota((cap, sz.users), 0).astype(F32) < owned_count[0:1, : sz.users]
    pos_here = slots[sz.cap_tiles + c, 0:1, :]
    pos_ok = (iota((sz.users, sz.users), 0) == iota((sz.users, sz.users), 1)) & (pos_here >= 0.0)
    neg_logits = jnp.where(slot_ok, neg_logits, NEG_FLOOR)
    pos_masked = jnp.where(pos_ok, pos_logits, NEG_FLOOR)
    peak = jnp.maximum(
        jnp.max(neg_logits, axis=0, keepdims=True), jnp.max(pos_masked, axis=0, keepdims=True)
    )
    bare = jnp.where(slot_ok, jnp.exp(neg_logits - peak), 0.0)
    mass = jnp.sum(bare, axis=0, keepdims=True) + jnp.sum(
        jnp.where(pos_ok, jnp.exp(pos_masked - peak), 0.0), axis=0, keepdims=True
    )
    pos_value = jnp.sum(jnp.where(pos_ok, pos_logits, 0.0), axis=0, keepdims=True)
    stats[b] = jnp.concatenate([peak, mass, pos_value, jnp.zeros((5, sz.users), F32)], axis=0)
    for i in range(1, nb):
        copy = send(stats.at[b], stats.at[b], st_s.at[i - 1], st_r.at[i - 1], (batch_peer(i), c))
        copy.start()
        last_sends.append(copy)

    probs[...] = bare.astype(BF16)
    grad_user = dot_as(probs[...], e_rows[0:cap, :], 0, 0)
    for j in range(nb):
        g_send[j] = grad_user[j * sz.quarter : (j + 1) * sz.quarter].astype(BF16)
    for i in range(1, nb):
        to = batch_peer(i)
        copy = send(g_send.at[to], g_recv.at[i - 1], gs_s.at[i - 1], gs_r.at[i - 1], (to, c))
        copy.start()
        last_sends.append(copy)

    def some_slopes(k, _):
        slopes(k)
        return 0

    lax.fori_loop(0, sz.steps, some_slopes, 0)
    for i in range(1, nb):
        src = batch_from(i)
        send(stats.at[src], stats.at[src], st_s.at[i - 1], st_r.at[i - 1], (b, c)).wait_recv()
    order = [batch_from(i) for i in range(nb)]
    peaks = [stats[j, 0:1, :] for j in range(nb)]
    top = peaks[0]
    for j in range(1, nb):
        top = jnp.maximum(top, peaks[j])
    full_mass = jnp.zeros((1, sz.users), F32)
    pos_logit = jnp.zeros((1, sz.users), F32)
    for j in range(nb):
        full_mass = full_mass + stats[j, 1:2, :] * jnp.exp(peaks[j] - top)
        pos_logit = pos_logit + stats[j, 2:3, :]
    lse = top + jnp.log(full_mass)
    loss_part = jnp.sum(weight * (lse - pos_logit), axis=1, keepdims=True)
    scale = weight / full_mass
    pos_grad = weight * (jnp.exp(pos_logit - top) / full_mass - 1.0)
    lines_of = [jnp.exp(stats[j, 0:1, :] - top) * scale for j in order]
    lines_of += [pos_grad, jnp.zeros((16 - nb - 1, sz.users), F32)]
    factors[...] = jnp.concatenate(lines_of, axis=0).T
    probs[...] = jnp.where(slot_ok, jnp.exp(neg_logits - top) * scale, 0.0).astype(BF16)
    gp_all[c] = jnp.broadcast_to(jnp.where(pos_here >= 0.0, pos_grad, 0.0), (8, sz.users))
    loss_all[c] = jnp.broadcast_to(loss_part, (8, 128))
    for i in range(1, nc):
        to = col_peer(i)
        for copy in (
            send(gp_all.at[c], gp_all.at[c], gp_s.at[i - 1], gp_r.at[i - 1], (b, to)),
            send(loss_all.at[c], loss_all.at[c], lo_s.at[i - 1], lo_r.at[i - 1], (b, to)),
        ):
            copy.start()
            last_sends.append(copy)
    rows_grad = dot_as(probs[...], quarter_users, 1, 0)
    rows_grad = rows_grad.T.astype(BF16)
    for i in range(nc):
        rg_send[i] = rows_grad[i * width : (i + 1) * width]
    for i in range(1, nc):
        to = col_peer(i)
        copy = send(rg_send.at[to], rg_recv.at[c], rg_s.at[i - 1], rg_r.at[i - 1], (b, to))
        copy.start()
        last_sends.append(copy)
    rg_recv[c] = rg_send[c]
    for i in range(1, nb):
        send(g_send.at[0], g_recv.at[i - 1], gs_s.at[i - 1], gs_r.at[i - 1], (b, c)).wait_recv()
    factor = factors[pl.ds(pl.multiple_of(b * sz.quarter, sz.quarter), sz.quarter), :]
    total = factor[:, 0:1] * g_send[b].astype(F32)
    own_pos = e_rows[pl.ds(pl.multiple_of(cap + b * sz.quarter, sz.quarter), sz.quarter), :].astype(F32)
    for i in range(1, nb):
        home_send(i).wait_recv()
        total = total + factor[:, i : i + 1] * g_recv[i - 1].astype(F32)
        own_pos = own_pos + home[i - 1].astype(F32)
    total = total + factor[:, nb : nb + 1].astype(BF16).astype(F32) * own_pos

    def gu_at(block, col):
        return gu.at[block, pl.ds(pl.multiple_of(col * sz.quarter, sz.quarter), sz.quarter), :]

    def gu_all(col):
        return gu.at[:, pl.ds(pl.multiple_of(col * sz.quarter, sz.quarter), sz.quarter), :]

    gu[b, pl.ds(pl.multiple_of(c * sz.quarter, sz.quarter), sz.quarter), :] = total.astype(BF16)
    for i in range(1, nb):
        copy = send(gu_at(b, c), gu_at(b, c), ga_s.at[i - 1], ga_r.at[i - 1], (batch_peer(i), c))
        copy.start()
        last_sends.append(copy)

    for k in range(nc):
        low = slots[sz.cap_tiles + k, 1:2, :].astype(BF16)
        hot = one_where(low == iota((LOW, CHUNK), 0).astype(BF16), BF16)
        low_rows[k * CHUNK : (k + 1) * CHUNK, :] = hot.T
    pick_own = one_where(iota((width, embed), 1) == c * width + iota((width, embed), 0), BF16)
    for i in range(1, nc):
        src = col_from(i)
        send(gp_all.at[src], gp_all.at[src], gp_s.at[i - 1], gp_r.at[i - 1], (b, c)).wait_recv()
    pos_rows = []
    for quarter in range(nc):
        own_part = dot_as(pick_own, users_of(quarter), 1, 1)
        grad = gp_all[quarter, 0:1, :].astype(BF16).astype(F32)
        mine = slots[sz.cap_tiles + quarter, 0:1, :] >= 0.0
        pos_rows.append(jnp.where(mine, grad * own_part, 0.0).astype(BF16))
    pos_rows = jnp.concatenate(pos_rows, axis=1)
    pos_parts = jnp.concatenate(
        [slots[sz.cap_tiles + k, 0:1, :] for k in range(nc)], axis=1
    ).astype(BF16)

    def pos_scatter(n, _):
        found = scattered(n, pos_parts, pos_rows, low_rows[...])
        for j in range(2):
            for i in range(4):
                pos_table[n * 2 + j, :, i * LOW : (i + 1) * LOW] = found[
                    (j * 4 + i) * width : (j * 4 + i + 1) * width
                ]
        return 0

    lax.fori_loop(0, sz.high_parts // 2, pos_scatter, 0)
    pos_copy = pltpu.make_async_copy(pos_table, pos_table_out, out_sem.at[5])
    pos_copy.start()
    for i in range(nb):
        src = batch_from(i)
        if i > 0:
            send(gu_at(src, c), gu_at(src, c), ga_s.at[i - 1], ga_r.at[i - 1], (b, c)).wait_recv()
        copy = send(gu_at(src, c), gu_at(src, c), gx_s.at[i], gx_r.at[i], (b, cx))
        copy.start()
        last_sends.append(copy)
    copy = send(gu_all(c), gu_all(c), gc_s.at[0], gc_r.at[0], (b, ck))
    copy.start()
    last_sends.append(copy)

    def rows_at(ref, col):
        return ref.at[:, pl.ds(pl.multiple_of(col * sz.quarter, sz.quarter), sz.quarter), :]

    def down_copies(col, i):
        return [
            pltpu.make_async_copy(rows_at(kept, col), rows_at(out, col), down_sem.at[i, k])
            for k, (kept, out) in enumerate(((gps, gps_out), (gpf, gpf_out), (gx, gx_out)))
        ]

    def down(i, col):
        def spread_out(ref, value):
            for j in range(nb):
                ref[j, pl.ds(pl.multiple_of(col * sz.quarter, sz.quarter), sz.quarter), :] = value[
                    j * sz.quarter : (j + 1) * sz.quarter
                ]

        def gathered(ref):
            return jnp.concatenate(
                [
                    ref[pl.ds(pl.multiple_of(j * sz.rows + col * sz.quarter, sz.quarter), sz.quarter), :]
                    for j in range(nb)
                ],
                axis=0,
            )

        top = jnp.concatenate(
            [gu[j, pl.ds(pl.multiple_of(col * sz.quarter, sz.quarter), sz.quarter), :] for j in range(nb)],
            axis=0,
        )
        second = (dot_as(top, w3[...], 1, 1) * gathered(slopes2).astype(F32)).astype(BF16)
        spread_out(gps, second)
        first = (dot_as(second, w2[...], 1, 1) * gathered(slopes1).astype(F32)).astype(BF16)
        spread_out(gpf, first)
        spread_out(gx, dot_as(first, w1_own[...], 1, 1).astype(BF16))
        for copy in down_copies(col, i):
            copy.start()

    def quarter_down(i, _):
        flip = jnp.where(i == 0, c, jnp.where(i == 1, ck, jnp.where(i == 2, cx, ckx)))

        @pl.when(i == 1)
        def _():
            send(gu_all(ck), gu_all(ck), gc_s.at[0], gc_r.at[0], (b, ck)).wait_recv()

        @pl.when(i == 2)
        def _():
            for k in range(nb):
                src = batch_from(k)
                send(gu_at(src, cx), gu_at(src, cx), gx_s.at[k], gx_r.at[k], (b, cx)).wait_recv()
            send(gu_all(cx), gu_all(cx), gc_s.at[1], gc_r.at[1], (b, ck)).start()

        @pl.when(i == 3)
        def _():
            send(gu_all(ckx), gu_all(ckx), gc_s.at[1], gc_r.at[1], (b, ck)).wait_recv()

        down(i, flip)
        return 0

    lax.fori_loop(0, nc, quarter_down, 0)
    gu_copy = pltpu.make_async_copy(gu, gu_out, out_sem.at[4])
    gu_copy.start()

    for i in range(1, nc):
        src = col_from(i)
        send(loss_all.at[src], loss_all.at[src], lo_s.at[i - 1], lo_r.at[i - 1], (b, c)).wait_recv()
        send(rg_recv.at[src], rg_recv.at[src], rg_s.at[i - 1], rg_r.at[i - 1], (b, c)).wait_recv()
    loss = loss_all[0]
    neg_total = rg_recv[0].astype(F32)
    for i in range(1, nc):
        loss = loss + loss_all[i]
        neg_total = neg_total + rg_recv[i].astype(F32)
    neg_rows_out[...] = neg_total.astype(BF16)
    loss_out[...] = loss[0:1, 0:1]

    last_sends.append(send(gu_all(cx), gu_all(cx), gc_s.at[1], gc_r.at[1], (b, ck)))
    for i in range(1, nc):
        last_sends.append(pos_send(i))
    for i in range(1, nb):
        last_sends.append(home_send(i))
    for copy in last_sends:
        copy.wait_send()

    def drain(t, _):
        for i in range(1, nb):
            send(sums.at[t, pl.ds(0, piece)], pieces.at[t, 0], rs_s.at[t, i - 1], rs_r.at[t], (b, c)).wait_send()
            send(x_piece(t, b), x_piece(t, b), ag_s.at[t, i - 1], ag_r.at[t], (b, c)).wait_send()
        send(x_at(t, c), x_at(t, c), xx_s.at[t], xx_r.at[t], (b, cx)).wait_send()
        send(x_pair(t, c), x_pair(t, c), co_s.at[t], co_r.at[t], (b, ck)).wait_send()
        return 0

    lax.fori_loop(0, sz.steps, drain, 0)
    for table in range(2):
        for t in (sz.steps - 2, sz.steps - 1):
            count_copy(t, table, t % 2).wait()
    gu_copy.wait()
    pos_copy.wait()
    for copy in out_copies:
        copy.wait()
    for i, col in enumerate((c, ck, cx, ckx)):
        for copy in down_copies(col, i):
            copy.wait()


def front(sz, args):
    nb, nc, total = sz.batch, sz.col, sz.total
    width, embed, cap, users = sz.width, sz.embed, sz.cap, sz.users
    slots = cap + users
    first, second = args["w_second"].shape
    buckets = args["demo_table"].shape[0]
    x_width = sz.x_width
    vmem = pl.BlockSpec(memory_space=pltpu.VMEM)
    smem = pl.BlockSpec(memory_space=pltpu.SMEM)
    hbm = pl.BlockSpec(memory_space=pl.ANY)
    dma = pltpu.SemaphoreType.DMA

    def shape(dims, kind=BF16):
        return jax.ShapeDtypeStruct(dims, kind)

    outs = [
        (shape((2, sz.high_parts, 4, total, LOW)), hbm), (shape((total, x_width)), hbm),
        (shape((total, first)), hbm), (shape((total, second)), hbm), (shape((nb, sz.rows, embed)), hbm),
        (shape((nb, sz.rows, second)), hbm), (shape((nb, sz.rows, first)), hbm),
        (shape((nb, sz.rows, 256)), hbm), (shape((buckets, total)), hbm),
        (shape((width, cap)), vmem), (shape((sz.high_parts, width, 4 * LOW), F32), hbm),
        (shape((sz.tiles, 8, CHUNK), F32), vmem),
        (shape((sz.quarter, embed)), vmem), (shape((1, 1), F32), vmem), (shape((1, 1), I32), vmem),
    ]
    scratch = [
        pltpu.VMEM((3, width, sz.vocab), BF16),
        pltpu.VMEM((sz.high * width, LOW), BF16),
        pltpu.VMEM((2, sz.high_parts * LOW, 4 * width), BF16),
        pltpu.VMEM(args["w_first"].shape, BF16),
        pltpu.VMEM((x_width, first), BF16),
        pltpu.VMEM((256, first), BF16),
        pltpu.VMEM((first, second), BF16),
        pltpu.VMEM((second, embed), BF16),
        pltpu.VMEM((BAG_PAD, 128), I32),
        pltpu.VMEM((sz.rows, BAG_PAD), I32),
        pltpu.VMEM((sz.groups, CHUNK), I32),
        pltpu.VMEM((nb, sz.groups, CHUNK), I32),
        pltpu.VMEM((nb, 8, 128), I32),
        pltpu.VMEM((sz.neg_lines, CHUNK), F32),
        pltpu.VMEM((4, sz.neg_lines, CHUNK), F32),
        pltpu.VMEM((2, 2, sz.high_parts, 4, sz.span, LOW), BF16),
        pltpu.VMEM((2, sz.span, 128), F32),
        pltpu.VMEM((sz.steps, sz.span, 128), BF16),
        pltpu.VMEM((sz.steps, nb - 1, sz.span // nb, 128), BF16),
        pltpu.VMEM((total, x_width), BF16),
        pltpu.VMEM((total, first), F32),
        pltpu.VMEM((total, second), F32),
        pltpu.VMEM((total, first), BF16),
        pltpu.VMEM((total, first), BF16),
        pltpu.VMEM((total, second), BF16),
        pltpu.VMEM((total, second), BF16),
        pltpu.VMEM((total, embed), BF16),
        pltpu.VMEM((buckets, total), BF16),
        pltpu.VMEM((sz.tiles, 8, CHUNK), F32),
        pltpu.VMEM((sz.tiles, width, CHUNK), BF16),
        pltpu.VMEM((nc, sz.cap_tiles, width, CHUNK), BF16),
        pltpu.VMEM((nc, width, users), BF16),
        pltpu.VMEM((embed, slots), BF16),
        pltpu.VMEM((slots, embed), BF16),
        pltpu.VMEM((nc * CHUNK, LOW), BF16),
        pltpu.VMEM((sz.high_parts, width, 4 * LOW), F32),
        pltpu.VMEM((cap, users), BF16),
        pltpu.VMEM((nb, 8, users), F32),
        pltpu.VMEM((users, 16), F32),
        pltpu.VMEM((nb - 1, sz.quarter, embed), BF16),
        pltpu.VMEM((nb, sz.quarter, embed), BF16),
        pltpu.VMEM((nb - 1, sz.quarter, embed), BF16),
        pltpu.VMEM((nb, sz.rows, embed), BF16),
        pltpu.VMEM((nb, sz.rows, second), BF16),
        pltpu.VMEM((nb, sz.rows, first), BF16),
        pltpu.VMEM((nb, sz.rows, 256), BF16),
        pltpu.VMEM((nc, width, cap), BF16),
        pltpu.VMEM((nc, width, cap), BF16),
        pltpu.VMEM((nc, 8, users), F32),
        pltpu.VMEM((nc, 8, 128), F32),
        dma((6,)), dma((6,)), dma((nc, 3)), dma((2, 2)),
        dma((nb - 1,)), dma((nb - 1,)), dma((nb - 1,)), dma((nb - 1,)), dma((nc - 1,)), dma((nc - 1,)),
        dma((sz.steps, nb - 1)), dma((sz.steps,)), dma((sz.steps, nb - 1)), dma((sz.steps,)),
        dma((sz.steps,)), dma((sz.steps,)), dma((sz.steps,)), dma((sz.steps,)),
        dma((nc - 1,)), dma((nc - 1,)), dma((nc - 1,)), dma((nc - 1,)), dma((nb - 1,)), dma((nb - 1,)),
        dma((nb - 1,)), dma((nb - 1,)), dma((nb - 1,)), dma((nb - 1,)),
        dma((nb - 1,)), dma((nb - 1,)), dma((nb,)), dma((nb,)), dma((2,)), dma((2,)),
        dma((nc - 1,)), dma((nc - 1,)), dma((nc - 1,)), dma((nc - 1,)), dma((nc - 1,)), dma((nc - 1,)),
    ]
    operands = [
        (args["watch_ids"].T, vmem), (args["search_ids"].T, vmem), (args["demo_ids"].T, vmem),
        (args["pos_ids"].reshape(1, -1), vmem), (args["neg_ids"].reshape(-1, 128), vmem),
        (args["demo_table"].T, vmem), (args["b_first"].reshape(1, -1), vmem),
        (args["b_second"].reshape(1, -1), vmem), (args["b_third"].reshape(1, -1), vmem),
        (args["valid_counts"], smem),
        (args["watch_table"], hbm), (args["search_table"], hbm), (args["out_table"], hbm),
        (args["w_first"], hbm), (args["w_second"], hbm), (args["w_third"], hbm),
    ]
    return pl.pallas_call(
        functools.partial(front_kernel, sz),
        out_shape=[o for o, _ in outs],
        in_specs=[s for _, s in operands],
        out_specs=[s for _, s in outs],
        scratch_shapes=scratch,
        compiler_params=pltpu.CompilerParams(
            collective_id=0, has_side_effects=True, vmem_limit_bytes=63 * 2**20
        ),
        name="front",
    )(*[o for o, _ in operands])


def back_kernel(
    sz, neg_rows, slots, user_in, loss_in, pos_in, counts, x_in, act1_in, act2_in, gu_in, gps_in, gpf_in, gx_in, buckets_in,
    watch_out, search_out, table_out, gw1_out, gw2_out, gw3_out, demo_out, gb1_out, gb2_out, gb3_out, user_out, loss_out,
    pos_table, x, act1, act2, gu, gps, gpf, gx, buckets, grads, ring,
    lines, low_rows, gw1, gw2, gw3, in_sem, ring_sem, line_sem, out_sem,
):
    width, cap, total, nb = sz.width, sz.cap, sz.total, sz.batch
    parts, nc, embed = sz.high_parts, sz.col, sz.embed
    depth = ring.shape[0]
    names = [
        (gx_in, gx), (pos_in, pos_table), (act2_in, act2), (gu_in, gu), (act1_in, act1), (gps_in, gps), (x_in, x), (gpf_in, gpf),
        (buckets_in, buckets),
    ]
    loads = [pltpu.make_async_copy(s, d, in_sem.at[i]) for i, (s, d) in enumerate(names)]
    loads[0].start()
    loads[1].start()
    user_out[...] = user_in[...]
    loss_out[...] = loss_in[...]

    def ring_load(n):
        return pltpu.make_async_copy(
            counts.at[lax.rem(n, 2), n // 2], ring.at[lax.rem(n, depth)], ring_sem.at[lax.rem(n, depth)]
        )

    early = depth - 2
    for n in range(early):
        ring_load(n).start()
    for load in loads[2:]:
        load.start()
    for n in range(early, depth):
        ring_load(n).start()
    loads[0].wait()

    own_grads = gx[...].reshape(total, gx.shape[2])[:, 0:128]
    grads[0] = own_grads.T
    grads[1] = flip_rows(own_grads.astype(F32)).astype(BF16).T

    def line_store(out, slot, hh):
        at = pl.ds(pl.multiple_of(hh * 4 * LOW, 4 * LOW), 4 * LOW)
        return pltpu.make_async_copy(lines.at[slot], out.at[:, at], line_sem.at[slot])

    def put(slot, found, factor):
        for i in range(4):
            lines[slot, :, i * LOW : (i + 1) * LOW] = found[i] * factor

    for k in range(sz.cap_tiles):
        low = slots[k, 1:2, :].astype(BF16)
        hot = one_where(low == iota((LOW, CHUNK), 0).astype(BF16), BF16)
        low_rows[k * CHUNK : (k + 1) * CHUNK, :] = hot.T
    high = jnp.concatenate([slots[k, 0:1, :] for k in range(sz.cap_tiles)], axis=1).astype(BF16)
    loads[1].wait()

    def scatter(n, _):
        found = scattered(n, high, neg_rows[...], low_rows[...])
        for j in range(2):

            @pl.when(n >= 1)
            def _():
                line_store(table_out, 4 + j, (n - 1) * 2 + j).wait()

            rows = [found[(j * 4 + i) * width : (j * 4 + i + 1) * width] for i in range(4)]
            rows = [rows[i] + pos_table[n * 2 + j, :, i * LOW : (i + 1) * LOW] for i in range(4)]
            put(4 + j, rows, 1.0)
            line_store(table_out, 4 + j, n * 2 + j).start()
        return 0

    lax.fori_loop(0, parts // 2, scatter, 0)
    def bags(hh, _):
        for table, out in enumerate((watch_out, search_out)):
            n = hh * 2 + table
            slot = table * 2 + lax.rem(hh, 2)
            ring_load(n).wait()
            found = [
                dot_as(grads[i % 2, table * width : (table + 1) * width, :], ring[lax.rem(n, depth), i], 1, 0)
                for i in range(4)
            ]

            @pl.when(n + depth < 2 * parts)
            def _():
                ring_load(n + depth).start()

            @pl.when(hh >= 2)
            def _():
                line_store(out, slot, hh - 2).wait()

            put(slot, found, 1.0 / sz.bag)
            line_store(out, slot, hh).start()
        return 0

    lax.fori_loop(0, parts // 2, bags, 0)

    for load in loads[2:]:
        load.wait()
    gu_rows = gu[...].reshape(total, embed)
    second = gps[...].reshape(total, gps.shape[2])
    first = gpf[...].reshape(total, gpf.shape[2])
    demo_grad = gx[...].reshape(total, 256)[:, 128:]
    gw3[...] = dot_as(act2[...], gu_rows, 0, 0)
    gw2[...] = dot_as(act1[...], second, 0, 0)
    gw1[...] = dot_as(x[...], first, 0, 0)
    stores = [(gw3, gw3_out), (gw2, gw2_out)]
    for i in range(nc):
        at = x_place(i)
        stores.append((gw1.at[pl.ds(at, width)], gw1_out.at[pl.ds(i * width, width)]))
        stores.append((gw1.at[pl.ds(at + width, width)], gw1_out.at[pl.ds(embed + i * width, width)]))
    stores.append((gw1.at[pl.ds(nc * 128, sz.demo_width)], gw1_out.at[pl.ds(2 * embed, sz.demo_width)]))
    stores = [pltpu.make_async_copy(s, d, out_sem.at[i]) for i, (s, d) in enumerate(stores)]
    for store in stores:
        store.start()
    demo = dot_as(buckets[...], demo_grad, 1, 0)
    demo_out[...] = demo.T[0 : sz.demo_width, :]
    gb1_out[...] = jnp.sum(first.astype(F32), axis=0, keepdims=True)
    gb2_out[...] = jnp.sum(second.astype(F32), axis=0, keepdims=True)
    gb3_out[...] = jnp.sum(gu_rows.astype(F32), axis=0, keepdims=True)

    lax.fori_loop(parts // 2, parts, bags, 0)

    for table, out in enumerate((watch_out, search_out)):
        for hh in (parts - 2, parts - 1):
            line_store(out, table * 2 + hh % 2, hh).wait()
    for j in range(2):
        line_store(table_out, 4 + j, parts - 2 + j).wait()
    for store in stores:
        store.wait()


def back(sz, args, kept):
    vmem = pl.BlockSpec(memory_space=pltpu.VMEM)
    hbm = pl.BlockSpec(memory_space=pl.ANY)
    total, nb = sz.total, sz.batch
    first, second = args["w_second"].shape
    embed, buckets = sz.embed, args["demo_table"].shape[0]
    dma = pltpu.SemaphoreType.DMA

    def shape(dims, kind=F32):
        return jax.ShapeDtypeStruct(dims, kind)

    table = shape((sz.width, sz.vocab))
    outs = [(table, hbm)] * 3 + [
        (shape((args["w_first"].shape)), hbm), (shape((first, second)), hbm), (shape((second, embed)), hbm),
        (shape((sz.demo_width, buckets)), vmem), (shape((1, first)), vmem), (shape((1, second)), vmem),
        (shape((1, embed)), vmem), (shape((sz.quarter, embed), BF16), vmem), (shape((1, 1)), vmem),
    ]
    slots = sz.cap
    return pl.pallas_call(
        functools.partial(back_kernel, sz),
        out_shape=[o for o, _ in outs],
        in_specs=[vmem] * 4 + [hbm] * 10,
        out_specs=[s for _, s in outs],
        scratch_shapes=[
            pltpu.VMEM((sz.high_parts, sz.width, 4 * LOW), F32),
            pltpu.VMEM((total, sz.x_width), BF16), pltpu.VMEM((total, first), BF16),
            pltpu.VMEM((total, second), BF16), pltpu.VMEM((nb, sz.rows, embed), BF16),
            pltpu.VMEM((nb, sz.rows, second), BF16), pltpu.VMEM((nb, sz.rows, first), BF16),
            pltpu.VMEM((nb, sz.rows, 256), BF16), pltpu.VMEM((buckets, total), BF16),
            pltpu.VMEM((2, 128, total), BF16), pltpu.VMEM((8, 4, total, LOW), BF16),
            pltpu.VMEM((6, sz.width, 4 * LOW), F32), pltpu.VMEM((slots, LOW), BF16),
            pltpu.VMEM((sz.x_width, first), F32), pltpu.VMEM((first, second), F32),
            pltpu.VMEM((second, embed), F32),
            dma((9,)), dma((8,)), dma((6,)), dma((3 + 2 * sz.col,)),
        ],
        compiler_params=pltpu.CompilerParams(vmem_limit_bytes=62 * 2**20),
        name="back",
    )(*kept)


def fast_device(sz, *inputs):
    names = (
        "watch_ids", "search_ids", "demo_ids", "pos_ids", "neg_ids", "valid_counts", "watch_table",
        "search_table", "demo_table", "out_table", "w_first", "b_first", "w_second", "b_second",
        "w_third", "b_third",
    )
    args = dict(zip(names, inputs))
    (
        counts, x, act1, act2, gu, gps, gpf, gx, buckets, neg_rows, pos_table, slots, user_vecs, loss, fits,
    ) = front(sz, args)

    def finish(*operands):
        kept = (neg_rows, slots, user_vecs, loss, pos_table, counts, x, act1, act2, gu, gps, gpf, gx, buckets)
        watch, search, table, gw1, gw2, gw3, demo, gb1, gb2, gb3, user, mean = back(sz, args, kept)
        return (
            user, mean.reshape(()), watch, search, table, demo.T, gw1, gb1.reshape(-1),
            gw2, gb2.reshape(-1), gw3, gb3.reshape(-1),
        )

    def general(*operands):
        return per_device(RingCollectives(), *operands)

    return lax.cond(fits.reshape(()) > 0, finish, general, *inputs)


def fast_sizes(mesh, shapes):
    watch, demo, negs, table, first = shapes
    batch, col = mesh.shape["batch"], mesh.shape["col"]
    rows, width, vocab = watch[0] // batch, table[0] // col, table[1] // batch
    demo_width = first[0] - 2 * table[0]
    sz = Sizes(batch, col, rows, watch[1], width, vocab, negs[0], table[0], demo_width)
    good = (
        batch == 8 and col == 4 and rows == 128 and watch[1] <= BAG_PAD and width == 64
        and vocab == 32 * LOW and table[1] <= 65536 and demo[1] <= 4 and demo_width <= 128
        and negs[0] % 128 == 0 and negs[0] <= 256 * CHUNK
    )
    return sz if good else None


def solution(mesh):
    in_specs = (
        P("batch", None),
        P("batch", None),
        P("batch", None),
        P("batch"),
        P(),
        P("batch"),
        P("col", "batch"),
        P("col", "batch"),
        P(),
        P("col", "batch"),
        P(),
        P(),
        P(),
        P(),
        P(),
        P(),
    )
    out_specs = (
        P(("batch", "col"), None),
        P(),
        P("col", "batch"),
        P("col", "batch"),
        P("col", "batch"),
        P(),
        P(),
        P(),
        P(),
        P(),
        P(),
        P(),
    )
    def whole(*inputs):
        shapes = [inputs[i].shape for i in (0, 2, 4, 6, 10)]
        sz = fast_sizes(mesh, shapes)
        if sz is None:
            body = functools.partial(per_device, Collectives())
        else:
            body = functools.partial(fast_device, sz)
        return jax.shard_map(
            body, mesh=mesh, in_specs=in_specs, out_specs=out_specs, check_vma=False
        )(*inputs)

    return whole
```

```python
import functools
import math

import jax
import jax.numpy as jnp
from jax import lax
from jax.experimental import pallas as pl
from jax.experimental.pallas import tpu as pltpu
from jax.sharding import PartitionSpec as P


def contract_rows(left, right):
    return lax.dot_general(
        left, right, (((0,), (0,)), ((), ())), preferred_element_type=jnp.float32
    )


def contract_cols(left, right):
    return lax.dot_general(
        left, right, (((1,), (1,)), ((), ())), preferred_element_type=jnp.float32
    )


def gelu_back(pre_value, grad_value):
    return jax.vjp(jax.nn.gelu, pre_value)[1](grad_value)[0]


class Collectives:
    def gather(self, value, name, axis):
        return lax.all_gather(value, name, axis=axis, tiled=True)

    def scatter_sum(self, value, name, axis):
        return lax.psum_scatter(value, name, scatter_dimension=axis, tiled=True)

    def total(self, values, name):
        return lax.psum(values, name)


class RingCollectives:
    def shift(self, value, name):
        size = lax.axis_size(name)
        return lax.ppermute(value, name, [(i, (i + 1) % size) for i in range(size)])

    def stack(self, value, name):
        size, me = lax.axis_size(name), lax.axis_index(name)
        held = [value]
        for _ in range(size - 1):
            held.append(self.shift(held[-1], name))
        return jnp.take(jnp.stack(held), (me - jnp.arange(size)) % size, axis=0)

    def gather(self, value, name, axis):
        parts = self.stack(value, name)
        return jnp.concatenate([parts[i] for i in range(parts.shape[0])], axis=axis)

    def ring_sum(self, parts, name):
        size, me = lax.axis_size(name), lax.axis_index(name)
        held = jnp.take(parts, (me - 1) % size, axis=0)
        for step in range(1, size):
            held = self.shift(held, name) + jnp.take(parts, (me - 1 - step) % size, axis=0)
        return held

    def scatter_sum(self, value, name, axis):
        size = lax.axis_size(name)
        return self.ring_sum(jnp.stack(jnp.split(value, size, axis=axis)), name)

    def total(self, values, name):
        size = lax.axis_size(name)
        flat = jnp.concatenate([v.reshape(-1) for v in values])
        length = -(-flat.shape[0] // (size * 128)) * 128
        parts = jnp.pad(flat, (0, size * length - flat.shape[0])).reshape(size, length)
        whole = self.stack(self.ring_sum(parts, name), name).reshape(-1)
        out, at = [], 0
        for v in values:
            out.append(whole[at : at + v.size].reshape(v.shape))
            at += v.size
        return tuple(out)


def per_device(
    comm,
    watch_ids,
    search_ids,
    demo_ids,
    pos_ids,
    neg_ids,
    valid_counts,
    watch_table,
    search_table,
    demo_table,
    out_table,
    w_first,
    b_first,
    w_second,
    b_second,
    w_third,
    b_third,
):
    row_count = watch_ids.shape[0]
    bag_size = watch_ids.shape[1]
    col_width = watch_table.shape[0]
    vocab_rows = watch_table.shape[1]
    embed_width = col_width * lax.axis_size("col")
    offset = lax.axis_index("batch") * vocab_rows
    col_slot = lax.axis_index("col")
    quarter = row_count // lax.axis_size("col")
    low_width = math.gcd(vocab_rows, 128)
    high_width = vocab_rows // low_width

    def owned(id_values):
        local_ids = id_values - offset
        return jnp.where((local_ids >= 0) & (local_ids < vocab_rows), local_ids, vocab_rows)

    def bag_counts(id_block):
        local_ids = owned(id_block)
        high_hot = (
            local_ids[:, :, None] // low_width == jnp.arange(high_width)[None, None, :]
        ).astype(jnp.bfloat16)
        low_hot = (
            local_ids[:, :, None] % low_width == jnp.arange(low_width)[None, None, :]
        ).astype(jnp.bfloat16)
        counted = jnp.einsum("rbh,rbl->rhl", high_hot, low_hot, preferred_element_type=jnp.bfloat16)
        return counted.reshape(id_block.shape[0], vocab_rows)

    def single_hot(id_block):
        return (owned(id_block)[:, None] == jnp.arange(vocab_rows)[None, :]).astype(jnp.bfloat16)

    zero_col = jnp.zeros((col_width, 1), jnp.bfloat16)
    padded_out = jnp.concatenate([out_table, zero_col], axis=1)
    all_watch, all_search, all_pos = (
        comm.gather(watch_ids, "batch", 0),
        comm.gather(search_ids, "batch", 0),
        comm.gather(pos_ids, "batch", 0),
    )
    total_rows = all_watch.shape[0]
    block_rows = min(1024, total_rows)
    block_count = total_rows // block_rows
    neg_local = owned(neg_ids)
    neg_part = jnp.take(padded_out, neg_local, axis=1).astype(jnp.float32)

    def flatten_blocks(stacked):
        return stacked.transpose(1, 0, 2).reshape(col_width, total_rows)

    def bag_block(inputs_block):
        watch_block, search_block, pos_block = inputs_block
        watch_part = contract_cols(watch_table, bag_counts(watch_block))
        search_part = contract_cols(search_table, bag_counts(search_block))
        pos_part = contract_cols(out_table, single_hot(pos_block))
        return (watch_part, search_part, pos_part)

    id_blocks = (
        all_watch.reshape(block_count, block_rows, bag_size),
        all_search.reshape(block_count, block_rows, bag_size),
        all_pos.reshape(block_count, block_rows),
    )
    watch_parts, search_parts, pos_parts = lax.map(bag_block, id_blocks)
    watch_sum, search_sum, pos_rows = (
        comm.scatter_sum(flatten_blocks(watch_parts), "batch", 1),
        comm.scatter_sum(flatten_blocks(search_parts), "batch", 1),
        comm.scatter_sum(flatten_blocks(pos_parts), "batch", 1),
    )
    neg_rows, valid_total = comm.total(
        (neg_part, jnp.sum(valid_counts).astype(jnp.float32)), "batch"
    )
    pooled_watch = (watch_sum / bag_size).astype(jnp.bfloat16)
    pooled_search = (search_sum / bag_size).astype(jnp.bfloat16)
    pos_bf = pos_rows.astype(jnp.bfloat16)
    neg_bf = neg_rows.astype(jnp.bfloat16)
    count_here = valid_counts[0]
    full_watch, full_search, full_pos, full_neg = (
        comm.gather(pooled_watch, "col", 0),
        comm.gather(pooled_search, "col", 0),
        comm.gather(pos_bf, "col", 0),
        comm.gather(neg_bf, "col", 0),
    )
    watch_rows = full_watch.T
    search_rows = full_search.T
    pos_full = full_pos.T
    live_rows = jnp.arange(row_count) < count_here
    weight = jnp.where(live_rows, 1.0 / valid_total, 0.0)
    buckets = demo_table.shape[0]
    bucket_counts = jnp.sum(
        (demo_ids[:, :, None] == jnp.arange(buckets)[None, None, :]).astype(jnp.float32), axis=1
    ).astype(jnp.bfloat16)
    demo_vec = jnp.dot(bucket_counts, demo_table, preferred_element_type=jnp.float32)
    joined = jnp.concatenate([watch_rows, search_rows, demo_vec.astype(jnp.bfloat16)], axis=1)
    pre_first = jnp.dot(joined, w_first, preferred_element_type=jnp.float32) + b_first
    act_first = jax.nn.gelu(pre_first).astype(jnp.bfloat16)
    pre_second = jnp.dot(act_first, w_second, preferred_element_type=jnp.float32) + b_second
    act_second = jax.nn.gelu(pre_second).astype(jnp.bfloat16)
    user_block = (
        jnp.dot(act_second, w_third, preferred_element_type=jnp.float32) + b_third
    ).astype(jnp.bfloat16)
    neg_logits = jnp.dot(user_block, full_neg, preferred_element_type=jnp.float32)
    pos_logit = jnp.sum(user_block.astype(jnp.float32) * pos_full.astype(jnp.float32), axis=1)
    row_peak = jnp.maximum(jnp.max(neg_logits, axis=1), pos_logit)
    exp_neg = jnp.exp(neg_logits - row_peak[:, None])
    exp_pos = jnp.exp(pos_logit - row_peak)
    row_total = jnp.sum(exp_neg, axis=1) + exp_pos
    lse = row_peak + jnp.log(row_total)
    loss_here = jnp.sum(weight * (lse - pos_logit))
    grad_neg = (weight[:, None] * exp_neg / row_total[:, None]).astype(jnp.bfloat16)
    grad_pos = (weight * (exp_pos / row_total - 1.0)).astype(jnp.bfloat16)
    grad_user = (
        contract_cols(grad_neg, full_neg)
        + grad_pos.astype(jnp.float32)[:, None] * pos_full.astype(jnp.float32)
    ).astype(jnp.bfloat16)
    neg_row_grad = contract_rows(user_block, grad_neg)
    pos_row_grad = (grad_pos.astype(jnp.float32)[:, None] * user_block.astype(jnp.float32)).astype(
        jnp.bfloat16
    )
    grad_w_third = contract_rows(act_second, grad_user)
    grad_b_third = jnp.sum(grad_user.astype(jnp.float32), axis=0)
    grad_pre_second = gelu_back(pre_second, contract_cols(grad_user, w_third)).astype(jnp.bfloat16)
    grad_w_second = contract_rows(act_first, grad_pre_second)
    grad_b_second = jnp.sum(grad_pre_second.astype(jnp.float32), axis=0)
    grad_pre_first = gelu_back(pre_first, contract_cols(grad_pre_second, w_second)).astype(
        jnp.bfloat16
    )
    grad_w_first = contract_rows(joined, grad_pre_first)
    grad_b_first = jnp.sum(grad_pre_first.astype(jnp.float32), axis=0)
    grad_joined = contract_cols(grad_pre_first, w_first).astype(jnp.bfloat16)
    grad_pw = grad_joined[:, :embed_width]
    grad_ps = grad_joined[:, embed_width : 2 * embed_width]
    grad_demo = contract_rows(bucket_counts, grad_joined[:, 2 * embed_width :])
    col_start = col_slot * col_width
    own_pw = lax.dynamic_slice_in_dim(grad_pw, col_start, col_width, 1).T
    own_ps = lax.dynamic_slice_in_dim(grad_ps, col_start, col_width, 1).T
    own_pos = lax.dynamic_slice_in_dim(pos_row_grad, col_start, col_width, 1).T
    user_vecs = lax.dynamic_slice_in_dim(user_block, col_slot * quarter, quarter, 0)
    all_pw, all_ps, all_dpos = (
        comm.gather(own_pw, "batch", 1),
        comm.gather(own_ps, "batch", 1),
        comm.gather(own_pos, "batch", 1),
    )
    neg_own = lax.dynamic_slice_in_dim(neg_row_grad, col_slot * col_width, col_width, 0)
    sums_out = comm.total(
        (
            grad_w_first,
            grad_b_first,
            grad_w_second,
            grad_b_second,
            grad_w_third,
            grad_b_third,
            grad_demo,
            neg_own,
            loss_here,
        ),
        "batch",
    )
    neg_sum_own = sums_out[7]

    def split_blocks(columns):
        return columns.reshape(col_width, block_count, block_rows).transpose(1, 0, 2)

    def grad_block(running, inputs_block):
        watch_block, search_block, pos_block, block_pw, block_ps, block_pos = inputs_block
        new_watch = running[0] + jnp.dot(
            block_pw, bag_counts(watch_block), preferred_element_type=jnp.float32
        )
        new_search = running[1] + jnp.dot(
            block_ps, bag_counts(search_block), preferred_element_type=jnp.float32
        )
        new_out = running[2] + jnp.dot(
            block_pos, single_hot(pos_block), preferred_element_type=jnp.float32
        )
        return ((new_watch, new_search, new_out), None)

    zeros_table = jnp.zeros((col_width, vocab_rows), jnp.float32)
    (table_watch, table_search, table_out), _ = lax.scan(
        grad_block,
        (zeros_table, zeros_table, zeros_table),
        id_blocks + (split_blocks(all_pw), split_blocks(all_ps), split_blocks(all_dpos)),
    )
    neg_added = (
        jnp.zeros((col_width, vocab_rows + 1), jnp.float32).at[:, neg_local].add(neg_sum_own)
    )
    table_out = table_out + neg_added[:, :vocab_rows]
    return (
        user_vecs,
        sums_out[8],
        table_watch / bag_size,
        table_search / bag_size,
        table_out,
        sums_out[6],
        sums_out[0],
        sums_out[1],
        sums_out[2],
        sums_out[3],
        sums_out[4],
        sums_out[5],
    )


F32, BF16, FP8, I32 = jnp.float32, jnp.bfloat16, jnp.float8_e4m3fn, jnp.int32
MESH = pl.DeviceIdType.MESH
LOW = 256
ROWS_IN_GROUP = 4
BAG_PAD = 64
CHUNK = 256
NEG_FLOOR = -1e30


def dot_as(left, right, left_dim, right_dim):
    return lax.dot_general(
        left, right, (((left_dim,), (right_dim,)), ((), ())), preferred_element_type=F32
    )


def iota(shape, dim):
    return lax.broadcasted_iota(I32, shape, dim)


def one_where(mask, kind):
    return jnp.where(mask, jnp.ones((), BF16), jnp.zeros((), BF16)).astype(kind)


def slot_cap(neg_count, batch):
    mean = neg_count / batch
    return int(math.ceil((mean + 4.5 * math.sqrt(mean)) / CHUNK)) * CHUNK


def gelu(pre):
    bent = jnp.tanh(math.sqrt(2.0 / math.pi) * (pre + 0.044715 * (pre * pre * pre)))
    return 0.5 * pre * (1.0 + bent)


def gelu_slope(pre):
    inner_scale = math.sqrt(2.0 / math.pi)
    square = pre * pre
    bent = jnp.tanh(inner_scale * (pre + 0.044715 * (square * pre)))
    return 0.5 * (1.0 + bent) + 0.5 * pre * (1.0 - bent * bent) * (
        inner_scale * (1.0 + 3.0 * 0.044715 * square)
    )


def flip_rows(value):
    rows, lanes = value.shape
    return pltpu.roll(value.reshape(rows // 8, 8, lanes), 4, 1).reshape(rows, lanes)


def x_place(col):
    return ((col % 2) * 2 + col // 2) * 128


def scattered(n, high, values, low_rows):
    left = []
    for i in range(8):
        at = (n * 8 + i).astype(F32).astype(BF16)
        left.append(jnp.where(high == at, values, jnp.zeros((), BF16)))
    return dot_as(jnp.concatenate(left, axis=0), low_rows, 1, 0)


class Sizes:
    def __init__(self, batch, col, rows, bag, width, vocab, negs, embed, demo_width):
        self.batch, self.col, self.rows, self.bag = batch, col, rows, bag
        self.width, self.vocab, self.negs, self.embed = width, vocab, negs, embed
        self.demo_width = demo_width
        self.total = batch * rows
        self.quarter = rows // col
        self.users = batch * self.quarter
        self.groups = rows // ROWS_IN_GROUP
        self.high = vocab // LOW
        self.high_parts = self.high // 4
        self.cap = slot_cap(negs, batch)
        self.cap_tiles = self.cap // CHUNK
        self.tiles = self.cap_tiles + col
        self.neg_lines = -(-negs // (CHUNK * 8)) * 8
        self.steps = 4
        self.span = self.total // self.steps
        self.x_width = col * 128 + 128


def front_kernel(
    sz,
    watch_ids, search_ids, demo_ids, pos_ids, neg_ids, demo_table, b_first, b_second, b_third, valid_count,
    watch_table, search_table, out_table, w_first, w_second, w_third,
    counts_out, x_out, act1_out, act2_out, gu_out, gps_out, gpf_out, gx_out, buckets_out,
    neg_rows_out, pos_table_out, slots_out, user_out, loss_out, fits_out,
    tabs, tall, mix, w1_raw, w1, w1_own, w2, w3, turned, upright, lines_own, ids, side, neg_dest, neg_digits, counts, found_sums, sums, pieces, x,
    pre1, pre2, acts1, slopes1, acts2, slopes2, users, buckets, slots, picked, neg_all, pos_all, e_cols,
    e_rows, low_rows, pos_table, probs, stats, factors, home, g_send, g_recv, gu, gps, gpf, gx, rg_send, rg_recv, gp_all, loss_all,
    local_sem, out_sem, down_sem, count_sem, ids_s, ids_r, sd_s, sd_r, dx_s, dx_r, rs_s, rs_r, ag_s, ag_r, xx_s, xx_r, co_s, co_r,
    ne_s, ne_r, pe_s, pe_r, ho_s, ho_r, st_s, st_r, gs_s, gs_r, ga_s, ga_r, gx_s, gx_r, gc_s, gc_r,
    rg_s, rg_r, gp_s, gp_r, lo_s, lo_r,
):
    b, c = lax.axis_index("batch"), lax.axis_index("col")
    nb, nc = sz.batch, sz.col
    offset = b * sz.vocab
    cap, width, embed = sz.cap, sz.width, sz.embed
    cx = lax.rem(c + 2, nc)
    ck = c + 1 - 2 * lax.rem(c, 2)
    ckx = lax.rem(ck + 2, nc)

    def batch_peer(i):
        return lax.rem(b + i, nb)

    def batch_from(i):
        return lax.rem(b + nb - i, nb)

    def col_peer(i):
        return lax.rem(c + i, nc)

    def col_from(i):
        return lax.rem(c + nc - i, nc)

    def send(src, dst, ssem, rsem, to):
        return pltpu.make_async_remote_copy(
            src_ref=src, dst_ref=dst, send_sem=ssem, recv_sem=rsem,
            device_id=to, device_id_type=MESH,
        )

    barrier = pltpu.get_barrier_semaphore()
    for i in range(nb):
        for k in range(nc):
            if i + k > 0:
                pl.semaphore_signal(
                    barrier, inc=1, device_id=(batch_peer(i), col_peer(k)), device_id_type=MESH
                )

    loads = [
        (watch_table, tabs.at[0]), (search_table, tabs.at[1]), (out_table, tabs.at[2]),
        (w_first, w1_raw), (w_second, w2), (w_third, w3),
    ]
    loads = [pltpu.make_async_copy(s, d, local_sem.at[i]) for i, (s, d) in enumerate(loads)]
    for load in loads:
        load.start()

    turned[...] = jnp.zeros((BAG_PAD, 128), I32)
    turned[0 : sz.bag, :] = (watch_ids[...] & 0xFFFF) | (search_ids[...] << 16)
    upright[...] = turned[...].T
    for r4 in range(ROWS_IN_GROUP):
        lines_own[:, r4 * BAG_PAD : (r4 + 1) * BAG_PAD] = upright[
            pl.ds(r4, sz.groups, stride=ROWS_IN_GROUP), :
        ]
    share = sz.groups // nc

    def share_of(col):
        return pl.ds(pl.multiple_of(col * share, share), share)

    ids[b] = lines_own[...]
    side[b] = jnp.zeros((8, 128), I32)
    side[b, 0:1, :] = pos_ids[...]
    side[b, 1:2, :] = jnp.full((1, 128), valid_count[0], I32)
    side[b, 2 : 2 + demo_ids.shape[0], :] = demo_ids[...]

    pl.semaphore_wait(barrier, nb * nc - 1)
    last_sends = []
    for i in range(1, nb):
        for k in range(nc):
            place = ids.at[b, share_of(c)]
            copy = send(place, place, ids_s.at[k, i - 1], ids_r.at[k], (batch_peer(i), col_peer(k)))
            copy.start()
            last_sends.append(copy)

    for i in range(1, nb):
        copy = send(side.at[b], side.at[b], sd_s.at[i - 1], sd_r.at[i - 1], (batch_peer(i), c))
        copy.start()
        last_sends.append(copy)

    negs = neg_ids[...]
    lines = sz.neg_lines
    missing = 2 * lines - negs.shape[0]
    second = jnp.concatenate([negs[lines:], jnp.full((missing, 128), -1, I32)], axis=0)
    negs = jnp.concatenate([negs[:lines], second], axis=1)
    neg_local = negs - offset
    own = (neg_local >= 0) & (neg_local < sz.vocab)
    own_bf = one_where(own, BF16)
    upper = one_where(iota((CHUNK, CHUNK), 0) < iota((CHUNK, CHUNK), 1), BF16)
    before = dot_as(own_bf, upper, 1, 0)
    in_row = dot_as(own_bf, jnp.ones((CHUNK, CHUNK), BF16), 1, 0)
    lower = one_where(iota((lines, lines), 1) < iota((lines, lines), 0), BF16)
    rows_before = dot_as(lower, in_row.astype(BF16), 1, 0)
    neg_dest[...] = jnp.where(own, before + rows_before, -1.0)
    owned_count = dot_as(jnp.ones((8, lines), BF16), in_row.astype(BF16), 1, 0)
    most = jnp.zeros((1, 1), F32)
    for shard in range(nb):
        part = negs - shard * sz.vocab
        hits = jnp.where((part >= 0) & (part < sz.vocab), 1.0, 0.0)
        most = jnp.maximum(most, jnp.sum(jnp.sum(hits, axis=1, keepdims=True), axis=0, keepdims=True))
    fits_out[...] = jnp.where(most <= float(cap), 1, 0)
    for digit in range(4):
        neg_digits[digit] = ((neg_local >> (4 * digit)) & 15).astype(F32)

    def compact(k, total):
        place = neg_dest[pl.ds(k, 1), :]
        hot = one_where(place == iota((cap, CHUNK), 0).astype(F32), FP8)
        line = iota((32, CHUNK), 0)
        value = jnp.where(line == 4, 1.0, 0.0)
        for digit in range(4):
            value = jnp.where(line == digit, neg_digits[digit, pl.ds(k, 1), :], value)
        return total + dot_as(value.astype(FP8), hot, 1, 1)

    slot = lax.fori_loop(0, lines, compact, jnp.zeros((32, cap), F32))
    neg_low = slot[0:1] + 16.0 * slot[1:2]
    neg_high = jnp.where(slot[4:5] > 0.5, slot[2:3] + 16.0 * slot[3:4], -1.0)
    slots[...] = jnp.zeros((sz.tiles, 8, CHUNK), F32)
    for k in range(sz.cap_tiles):
        slots[k, 0:1, :] = neg_high[:, k * CHUNK : (k + 1) * CHUNK]
        slots[k, 1:2, :] = neg_low[:, k * CHUNK : (k + 1) * CHUNK]

    for t in range(2):
        loads[t].wait()

    def turn(n, _):
        t, hh = n // sz.high_parts, n % sz.high_parts
        base = pl.multiple_of(hh * 4 * LOW, 4 * LOW)
        stack = jnp.concatenate([tabs[t, :, pl.ds(base + i * LOW, LOW)] for i in range(4)], axis=0)
        mix[t, pl.ds(pl.multiple_of(hh * LOW, LOW), LOW), :] = stack.T
        return 0

    lax.fori_loop(0, 2 * sz.high_parts, turn, 0)

    loads[2].wait()

    def stack_up(hh, _):
        for i in range(4):
            tall[pl.ds(pl.multiple_of((hh * 4 + i) * width, width), width), :] = tabs[
                2, :, pl.ds(pl.multiple_of((hh * 4 + i) * LOW, LOW), LOW)
            ]
        return 0

    lax.fori_loop(0, sz.high_parts, stack_up, 0)

    def pick_tile(k, _):
        high, low = slots[k, 0:1, :], slots[k, 1:2, :]
        low_hot = one_where(low.astype(BF16) == iota((LOW, CHUNK), 0).astype(BF16), BF16)
        total = jnp.zeros((width, CHUNK), F32)
        for part in range(4):
            tall_rows = width * sz.high // 4
            got = dot_as(tall[part * tall_rows : (part + 1) * tall_rows, :], low_hot, 1, 0)
            for i in range(sz.high // 4):
                at = float(part * (sz.high // 4) + i)
                total = total + jnp.where(high == at, got[i * width : (i + 1) * width], 0.0)
        picked[k] = total.astype(BF16)
        return 0

    lax.fori_loop(0, sz.cap_tiles, pick_tile, 0)
    neg_part = picked.at[pl.ds(0, sz.cap_tiles)]
    for i in range(1, nc):
        copy = send(neg_part, neg_all.at[c], ne_s.at[i - 1], ne_r.at[i - 1], (b, col_peer(i)))
        copy.start()
        last_sends.append(copy)
    for k in range(sz.cap_tiles):
        neg_all[c, k] = picked[k]

    loads[3].wait()
    w1[nc * 128 :, :] = jnp.zeros((128, w1.shape[1]), BF16)
    for i in range(nc):
        at = x_place(i)
        w1[at : at + width, :] = w1_raw[i * width : (i + 1) * width, :]
        w1[at + width : at + 128, :] = w1_raw[embed + i * width : embed + (i + 1) * width, :]
    w1[nc * 128 : nc * 128 + sz.demo_width, :] = w1_raw[2 * embed :, :]
    loads[4].wait()
    loads[5].wait()

    w1_own[...] = jnp.zeros(w1_own.shape, BF16)
    w1_own[0 : 2 * width, :] = w1[pl.ds(pl.multiple_of((lax.rem(c, 2) * 2 + c // 2) * 128, 128), 128), :]
    w1_own[2 * width : 2 * width + sz.demo_width, :] = w1_raw[2 * embed :, :]
    for k in range(nc):
        place = ids.at[pl.ds(0, nb - 1), share_of(col_from(k))]
        send(place, place, ids_s.at[k, 0], ids_r.at[k], (b, c)).wait_recv()

    users_shape = (nb, CHUNK)
    at_block = iota(users_shape, 1) // sz.quarter == iota(users_shape, 0)

    def demo_part():
        for i in range(1, nb):
            place = side.at[batch_from(i)]
            send(place, place, sd_s.at[i - 1], sd_r.at[i - 1], (b, c)).wait_recv()
        bucket_total = jnp.zeros((buckets.shape[0], sz.total), BF16)
        bucket_line = iota((buckets.shape[0], sz.total), 0).astype(BF16)
        for field in range(demo_ids.shape[0]):
            line = jnp.concatenate([side[j, 2 + field : 3 + field, :] for j in range(nb)], axis=1)
            bucket_total = bucket_total + one_where(line.astype(F32).astype(BF16) == bucket_line, BF16)
        buckets[...] = bucket_total
        demo_rows = demo_table[...].astype(F32).T.astype(BF16)
        x[:, nc * 128 :] = jnp.zeros((sz.total, 128), BF16)
        x[:, nc * 128 : nc * 128 + sz.demo_width] = dot_as(bucket_total, demo_rows, 0, 0).astype(BF16)

    def pos_part():
        all_pos = jnp.concatenate([side[j, 0:1, :] for j in range(nb)], axis=0)
        pos_local = all_pos - offset
        pos_owned = (pos_local >= 0) & (pos_local < sz.vocab)
        pos_pair = jnp.concatenate(
            [
                jnp.where(pos_owned, pos_local >> 8, 255).astype(F32),
                (pos_local & 255).astype(F32),
            ],
            axis=0,
        ).astype(BF16)
        for quarter in range(nc):
            shape = (128, CHUNK)
            pick = one_where(iota(shape, 0) == quarter * sz.quarter + iota(shape, 1) % sz.quarter, BF16)
            wide = dot_as(pos_pair, pick, 1, 0)
            high = jnp.sum(jnp.where(at_block, wide[0:nb], 0.0), axis=0, keepdims=True)
            low = jnp.sum(jnp.where(at_block, wide[nb : 2 * nb], 0.0), axis=0, keepdims=True)
            slots[sz.cap_tiles + quarter, 0:1, :] = jnp.where(high > 254.0, -1.0, high)
            slots[sz.cap_tiles + quarter, 1:2, :] = low
        slots_out[...] = slots[...]
        lax.fori_loop(sz.cap_tiles, sz.tiles, pick_tile, 0)
        pos_all[c] = picked[sz.cap_tiles + c]
        for i in range(1, nc):
            pos_send(i).start()

    def slot_rows():
        for i in range(1, nc):
            src = col_from(i)
            send(neg_all.at[src], neg_all.at[src], ne_s.at[i - 1], ne_r.at[i - 1], (b, c)).wait_recv()
            send(pos_all.at[src], pos_all.at[src], pe_s.at[i - 1], pe_r.at[i - 1], (b, c)).wait_recv()
        for i in range(nc):
            for k in range(sz.cap_tiles):
                e_cols[i * width : (i + 1) * width, k * CHUNK : (k + 1) * CHUNK] = neg_all[i, k]
            e_cols[i * width : (i + 1) * width, cap:] = pos_all[i]
        e_rows[...] = e_cols[...].T
        for i in range(1, nb):
            home_send(i).start()

    def home_send(i):
        to = batch_peer(i)
        rows = e_rows.at[pl.ds(pl.multiple_of(cap + to * sz.quarter, sz.quarter), sz.quarter)]
        return send(rows, home.at[i - 1], ho_s.at[i - 1], ho_r.at[i - 1], (to, c))

    def pos_send(i):
        to = col_peer(i)
        return send(picked.at[sz.cap_tiles + to], pos_all.at[c], pe_s.at[i - 1], pe_r.at[i - 1], (b, to))

    span = sz.span
    piece = span // nb
    lane_mod = iota((16, CHUNK), 1) % BAG_PAD
    lane_r4 = iota((16, CHUNK), 1) // BAG_PAD
    odd_group = iota((16, CHUNK), 0) & 1
    blocks = span // sz.rows
    parts_in_block = sz.groups // 16

    def count_copy(t, table, slot_at):
        rows = pl.ds(pl.multiple_of(t * span, span), span)
        return pltpu.make_async_copy(
            counts.at[table, slot_at], counts_out.at[table, :, :, rows], count_sem.at[table, slot_at]
        )

    def bag_table(t, table, between):
        slot_at = lax.rem(t, 2)

        @pl.when(t >= 2)
        def _():
            count_copy(t - 2, table, slot_at).wait()

        code_line = iota((4 * sz.high, CHUNK), 0).astype(BF16)
        low_line = iota((LOW, CHUNK), 0).astype(BF16)

        def groups_of(q, _):
            block = t * blocks + q // parts_in_block
            word = ids[block, pl.ds(pl.multiple_of((q % parts_in_block) * 16, 16), 16), :]
            value = lax.shift_right_logical(word, 16 * table) & 0xFFFF
            local = value - offset
            mine = (local >= 0) & (local < sz.vocab) & (lane_mod < sz.bag)
            code = jnp.where(mine, ((local >> 8) ^ odd_group) * 4 + lane_r4, -1).astype(F32).astype(BF16)
            low = (local & 255).astype(F32).astype(BF16)
            low_half = iota((sz.high // 2, 8, LOW), 1) < 4
            for quad in range(4):
                pairs = []
                for pair in range(2):
                    found = []
                    for g in (quad * 4 + pair * 2, quad * 4 + pair * 2 + 1):
                        left = one_where(code[g : g + 1, :] == code_line, FP8)
                        right = one_where(low[g : g + 1, :] == low_line, FP8)
                        found.append(dot_as(left, right, 1, 1).reshape(sz.high // 2, 8, LOW))
                    even = jnp.where(low_half, found[0], found[1])
                    odd = jnp.where(low_half, found[1], found[0])
                    pairs.append((even, odd))
                line = pl.ds(pl.multiple_of(q * 64 + quad * 16, 16), 16)
                for part in range(sz.high):
                    both = [pairs[k][part % 2][part // 2] for k in range(2)]
                    counts[table, slot_at, part // 4, part % 4, line, :] = jnp.concatenate(
                        both, axis=0
                    ).astype(BF16)
            return 0

        lax.fori_loop(0, blocks * parts_in_block, groups_of, 0)
        count_copy(t, table, slot_at).start()
        between()
        left = jnp.concatenate(
            [counts[table, slot_at, hh].reshape(4 * span, LOW) for hh in range(sz.high_parts)], axis=1
        )
        total = dot_as(left, mix[table], 1, 0)
        left_side = iota((span, 128), 1) < width
        first = jnp.where(left_side, total[0:span, 0:128], flip_rows(total[span : 2 * span, 0:128]))
        second = jnp.where(left_side, total[2 * span : 3 * span, 128:], flip_rows(total[3 * span :, 128:]))
        both = first + second
        found_sums[table] = both + pltpu.roll(both, width, 1)

    def bag_sums(t):
        joined = jnp.where(iota((span, 128), 1) < width, found_sums[0], found_sums[1])
        sums[t] = joined.astype(BF16)
        for i in range(1, nb):
            to = batch_peer(i)
            send(
                sums.at[t, pl.ds(pl.multiple_of(to * piece, piece), piece)], pieces.at[t, i - 1],
                rs_s.at[t, i - 1], rs_r.at[t], (to, c),
            ).start()

    def lanes_of(col):
        return pl.ds(pl.multiple_of((lax.rem(col, 2) * 2 + col // 2) * 128, 128), 128)

    def x_at(t, col):
        return x.at[pl.ds(pl.multiple_of(t * span, span), span), lanes_of(col)]

    def x_pair(t, col):
        return x.at[
            pl.ds(pl.multiple_of(t * span, span), span),
            pl.ds(pl.multiple_of(lax.rem(col, 2) * 256, 256), 256),
        ]

    def x_piece(t, owner):
        return x.at[
            pl.ds(pl.multiple_of(t * span + owner * piece, piece), piece), lanes_of(c)
        ]

    def reduce_step(t, direct=False):
        send(pieces.at[t], pieces.at[t], rs_s.at[t, 0], rs_r.at[t], (b, c)).wait_recv()
        total = sums[t, pl.ds(pl.multiple_of(b * piece, piece), piece), :].astype(F32)
        for i in range(nb - 1):
            total = total + pieces[t, i].astype(F32)
        x[
            pl.ds(pl.multiple_of(t * span + b * piece, piece), piece), lanes_of(c)
        ] = (total / sz.bag).astype(BF16)
        for i in range(1, nb):
            send(x_piece(t, b), x_piece(t, b), ag_s.at[t, i - 1], ag_r.at[t], (batch_peer(i), c)).start()
        if direct:
            for i in range(nb):
                for k in range(1, nc):
                    direct_send(t, i, k).start()

    def direct_send(t, i, k):
        return send(
            x_piece(t, b), x_piece(t, b), dx_s.at[k - 1, i], dx_r.at[k - 1], (batch_peer(i), col_peer(k))
        )

    def direct_wait(t):
        send(pieces.at[t], pieces.at[t], ag_s.at[t, 0], ag_r.at[t], (b, c)).wait_recv()
        for k in range(1, nc):
            place = x_at(t, col_from(k))
            send(place, place, dx_s.at[k - 1, 0], dx_r.at[k - 1], (b, c)).wait_recv()

    def cross_step(t):
        send(pieces.at[t], pieces.at[t], ag_s.at[t, 0], ag_r.at[t], (b, c)).wait_recv()
        send(x_at(t, c), x_at(t, c), xx_s.at[t], xx_r.at[t], (b, cx)).start()

    def core_step(t):
        send(x_at(t, cx), x_at(t, cx), xx_s.at[t], xx_r.at[t], (b, cx)).wait_recv()
        send(x_pair(t, c), x_pair(t, c), co_s.at[t], co_r.at[t], (b, ck)).start()

    def full_step(t):
        send(x_pair(t, ck), x_pair(t, ck), co_s.at[t], co_r.at[t], (b, ck)).wait_recv()

    def tower(k):
        at = pl.ds(pl.multiple_of(k * span, span), span)
        pre = dot_as(x[at, :], w1[...], 1, 0) + b_first[...]
        pre1[at, :] = pre
        value = gelu(pre).astype(BF16)
        acts1[at, :] = value
        pre = dot_as(value, w2[...], 1, 0) + b_second[...]
        pre2[at, :] = pre
        value = gelu(pre).astype(BF16)
        acts2[at, :] = value
        users[at, :] = (dot_as(value, w3[...], 1, 0) + b_third[...]).astype(BF16)

    def slopes(k):
        at = pl.ds(pl.multiple_of(k * span, span), span)
        slopes1[at, :] = gelu_slope(pre1[at, :]).astype(BF16)
        slopes2[at, :] = gelu_slope(pre2[at, :]).astype(BF16)

    bag_ticks = 2 * sz.steps
    last = sz.steps - 1

    def tick(n, _):
        half = n // 2
        odd = lax.rem(n, 2) == 1

        def between():
            @pl.when(odd & (n >= 3))
            def _():
                reduce_step((n - 3) // 2)

        @pl.when(n < bag_ticks)
        def _():
            bag_table(half, lax.rem(n, 2), between)

        @pl.when((n < bag_ticks) & odd)
        def _():
            bag_sums(half)

        @pl.when(n == bag_ticks)
        def _():
            demo_part()

        @pl.when(n == bag_ticks + 1)
        def _():
            pos_part()

        @pl.when(n == bag_ticks + 3)
        def _():
            slot_rows()

        @pl.when((~odd) & (n >= 6) & (n <= bag_ticks))
        def _():
            full_step((n - 6) // 2)

        done = jnp.where(n <= bag_ticks, 0, jnp.where(n <= bag_ticks + 2, 1, last))
        ready = jnp.where(
            n < bag_ticks, 0, jnp.where(n <= bag_ticks + 1, 1, jnp.where(n == bag_ticks + 2, last, sz.steps))
        )

        def some_tower(k, _):
            @pl.when(k == last - 1)
            def _():
                full_step(k)

            @pl.when(k == last)
            def _():
                direct_wait(last)

            tower(k)
            return 0

        lax.fori_loop(done, ready, some_tower, 0)

        @pl.when((~odd) & (n >= 4) & (n <= bag_ticks))
        def _():
            cross_step((n - 4) // 2)

        @pl.when(n == bag_ticks)
        def _():
            reduce_step(last, direct=True)

        @pl.when(odd & (n >= 5) & (n <= bag_ticks + 1))
        def _():
            core_step((n - 5) // 2)

        return 0

    lax.fori_loop(0, bag_ticks + 4, tick, 0)

    valid = jnp.concatenate([side[j, 1:2, :] for j in range(nb)], axis=0)
    valid_wide = jnp.concatenate([valid] * (sz.users // 128), axis=1).astype(F32)
    live_count = jnp.sum(jnp.where(at_block, valid_wide, 0.0), axis=0, keepdims=True)
    valid_total = jnp.sum(valid_wide, axis=0, keepdims=True)
    user_place = c * sz.quarter + iota((1, sz.users), 1) % sz.quarter
    weight = jnp.where(user_place.astype(F32) < live_count, 1.0 / valid_total, 0.0)

    out_copies = [(x, x_out), (acts1, act1_out), (acts2, act2_out), (buckets, buckets_out)]
    out_copies = [pltpu.make_async_copy(s, d, out_sem.at[i]) for i, (s, d) in enumerate(out_copies)]
    for copy in out_copies:
        copy.start()
    user_out[...] = users[pl.ds(pl.multiple_of(b * sz.rows + c * sz.quarter, sz.quarter), sz.quarter), :]

    def users_of(quarter):
        return jnp.concatenate(
            [
                users[pl.ds(pl.multiple_of(j * sz.rows + quarter * sz.quarter, sz.quarter), sz.quarter), :]
                for j in range(nb)
            ],
            axis=0,
        )

    quarter_users = users_of(c)
    logits = dot_as(e_rows[...], quarter_users, 1, 1)
    neg_logits, pos_logits = logits[0:cap], logits[cap:]
    slot_ok = iota((cap, sz.users), 0).astype(F32) < owned_count[0:1, : sz.users]
    pos_here = slots[sz.cap_tiles + c, 0:1, :]
    pos_ok = (iota((sz.users, sz.users), 0) == iota((sz.users, sz.users), 1)) & (pos_here >= 0.0)
    neg_logits = jnp.where(slot_ok, neg_logits, NEG_FLOOR)
    pos_masked = jnp.where(pos_ok, pos_logits, NEG_FLOOR)
    peak = jnp.maximum(
        jnp.max(neg_logits, axis=0, keepdims=True), jnp.max(pos_masked, axis=0, keepdims=True)
    )
    bare = jnp.where(slot_ok, jnp.exp(neg_logits - peak), 0.0)
    mass = jnp.sum(bare, axis=0, keepdims=True) + jnp.sum(
        jnp.where(pos_ok, jnp.exp(pos_masked - peak), 0.0), axis=0, keepdims=True
    )
    pos_value = jnp.sum(jnp.where(pos_ok, pos_logits, 0.0), axis=0, keepdims=True)
    stats[b] = jnp.concatenate([peak, mass, pos_value, jnp.zeros((5, sz.users), F32)], axis=0)
    for i in range(1, nb):
        copy = send(stats.at[b], stats.at[b], st_s.at[i - 1], st_r.at[i - 1], (batch_peer(i), c))
        copy.start()
        last_sends.append(copy)

    probs[...] = bare.astype(BF16)
    grad_user = dot_as(probs[...], e_rows[0:cap, :], 0, 0)
    for j in range(nb):
        g_send[j] = grad_user[j * sz.quarter : (j + 1) * sz.quarter].astype(BF16)
    for i in range(1, nb):
        to = batch_peer(i)
        copy = send(g_send.at[to], g_recv.at[i - 1], gs_s.at[i - 1], gs_r.at[i - 1], (to, c))
        copy.start()
        last_sends.append(copy)

    def some_slopes(k, _):
        slopes(k)
        return 0

    lax.fori_loop(0, sz.steps, some_slopes, 0)
    for i in range(1, nb):
        src = batch_from(i)
        send(stats.at[src], stats.at[src], st_s.at[i - 1], st_r.at[i - 1], (b, c)).wait_recv()
    order = [batch_from(i) for i in range(nb)]
    peaks = [stats[j, 0:1, :] for j in range(nb)]
    top = peaks[0]
    for j in range(1, nb):
        top = jnp.maximum(top, peaks[j])
    full_mass = jnp.zeros((1, sz.users), F32)
    pos_logit = jnp.zeros((1, sz.users), F32)
    for j in range(nb):
        full_mass = full_mass + stats[j, 1:2, :] * jnp.exp(peaks[j] - top)
        pos_logit = pos_logit + stats[j, 2:3, :]
    lse = top + jnp.log(full_mass)
    loss_part = jnp.sum(weight * (lse - pos_logit), axis=1, keepdims=True)
    scale = weight / full_mass
    pos_grad = weight * (jnp.exp(pos_logit - top) / full_mass - 1.0)
    lines_of = [jnp.exp(stats[j, 0:1, :] - top) * scale for j in order]
    lines_of += [pos_grad, jnp.zeros((16 - nb - 1, sz.users), F32)]
    factors[...] = jnp.concatenate(lines_of, axis=0).T
    probs[...] = jnp.where(slot_ok, jnp.exp(neg_logits - top) * scale, 0.0).astype(BF16)
    gp_all[c] = jnp.broadcast_to(jnp.where(pos_here >= 0.0, pos_grad, 0.0), (8, sz.users))
    loss_all[c] = jnp.broadcast_to(loss_part, (8, 128))
    for i in range(1, nc):
        to = col_peer(i)
        for copy in (
            send(gp_all.at[c], gp_all.at[c], gp_s.at[i - 1], gp_r.at[i - 1], (b, to)),
            send(loss_all.at[c], loss_all.at[c], lo_s.at[i - 1], lo_r.at[i - 1], (b, to)),
        ):
            copy.start()
            last_sends.append(copy)
    rows_grad = dot_as(probs[...], quarter_users, 1, 0)
    rows_grad = rows_grad.T.astype(BF16)
    for i in range(nc):
        rg_send[i] = rows_grad[i * width : (i + 1) * width]
    for i in range(1, nc):
        to = col_peer(i)
        copy = send(rg_send.at[to], rg_recv.at[c], rg_s.at[i - 1], rg_r.at[i - 1], (b, to))
        copy.start()
        last_sends.append(copy)
    rg_recv[c] = rg_send[c]
    for i in range(1, nb):
        send(g_send.at[0], g_recv.at[i - 1], gs_s.at[i - 1], gs_r.at[i - 1], (b, c)).wait_recv()
    factor = factors[pl.ds(pl.multiple_of(b * sz.quarter, sz.quarter), sz.quarter), :]
    total = factor[:, 0:1] * g_send[b].astype(F32)
    own_pos = e_rows[pl.ds(pl.multiple_of(cap + b * sz.quarter, sz.quarter), sz.quarter), :].astype(F32)
    for i in range(1, nb):
        home_send(i).wait_recv()
        total = total + factor[:, i : i + 1] * g_recv[i - 1].astype(F32)
        own_pos = own_pos + home[i - 1].astype(F32)
    total = total + factor[:, nb : nb + 1].astype(BF16).astype(F32) * own_pos

    def gu_at(block, col):
        return gu.at[block, pl.ds(pl.multiple_of(col * sz.quarter, sz.quarter), sz.quarter), :]

    def gu_all(col):
        return gu.at[:, pl.ds(pl.multiple_of(col * sz.quarter, sz.quarter), sz.quarter), :]

    gu[b, pl.ds(pl.multiple_of(c * sz.quarter, sz.quarter), sz.quarter), :] = total.astype(BF16)
    for i in range(1, nb):
        copy = send(gu_at(b, c), gu_at(b, c), ga_s.at[i - 1], ga_r.at[i - 1], (batch_peer(i), c))
        copy.start()
        last_sends.append(copy)
    for i in range(nb):
        copy = send(gu_at(b, c), gu_at(b, c), gx_s.at[i], gx_r.at[i], (batch_peer(i), cx))
        copy.start()
        last_sends.append(copy)

    for k in range(nc):
        low = slots[sz.cap_tiles + k, 1:2, :].astype(BF16)
        hot = one_where(low == iota((LOW, CHUNK), 0).astype(BF16), BF16)
        low_rows[k * CHUNK : (k + 1) * CHUNK, :] = hot.T
    pick_own = one_where(iota((width, embed), 1) == c * width + iota((width, embed), 0), BF16)
    for i in range(1, nc):
        src = col_from(i)
        send(gp_all.at[src], gp_all.at[src], gp_s.at[i - 1], gp_r.at[i - 1], (b, c)).wait_recv()
    pos_rows = []
    for quarter in range(nc):
        own_part = dot_as(pick_own, users_of(quarter), 1, 1)
        grad = gp_all[quarter, 0:1, :].astype(BF16).astype(F32)
        mine = slots[sz.cap_tiles + quarter, 0:1, :] >= 0.0
        pos_rows.append(jnp.where(mine, grad * own_part, 0.0).astype(BF16))
    pos_rows = jnp.concatenate(pos_rows, axis=1)
    pos_parts = jnp.concatenate(
        [slots[sz.cap_tiles + k, 0:1, :] for k in range(nc)], axis=1
    ).astype(BF16)

    def pos_scatter(n, _):
        found = scattered(n, pos_parts, pos_rows, low_rows[...])
        for j in range(2):
            for i in range(4):
                pos_table[n * 2 + j, :, i * LOW : (i + 1) * LOW] = found[
                    (j * 4 + i) * width : (j * 4 + i + 1) * width
                ]
        return 0

    lax.fori_loop(0, sz.high_parts // 2, pos_scatter, 0)
    pos_copy = pltpu.make_async_copy(pos_table, pos_table_out, out_sem.at[5])
    pos_copy.start()
    for i in range(1, nb):
        src = batch_from(i)
        send(gu_at(src, c), gu_at(src, c), ga_s.at[i - 1], ga_r.at[i - 1], (b, c)).wait_recv()
    copy = send(gu_all(c), gu_all(c), gc_s.at[0], gc_r.at[0], (b, ck))
    copy.start()
    last_sends.append(copy)

    def rows_at(ref, col):
        return ref.at[:, pl.ds(pl.multiple_of(col * sz.quarter, sz.quarter), sz.quarter), :]

    def down_copies(col, i):
        return [
            pltpu.make_async_copy(rows_at(kept, col), rows_at(out, col), down_sem.at[i, k])
            for k, (kept, out) in enumerate(((gps, gps_out), (gpf, gpf_out), (gx, gx_out)))
        ]

    def down(i, col):
        def spread_out(ref, value):
            for j in range(nb):
                ref[j, pl.ds(pl.multiple_of(col * sz.quarter, sz.quarter), sz.quarter), :] = value[
                    j * sz.quarter : (j + 1) * sz.quarter
                ]

        def gathered(ref):
            return jnp.concatenate(
                [
                    ref[pl.ds(pl.multiple_of(j * sz.rows + col * sz.quarter, sz.quarter), sz.quarter), :]
                    for j in range(nb)
                ],
                axis=0,
            )

        top = jnp.concatenate(
            [gu[j, pl.ds(pl.multiple_of(col * sz.quarter, sz.quarter), sz.quarter), :] for j in range(nb)],
            axis=0,
        )
        second = (dot_as(top, w3[...], 1, 1) * gathered(slopes2).astype(F32)).astype(BF16)
        spread_out(gps, second)
        first = (dot_as(second, w2[...], 1, 1) * gathered(slopes1).astype(F32)).astype(BF16)
        spread_out(gpf, first)
        spread_out(gx, dot_as(first, w1_own[...], 1, 1).astype(BF16))
        for copy in down_copies(col, i):
            copy.start()

    def quarter_down(i, _):
        flip = jnp.where(i == 0, c, jnp.where(i == 1, ck, jnp.where(i == 2, cx, ckx)))

        @pl.when(i == 1)
        def _():
            send(gu_all(ck), gu_all(ck), gc_s.at[0], gc_r.at[0], (b, ck)).wait_recv()

        @pl.when(i == 2)
        def _():
            for k in range(nb):
                src = batch_from(k)
                send(gu_at(src, cx), gu_at(src, cx), gx_s.at[k], gx_r.at[k], (b, cx)).wait_recv()
            send(gu_all(cx), gu_all(cx), gc_s.at[1], gc_r.at[1], (b, ck)).start()

        @pl.when(i == 3)
        def _():
            send(gu_all(ckx), gu_all(ckx), gc_s.at[1], gc_r.at[1], (b, ck)).wait_recv()

        down(i, flip)
        return 0

    lax.fori_loop(0, nc, quarter_down, 0)
    gu_copy = pltpu.make_async_copy(gu, gu_out, out_sem.at[4])
    gu_copy.start()

    for i in range(1, nc):
        src = col_from(i)
        send(loss_all.at[src], loss_all.at[src], lo_s.at[i - 1], lo_r.at[i - 1], (b, c)).wait_recv()
        send(rg_recv.at[src], rg_recv.at[src], rg_s.at[i - 1], rg_r.at[i - 1], (b, c)).wait_recv()
    loss = loss_all[0]
    neg_total = rg_recv[0].astype(F32)
    for i in range(1, nc):
        loss = loss + loss_all[i]
        neg_total = neg_total + rg_recv[i].astype(F32)
    neg_rows_out[...] = neg_total.astype(BF16)
    loss_out[...] = loss[0:1, 0:1]

    last_sends.append(send(gu_all(cx), gu_all(cx), gc_s.at[1], gc_r.at[1], (b, ck)))
    for i in range(1, nc):
        last_sends.append(pos_send(i))
    for i in range(1, nb):
        last_sends.append(home_send(i))
    for copy in last_sends:
        copy.wait_send()

    def drain(t, _):
        for i in range(1, nb):
            send(sums.at[t, pl.ds(0, piece)], pieces.at[t, 0], rs_s.at[t, i - 1], rs_r.at[t], (b, c)).wait_send()
            send(x_piece(t, b), x_piece(t, b), ag_s.at[t, i - 1], ag_r.at[t], (b, c)).wait_send()

        @pl.when(t < last)
        def _():
            send(x_at(t, c), x_at(t, c), xx_s.at[t], xx_r.at[t], (b, cx)).wait_send()
            send(x_pair(t, c), x_pair(t, c), co_s.at[t], co_r.at[t], (b, ck)).wait_send()

        return 0

    lax.fori_loop(0, sz.steps, drain, 0)
    for i in range(nb):
        for k in range(1, nc):
            direct_send(last, i, k).wait_send()
    for table in range(2):
        for t in (sz.steps - 2, sz.steps - 1):
            count_copy(t, table, t % 2).wait()
    gu_copy.wait()
    pos_copy.wait()
    for copy in out_copies:
        copy.wait()
    for i, col in enumerate((c, ck, cx, ckx)):
        for copy in down_copies(col, i):
            copy.wait()


def front(sz, args):
    nb, nc, total = sz.batch, sz.col, sz.total
    width, embed, cap, users = sz.width, sz.embed, sz.cap, sz.users
    slots = cap + users
    first, second = args["w_second"].shape
    buckets = args["demo_table"].shape[0]
    x_width = sz.x_width
    vmem = pl.BlockSpec(memory_space=pltpu.VMEM)
    smem = pl.BlockSpec(memory_space=pltpu.SMEM)
    hbm = pl.BlockSpec(memory_space=pl.ANY)
    dma = pltpu.SemaphoreType.DMA

    def shape(dims, kind=BF16):
        return jax.ShapeDtypeStruct(dims, kind)

    outs = [
        (shape((2, sz.high_parts, 4, total, LOW)), hbm), (shape((total, x_width)), hbm),
        (shape((total, first)), hbm), (shape((total, second)), hbm), (shape((nb, sz.rows, embed)), hbm),
        (shape((nb, sz.rows, second)), hbm), (shape((nb, sz.rows, first)), hbm),
        (shape((nb, sz.rows, 256)), hbm), (shape((buckets, total)), hbm),
        (shape((width, cap)), vmem), (shape((sz.high_parts, width, 4 * LOW), F32), hbm),
        (shape((sz.tiles, 8, CHUNK), F32), vmem),
        (shape((sz.quarter, embed)), vmem), (shape((1, 1), F32), vmem), (shape((1, 1), I32), vmem),
    ]
    scratch = [
        pltpu.VMEM((3, width, sz.vocab), BF16),
        pltpu.VMEM((sz.high * width, LOW), BF16),
        pltpu.VMEM((2, sz.high_parts * LOW, 4 * width), BF16),
        pltpu.VMEM(args["w_first"].shape, BF16),
        pltpu.VMEM((x_width, first), BF16),
        pltpu.VMEM((256, first), BF16),
        pltpu.VMEM((first, second), BF16),
        pltpu.VMEM((second, embed), BF16),
        pltpu.VMEM((BAG_PAD, 128), I32),
        pltpu.VMEM((sz.rows, BAG_PAD), I32),
        pltpu.VMEM((sz.groups, CHUNK), I32),
        pltpu.VMEM((nb, sz.groups, CHUNK), I32),
        pltpu.VMEM((nb, 8, 128), I32),
        pltpu.VMEM((sz.neg_lines, CHUNK), F32),
        pltpu.VMEM((4, sz.neg_lines, CHUNK), F32),
        pltpu.VMEM((2, 2, sz.high_parts, 4, sz.span, LOW), BF16),
        pltpu.VMEM((2, sz.span, 128), F32),
        pltpu.VMEM((sz.steps, sz.span, 128), BF16),
        pltpu.VMEM((sz.steps, nb - 1, sz.span // nb, 128), BF16),
        pltpu.VMEM((total, x_width), BF16),
        pltpu.VMEM((total, first), F32),
        pltpu.VMEM((total, second), F32),
        pltpu.VMEM((total, first), BF16),
        pltpu.VMEM((total, first), BF16),
        pltpu.VMEM((total, second), BF16),
        pltpu.VMEM((total, second), BF16),
        pltpu.VMEM((total, embed), BF16),
        pltpu.VMEM((buckets, total), BF16),
        pltpu.VMEM((sz.tiles, 8, CHUNK), F32),
        pltpu.VMEM((sz.tiles, width, CHUNK), BF16),
        pltpu.VMEM((nc, sz.cap_tiles, width, CHUNK), BF16),
        pltpu.VMEM((nc, width, users), BF16),
        pltpu.VMEM((embed, slots), BF16),
        pltpu.VMEM((slots, embed), BF16),
        pltpu.VMEM((nc * CHUNK, LOW), BF16),
        pltpu.VMEM((sz.high_parts, width, 4 * LOW), F32),
        pltpu.VMEM((cap, users), BF16),
        pltpu.VMEM((nb, 8, users), F32),
        pltpu.VMEM((users, 16), F32),
        pltpu.VMEM((nb - 1, sz.quarter, embed), BF16),
        pltpu.VMEM((nb, sz.quarter, embed), BF16),
        pltpu.VMEM((nb - 1, sz.quarter, embed), BF16),
        pltpu.VMEM((nb, sz.rows, embed), BF16),
        pltpu.VMEM((nb, sz.rows, second), BF16),
        pltpu.VMEM((nb, sz.rows, first), BF16),
        pltpu.VMEM((nb, sz.rows, 256), BF16),
        pltpu.VMEM((nc, width, cap), BF16),
        pltpu.VMEM((nc, width, cap), BF16),
        pltpu.VMEM((nc, 8, users), F32),
        pltpu.VMEM((nc, 8, 128), F32),
        dma((6,)), dma((6,)), dma((nc, 3)), dma((2, 2)),
        dma((nc, nb - 1)), dma((nc,)), dma((nb - 1,)), dma((nb - 1,)), dma((nc - 1, nb)), dma((nc - 1,)),
        dma((sz.steps, nb - 1)), dma((sz.steps,)), dma((sz.steps, nb - 1)), dma((sz.steps,)),
        dma((sz.steps,)), dma((sz.steps,)), dma((sz.steps,)), dma((sz.steps,)),
        dma((nc - 1,)), dma((nc - 1,)), dma((nc - 1,)), dma((nc - 1,)), dma((nb - 1,)), dma((nb - 1,)),
        dma((nb - 1,)), dma((nb - 1,)), dma((nb - 1,)), dma((nb - 1,)),
        dma((nb - 1,)), dma((nb - 1,)), dma((nb,)), dma((nb,)), dma((2,)), dma((2,)),
        dma((nc - 1,)), dma((nc - 1,)), dma((nc - 1,)), dma((nc - 1,)), dma((nc - 1,)), dma((nc - 1,)),
    ]
    operands = [
        (args["watch_ids"].T, vmem), (args["search_ids"].T, vmem), (args["demo_ids"].T, vmem),
        (args["pos_ids"].reshape(1, -1), vmem), (args["neg_ids"].reshape(-1, 128), vmem),
        (args["demo_table"].T, vmem), (args["b_first"].reshape(1, -1), vmem),
        (args["b_second"].reshape(1, -1), vmem), (args["b_third"].reshape(1, -1), vmem),
        (args["valid_counts"], smem),
        (args["watch_table"], hbm), (args["search_table"], hbm), (args["out_table"], hbm),
        (args["w_first"], hbm), (args["w_second"], hbm), (args["w_third"], hbm),
    ]
    return pl.pallas_call(
        functools.partial(front_kernel, sz),
        out_shape=[o for o, _ in outs],
        in_specs=[s for _, s in operands],
        out_specs=[s for _, s in outs],
        scratch_shapes=scratch,
        compiler_params=pltpu.CompilerParams(
            collective_id=0, has_side_effects=True, vmem_limit_bytes=63 * 2**20
        ),
        name="front",
    )(*[o for o, _ in operands])


def back_kernel(
    sz, neg_rows, slots, user_in, loss_in, pos_in, counts, x_in, act1_in, act2_in, gu_in, gps_in, gpf_in, gx_in, buckets_in,
    watch_out, search_out, table_out, gw1_out, gw2_out, gw3_out, demo_out, gb1_out, gb2_out, gb3_out, user_out, loss_out,
    pos_table, x, act1, act2, gu, gps, gpf, gx, buckets, grads, ring,
    lines, low_rows, gw1, gw2, gw3, in_sem, ring_sem, line_sem, out_sem,
):
    width, cap, total, nb = sz.width, sz.cap, sz.total, sz.batch
    parts, nc, embed = sz.high_parts, sz.col, sz.embed
    depth = ring.shape[0]
    names = [
        (gx_in, gx), (pos_in, pos_table), (act2_in, act2), (gu_in, gu), (act1_in, act1), (gps_in, gps), (x_in, x), (gpf_in, gpf),
        (buckets_in, buckets),
    ]
    loads = [pltpu.make_async_copy(s, d, in_sem.at[i]) for i, (s, d) in enumerate(names)]
    loads[0].start()
    loads[1].start()
    user_out[...] = user_in[...]
    loss_out[...] = loss_in[...]

    def ring_load(n):
        return pltpu.make_async_copy(
            counts.at[lax.rem(n, 2), n // 2], ring.at[lax.rem(n, depth)], ring_sem.at[lax.rem(n, depth)]
        )

    early = depth - 2
    for n in range(early):
        ring_load(n).start()
    for load in loads[2:]:
        load.start()
    for n in range(early, depth):
        ring_load(n).start()
    loads[0].wait()

    own_grads = gx[...].reshape(total, gx.shape[2])[:, 0:128]
    grads[0] = own_grads.T
    grads[1] = flip_rows(own_grads.astype(F32)).astype(BF16).T

    def line_store(out, slot, hh):
        at = pl.ds(pl.multiple_of(hh * 4 * LOW, 4 * LOW), 4 * LOW)
        return pltpu.make_async_copy(lines.at[slot], out.at[:, at], line_sem.at[slot])

    def put(slot, found, factor):
        for i in range(4):
            lines[slot, :, i * LOW : (i + 1) * LOW] = found[i] * factor

    for k in range(sz.cap_tiles):
        low = slots[k, 1:2, :].astype(BF16)
        hot = one_where(low == iota((LOW, CHUNK), 0).astype(BF16), BF16)
        low_rows[k * CHUNK : (k + 1) * CHUNK, :] = hot.T
    high = jnp.concatenate([slots[k, 0:1, :] for k in range(sz.cap_tiles)], axis=1).astype(BF16)
    loads[1].wait()

    def scatter(n, _):
        found = scattered(n, high, neg_rows[...], low_rows[...])
        for j in range(2):

            @pl.when(n >= 1)
            def _():
                line_store(table_out, 4 + j, (n - 1) * 2 + j).wait()

            rows = [found[(j * 4 + i) * width : (j * 4 + i + 1) * width] for i in range(4)]
            rows = [rows[i] + pos_table[n * 2 + j, :, i * LOW : (i + 1) * LOW] for i in range(4)]
            put(4 + j, rows, 1.0)
            line_store(table_out, 4 + j, n * 2 + j).start()
        return 0

    lax.fori_loop(0, parts // 2, scatter, 0)
    def bags(hh, _):
        for table, out in enumerate((watch_out, search_out)):
            n = hh * 2 + table
            slot = table * 2 + lax.rem(hh, 2)
            ring_load(n).wait()
            found = [
                dot_as(grads[i % 2, table * width : (table + 1) * width, :], ring[lax.rem(n, depth), i], 1, 0)
                for i in range(4)
            ]

            @pl.when(n + depth < 2 * parts)
            def _():
                ring_load(n + depth).start()

            @pl.when(hh >= 2)
            def _():
                line_store(out, slot, hh - 2).wait()

            put(slot, found, 1.0 / sz.bag)
            line_store(out, slot, hh).start()
        return 0

    lax.fori_loop(0, parts // 2, bags, 0)

    for load in loads[2:]:
        load.wait()
    gu_rows = gu[...].reshape(total, embed)
    second = gps[...].reshape(total, gps.shape[2])
    first = gpf[...].reshape(total, gpf.shape[2])
    demo_grad = gx[...].reshape(total, 256)[:, 128:]
    gw3[...] = dot_as(act2[...], gu_rows, 0, 0)
    gw2[...] = dot_as(act1[...], second, 0, 0)
    gw1[...] = dot_as(x[...], first, 0, 0)
    stores = [(gw3, gw3_out), (gw2, gw2_out)]
    for i in range(nc):
        at = x_place(i)
        stores.append((gw1.at[pl.ds(at, width)], gw1_out.at[pl.ds(i * width, width)]))
        stores.append((gw1.at[pl.ds(at + width, width)], gw1_out.at[pl.ds(embed + i * width, width)]))
    stores.append((gw1.at[pl.ds(nc * 128, sz.demo_width)], gw1_out.at[pl.ds(2 * embed, sz.demo_width)]))
    stores = [pltpu.make_async_copy(s, d, out_sem.at[i]) for i, (s, d) in enumerate(stores)]
    for store in stores:
        store.start()
    demo = dot_as(buckets[...], demo_grad, 1, 0)
    demo_out[...] = demo.T[0 : sz.demo_width, :]
    gb1_out[...] = jnp.sum(first.astype(F32), axis=0, keepdims=True)
    gb2_out[...] = jnp.sum(second.astype(F32), axis=0, keepdims=True)
    gb3_out[...] = jnp.sum(gu_rows.astype(F32), axis=0, keepdims=True)

    lax.fori_loop(parts // 2, parts, bags, 0)

    for table, out in enumerate((watch_out, search_out)):
        for hh in (parts - 2, parts - 1):
            line_store(out, table * 2 + hh % 2, hh).wait()
    for j in range(2):
        line_store(table_out, 4 + j, parts - 2 + j).wait()
    for store in stores:
        store.wait()


def back(sz, args, kept):
    vmem = pl.BlockSpec(memory_space=pltpu.VMEM)
    hbm = pl.BlockSpec(memory_space=pl.ANY)
    total, nb = sz.total, sz.batch
    first, second = args["w_second"].shape
    embed, buckets = sz.embed, args["demo_table"].shape[0]
    dma = pltpu.SemaphoreType.DMA

    def shape(dims, kind=F32):
        return jax.ShapeDtypeStruct(dims, kind)

    table = shape((sz.width, sz.vocab))
    outs = [(table, hbm)] * 3 + [
        (shape((args["w_first"].shape)), hbm), (shape((first, second)), hbm), (shape((second, embed)), hbm),
        (shape((sz.demo_width, buckets)), vmem), (shape((1, first)), vmem), (shape((1, second)), vmem),
        (shape((1, embed)), vmem), (shape((sz.quarter, embed), BF16), vmem), (shape((1, 1)), vmem),
    ]
    slots = sz.cap
    return pl.pallas_call(
        functools.partial(back_kernel, sz),
        out_shape=[o for o, _ in outs],
        in_specs=[vmem] * 4 + [hbm] * 10,
        out_specs=[s for _, s in outs],
        scratch_shapes=[
            pltpu.VMEM((sz.high_parts, sz.width, 4 * LOW), F32),
            pltpu.VMEM((total, sz.x_width), BF16), pltpu.VMEM((total, first), BF16),
            pltpu.VMEM((total, second), BF16), pltpu.VMEM((nb, sz.rows, embed), BF16),
            pltpu.VMEM((nb, sz.rows, second), BF16), pltpu.VMEM((nb, sz.rows, first), BF16),
            pltpu.VMEM((nb, sz.rows, 256), BF16), pltpu.VMEM((buckets, total), BF16),
            pltpu.VMEM((2, 128, total), BF16), pltpu.VMEM((8, 4, total, LOW), BF16),
            pltpu.VMEM((6, sz.width, 4 * LOW), F32), pltpu.VMEM((slots, LOW), BF16),
            pltpu.VMEM((sz.x_width, first), F32), pltpu.VMEM((first, second), F32),
            pltpu.VMEM((second, embed), F32),
            dma((9,)), dma((8,)), dma((6,)), dma((3 + 2 * sz.col,)),
        ],
        compiler_params=pltpu.CompilerParams(vmem_limit_bytes=62 * 2**20),
        name="back",
    )(*kept)


def fast_device(sz, *inputs):
    names = (
        "watch_ids", "search_ids", "demo_ids", "pos_ids", "neg_ids", "valid_counts", "watch_table",
        "search_table", "demo_table", "out_table", "w_first", "b_first", "w_second", "b_second",
        "w_third", "b_third",
    )
    args = dict(zip(names, inputs))
    (
        counts, x, act1, act2, gu, gps, gpf, gx, buckets, neg_rows, pos_table, slots, user_vecs, loss, fits,
    ) = front(sz, args)

    def finish(*operands):
        kept = (neg_rows, slots, user_vecs, loss, pos_table, counts, x, act1, act2, gu, gps, gpf, gx, buckets)
        watch, search, table, gw1, gw2, gw3, demo, gb1, gb2, gb3, user, mean = back(sz, args, kept)
        return (
            user, mean.reshape(()), watch, search, table, demo.T, gw1, gb1.reshape(-1),
            gw2, gb2.reshape(-1), gw3, gb3.reshape(-1),
        )

    def general(*operands):
        return per_device(RingCollectives(), *operands)

    return lax.cond(fits.reshape(()) > 0, finish, general, *inputs)


def fast_sizes(mesh, shapes):
    watch, demo, negs, table, first = shapes
    batch, col = mesh.shape["batch"], mesh.shape["col"]
    rows, width, vocab = watch[0] // batch, table[0] // col, table[1] // batch
    demo_width = first[0] - 2 * table[0]
    sz = Sizes(batch, col, rows, watch[1], width, vocab, negs[0], table[0], demo_width)
    good = (
        batch == 8 and col == 4 and rows == 128 and watch[1] <= BAG_PAD and width == 64
        and vocab == 32 * LOW and table[1] <= 65536 and demo[1] <= 4 and demo_width <= 128
        and negs[0] % 128 == 0 and negs[0] <= 256 * CHUNK
    )
    return sz if good else None


def solution(mesh):
    in_specs = (
        P("batch", None),
        P("batch", None),
        P("batch", None),
        P("batch"),
        P(),
        P("batch"),
        P("col", "batch"),
        P("col", "batch"),
        P(),
        P("col", "batch"),
        P(),
        P(),
        P(),
        P(),
        P(),
        P(),
    )
    out_specs = (
        P(("batch", "col"), None),
        P(),
        P("col", "batch"),
        P("col", "batch"),
        P("col", "batch"),
        P(),
        P(),
        P(),
        P(),
        P(),
        P(),
        P(),
    )
    def whole(*inputs):
        shapes = [inputs[i].shape for i in (0, 2, 4, 6, 10)]
        sz = fast_sizes(mesh, shapes)
        if sz is None:
            body = functools.partial(per_device, Collectives())
        else:
            body = functools.partial(fast_device, sz)
        return jax.shard_map(
            body, mesh=mesh, in_specs=in_specs, out_specs=out_specs, check_vma=False
        )(*inputs)

    return whole
```

```python
import functools
import math

import jax
import jax.numpy as jnp
from jax import lax
from jax.experimental import pallas as pl
from jax.experimental.pallas import tpu as pltpu
from jax.sharding import PartitionSpec as P


def contract_rows(left, right):
    return lax.dot_general(
        left, right, (((0,), (0,)), ((), ())), preferred_element_type=jnp.float32
    )


def contract_cols(left, right):
    return lax.dot_general(
        left, right, (((1,), (1,)), ((), ())), preferred_element_type=jnp.float32
    )


def gelu_back(pre_value, grad_value):
    return jax.vjp(jax.nn.gelu, pre_value)[1](grad_value)[0]


class Collectives:
    def gather(self, value, name, axis):
        return lax.all_gather(value, name, axis=axis, tiled=True)

    def scatter_sum(self, value, name, axis):
        return lax.psum_scatter(value, name, scatter_dimension=axis, tiled=True)

    def total(self, values, name):
        return lax.psum(values, name)


class RingCollectives:
    def shift(self, value, name):
        size = lax.axis_size(name)
        return lax.ppermute(value, name, [(i, (i + 1) % size) for i in range(size)])

    def stack(self, value, name):
        size, me = lax.axis_size(name), lax.axis_index(name)
        held = [value]
        for _ in range(size - 1):
            held.append(self.shift(held[-1], name))
        return jnp.take(jnp.stack(held), (me - jnp.arange(size)) % size, axis=0)

    def gather(self, value, name, axis):
        parts = self.stack(value, name)
        return jnp.concatenate([parts[i] for i in range(parts.shape[0])], axis=axis)

    def ring_sum(self, parts, name):
        size, me = lax.axis_size(name), lax.axis_index(name)
        held = jnp.take(parts, (me - 1) % size, axis=0)
        for step in range(1, size):
            held = self.shift(held, name) + jnp.take(parts, (me - 1 - step) % size, axis=0)
        return held

    def scatter_sum(self, value, name, axis):
        size = lax.axis_size(name)
        return self.ring_sum(jnp.stack(jnp.split(value, size, axis=axis)), name)

    def total(self, values, name):
        size = lax.axis_size(name)
        flat = jnp.concatenate([v.reshape(-1) for v in values])
        length = -(-flat.shape[0] // (size * 128)) * 128
        parts = jnp.pad(flat, (0, size * length - flat.shape[0])).reshape(size, length)
        whole = self.stack(self.ring_sum(parts, name), name).reshape(-1)
        out, at = [], 0
        for v in values:
            out.append(whole[at : at + v.size].reshape(v.shape))
            at += v.size
        return tuple(out)


def per_device(
    comm,
    watch_ids,
    search_ids,
    demo_ids,
    pos_ids,
    neg_ids,
    valid_counts,
    watch_table,
    search_table,
    demo_table,
    out_table,
    w_first,
    b_first,
    w_second,
    b_second,
    w_third,
    b_third,
):
    row_count = watch_ids.shape[0]
    bag_size = watch_ids.shape[1]
    col_width = watch_table.shape[0]
    vocab_rows = watch_table.shape[1]
    embed_width = col_width * lax.axis_size("col")
    offset = lax.axis_index("batch") * vocab_rows
    col_slot = lax.axis_index("col")
    quarter = row_count // lax.axis_size("col")
    low_width = math.gcd(vocab_rows, 128)
    high_width = vocab_rows // low_width

    def owned(id_values):
        local_ids = id_values - offset
        return jnp.where((local_ids >= 0) & (local_ids < vocab_rows), local_ids, vocab_rows)

    def bag_counts(id_block):
        local_ids = owned(id_block)
        high_hot = (
            local_ids[:, :, None] // low_width == jnp.arange(high_width)[None, None, :]
        ).astype(jnp.bfloat16)
        low_hot = (
            local_ids[:, :, None] % low_width == jnp.arange(low_width)[None, None, :]
        ).astype(jnp.bfloat16)
        counted = jnp.einsum("rbh,rbl->rhl", high_hot, low_hot, preferred_element_type=jnp.bfloat16)
        return counted.reshape(id_block.shape[0], vocab_rows)

    def single_hot(id_block):
        return (owned(id_block)[:, None] == jnp.arange(vocab_rows)[None, :]).astype(jnp.bfloat16)

    zero_col = jnp.zeros((col_width, 1), jnp.bfloat16)
    padded_out = jnp.concatenate([out_table, zero_col], axis=1)
    all_watch, all_search, all_pos = (
        comm.gather(watch_ids, "batch", 0),
        comm.gather(search_ids, "batch", 0),
        comm.gather(pos_ids, "batch", 0),
    )
    total_rows = all_watch.shape[0]
    block_rows = min(1024, total_rows)
    block_count = total_rows // block_rows
    neg_local = owned(neg_ids)
    neg_part = jnp.take(padded_out, neg_local, axis=1).astype(jnp.float32)

    def flatten_blocks(stacked):
        return stacked.transpose(1, 0, 2).reshape(col_width, total_rows)

    def bag_block(inputs_block):
        watch_block, search_block, pos_block = inputs_block
        watch_part = contract_cols(watch_table, bag_counts(watch_block))
        search_part = contract_cols(search_table, bag_counts(search_block))
        pos_part = contract_cols(out_table, single_hot(pos_block))
        return (watch_part, search_part, pos_part)

    id_blocks = (
        all_watch.reshape(block_count, block_rows, bag_size),
        all_search.reshape(block_count, block_rows, bag_size),
        all_pos.reshape(block_count, block_rows),
    )
    watch_parts, search_parts, pos_parts = lax.map(bag_block, id_blocks)
    watch_sum, search_sum, pos_rows = (
        comm.scatter_sum(flatten_blocks(watch_parts), "batch", 1),
        comm.scatter_sum(flatten_blocks(search_parts), "batch", 1),
        comm.scatter_sum(flatten_blocks(pos_parts), "batch", 1),
    )
    neg_rows, valid_total = comm.total(
        (neg_part, jnp.sum(valid_counts).astype(jnp.float32)), "batch"
    )
    pooled_watch = (watch_sum / bag_size).astype(jnp.bfloat16)
    pooled_search = (search_sum / bag_size).astype(jnp.bfloat16)
    pos_bf = pos_rows.astype(jnp.bfloat16)
    neg_bf = neg_rows.astype(jnp.bfloat16)
    count_here = valid_counts[0]
    full_watch, full_search, full_pos, full_neg = (
        comm.gather(pooled_watch, "col", 0),
        comm.gather(pooled_search, "col", 0),
        comm.gather(pos_bf, "col", 0),
        comm.gather(neg_bf, "col", 0),
    )
    watch_rows = full_watch.T
    search_rows = full_search.T
    pos_full = full_pos.T
    live_rows = jnp.arange(row_count) < count_here
    weight = jnp.where(live_rows, 1.0 / valid_total, 0.0)
    buckets = demo_table.shape[0]
    bucket_counts = jnp.sum(
        (demo_ids[:, :, None] == jnp.arange(buckets)[None, None, :]).astype(jnp.float32), axis=1
    ).astype(jnp.bfloat16)
    demo_vec = jnp.dot(bucket_counts, demo_table, preferred_element_type=jnp.float32)
    joined = jnp.concatenate([watch_rows, search_rows, demo_vec.astype(jnp.bfloat16)], axis=1)
    pre_first = jnp.dot(joined, w_first, preferred_element_type=jnp.float32) + b_first
    act_first = jax.nn.gelu(pre_first).astype(jnp.bfloat16)
    pre_second = jnp.dot(act_first, w_second, preferred_element_type=jnp.float32) + b_second
    act_second = jax.nn.gelu(pre_second).astype(jnp.bfloat16)
    user_block = (
        jnp.dot(act_second, w_third, preferred_element_type=jnp.float32) + b_third
    ).astype(jnp.bfloat16)
    neg_logits = jnp.dot(user_block, full_neg, preferred_element_type=jnp.float32)
    pos_logit = jnp.sum(user_block.astype(jnp.float32) * pos_full.astype(jnp.float32), axis=1)
    row_peak = jnp.maximum(jnp.max(neg_logits, axis=1), pos_logit)
    exp_neg = jnp.exp(neg_logits - row_peak[:, None])
    exp_pos = jnp.exp(pos_logit - row_peak)
    row_total = jnp.sum(exp_neg, axis=1) + exp_pos
    lse = row_peak + jnp.log(row_total)
    loss_here = jnp.sum(weight * (lse - pos_logit))
    grad_neg = (weight[:, None] * exp_neg / row_total[:, None]).astype(jnp.bfloat16)
    grad_pos = (weight * (exp_pos / row_total - 1.0)).astype(jnp.bfloat16)
    grad_user = (
        contract_cols(grad_neg, full_neg)
        + grad_pos.astype(jnp.float32)[:, None] * pos_full.astype(jnp.float32)
    ).astype(jnp.bfloat16)
    neg_row_grad = contract_rows(user_block, grad_neg)
    pos_row_grad = (grad_pos.astype(jnp.float32)[:, None] * user_block.astype(jnp.float32)).astype(
        jnp.bfloat16
    )
    grad_w_third = contract_rows(act_second, grad_user)
    grad_b_third = jnp.sum(grad_user.astype(jnp.float32), axis=0)
    grad_pre_second = gelu_back(pre_second, contract_cols(grad_user, w_third)).astype(jnp.bfloat16)
    grad_w_second = contract_rows(act_first, grad_pre_second)
    grad_b_second = jnp.sum(grad_pre_second.astype(jnp.float32), axis=0)
    grad_pre_first = gelu_back(pre_first, contract_cols(grad_pre_second, w_second)).astype(
        jnp.bfloat16
    )
    grad_w_first = contract_rows(joined, grad_pre_first)
    grad_b_first = jnp.sum(grad_pre_first.astype(jnp.float32), axis=0)
    grad_joined = contract_cols(grad_pre_first, w_first).astype(jnp.bfloat16)
    grad_pw = grad_joined[:, :embed_width]
    grad_ps = grad_joined[:, embed_width : 2 * embed_width]
    grad_demo = contract_rows(bucket_counts, grad_joined[:, 2 * embed_width :])
    col_start = col_slot * col_width
    own_pw = lax.dynamic_slice_in_dim(grad_pw, col_start, col_width, 1).T
    own_ps = lax.dynamic_slice_in_dim(grad_ps, col_start, col_width, 1).T
    own_pos = lax.dynamic_slice_in_dim(pos_row_grad, col_start, col_width, 1).T
    user_vecs = lax.dynamic_slice_in_dim(user_block, col_slot * quarter, quarter, 0)
    all_pw, all_ps, all_dpos = (
        comm.gather(own_pw, "batch", 1),
        comm.gather(own_ps, "batch", 1),
        comm.gather(own_pos, "batch", 1),
    )
    neg_own = lax.dynamic_slice_in_dim(neg_row_grad, col_slot * col_width, col_width, 0)
    sums_out = comm.total(
        (
            grad_w_first,
            grad_b_first,
            grad_w_second,
            grad_b_second,
            grad_w_third,
            grad_b_third,
            grad_demo,
            neg_own,
            loss_here,
        ),
        "batch",
    )
    neg_sum_own = sums_out[7]

    def split_blocks(columns):
        return columns.reshape(col_width, block_count, block_rows).transpose(1, 0, 2)

    def grad_block(running, inputs_block):
        watch_block, search_block, pos_block, block_pw, block_ps, block_pos = inputs_block
        new_watch = running[0] + jnp.dot(
            block_pw, bag_counts(watch_block), preferred_element_type=jnp.float32
        )
        new_search = running[1] + jnp.dot(
            block_ps, bag_counts(search_block), preferred_element_type=jnp.float32
        )
        new_out = running[2] + jnp.dot(
            block_pos, single_hot(pos_block), preferred_element_type=jnp.float32
        )
        return ((new_watch, new_search, new_out), None)

    zeros_table = jnp.zeros((col_width, vocab_rows), jnp.float32)
    (table_watch, table_search, table_out), _ = lax.scan(
        grad_block,
        (zeros_table, zeros_table, zeros_table),
        id_blocks + (split_blocks(all_pw), split_blocks(all_ps), split_blocks(all_dpos)),
    )
    neg_added = (
        jnp.zeros((col_width, vocab_rows + 1), jnp.float32).at[:, neg_local].add(neg_sum_own)
    )
    table_out = table_out + neg_added[:, :vocab_rows]
    return (
        user_vecs,
        sums_out[8],
        table_watch / bag_size,
        table_search / bag_size,
        table_out,
        sums_out[6],
        sums_out[0],
        sums_out[1],
        sums_out[2],
        sums_out[3],
        sums_out[4],
        sums_out[5],
    )


F32, BF16, FP8, I32 = jnp.float32, jnp.bfloat16, jnp.float8_e4m3fn, jnp.int32
MESH = pl.DeviceIdType.MESH
LOW = 256
ROWS_IN_GROUP = 4
BAG_PAD = 64
CHUNK = 256
NEG_FLOOR = -1e30


def dot_as(left, right, left_dim, right_dim):
    return lax.dot_general(
        left, right, (((left_dim,), (right_dim,)), ((), ())), preferred_element_type=F32
    )


def iota(shape, dim):
    return lax.broadcasted_iota(I32, shape, dim)


def one_where(mask, kind):
    return jnp.where(mask, jnp.ones((), BF16), jnp.zeros((), BF16)).astype(kind)


def slot_cap(neg_count, batch):
    mean = neg_count / batch
    return int(math.ceil((mean + 4.5 * math.sqrt(mean)) / CHUNK)) * CHUNK


def gelu(pre):
    bent = jnp.tanh(math.sqrt(2.0 / math.pi) * (pre + 0.044715 * (pre * pre * pre)))
    return 0.5 * pre * (1.0 + bent)


def gelu_slope(pre):
    inner_scale = math.sqrt(2.0 / math.pi)
    square = pre * pre
    bent = jnp.tanh(inner_scale * (pre + 0.044715 * (square * pre)))
    return 0.5 * (1.0 + bent) + 0.5 * pre * (1.0 - bent * bent) * (
        inner_scale * (1.0 + 3.0 * 0.044715 * square)
    )


def flip_rows(value):
    rows, lanes = value.shape
    return pltpu.roll(value.reshape(rows // 8, 8, lanes), 4, 1).reshape(rows, lanes)


def x_place(col):
    return ((col % 2) * 2 + col // 2) * 128


def scattered(n, high, values, low_rows):
    left = []
    for i in range(8):
        at = (n * 8 + i).astype(F32).astype(BF16)
        left.append(jnp.where(high == at, values, jnp.zeros((), BF16)))
    return dot_as(jnp.concatenate(left, axis=0), low_rows, 1, 0)


class Sizes:
    def __init__(self, batch, col, rows, bag, width, vocab, negs, embed, demo_width):
        self.batch, self.col, self.rows, self.bag = batch, col, rows, bag
        self.width, self.vocab, self.negs, self.embed = width, vocab, negs, embed
        self.demo_width = demo_width
        self.total = batch * rows
        self.quarter = rows // col
        self.users = batch * self.quarter
        self.groups = rows // ROWS_IN_GROUP
        self.high = vocab // LOW
        self.high_parts = self.high // 4
        self.cap = slot_cap(negs, batch)
        self.cap_tiles = self.cap // CHUNK
        self.tiles = self.cap_tiles + col
        self.neg_lines = -(-negs // (CHUNK * 8)) * 8
        self.steps = 4
        self.span = self.total // self.steps
        self.x_width = col * 128 + 128


def front_kernel(
    sz,
    watch_ids, search_ids, demo_ids, pos_ids, neg_ids, demo_table, b_first, b_second, b_third, valid_count,
    watch_table, search_table, out_table, w_first, w_second, w_third,
    counts_out, x_out, act1_out, act2_out, gu_out, gps_out, gpf_out, gx_out, buckets_out,
    neg_rows_out, pos_table_out, slots_out, user_out, loss_out, fits_out,
    tabs, tall, mix, w1_raw, w1, w1_own, w2, w3, turned, upright, lines_own, ids, side, neg_dest, neg_digits, counts, found_sums, sums, pieces, x,
    pre1, pre2, acts1, slopes1, acts2, slopes2, users, buckets, slots, picked, neg_all, pos_all, e_cols,
    e_rows, low_rows, pos_table, probs, stats, factors, home, g_send, g_recv, gu, gps, gpf, gx, rg_send, rg_recv, gp_all, loss_all,
    local_sem, out_sem, down_sem, count_sem, ids_s, ids_r, sd_s, sd_r, dx_s, dx_r, rs_s, rs_r, ag_s, ag_r, xx_s, xx_r, co_s, co_r,
    ne_s, ne_r, pe_s, pe_r, ho_s, ho_r, st_s, st_r, gs_s, gs_r, ga_s, ga_r, gx_s, gx_r, gc_s, gc_r,
    rg_s, rg_r, gp_s, gp_r, lo_s, lo_r,
):
    b, c = lax.axis_index("batch"), lax.axis_index("col")
    nb, nc = sz.batch, sz.col
    offset = b * sz.vocab
    cap, width, embed = sz.cap, sz.width, sz.embed
    cx = lax.rem(c + 2, nc)
    ck = c + 1 - 2 * lax.rem(c, 2)
    ckx = lax.rem(ck + 2, nc)

    def batch_peer(i):
        return lax.rem(b + i, nb)

    def batch_from(i):
        return lax.rem(b + nb - i, nb)

    def col_peer(i):
        return lax.rem(c + i, nc)

    def col_from(i):
        return lax.rem(c + nc - i, nc)

    def send(src, dst, ssem, rsem, to):
        return pltpu.make_async_remote_copy(
            src_ref=src, dst_ref=dst, send_sem=ssem, recv_sem=rsem,
            device_id=to, device_id_type=MESH,
        )

    barrier = pltpu.get_barrier_semaphore()
    for i in range(nb):
        for k in range(nc):
            if i + k > 0:
                pl.semaphore_signal(
                    barrier, inc=1, device_id=(batch_peer(i), col_peer(k)), device_id_type=MESH
                )

    loads = [
        (watch_table, tabs.at[0]), (search_table, tabs.at[1]), (out_table, tabs.at[2]),
        (w_first, w1_raw), (w_second, w2), (w_third, w3),
    ]
    loads = [pltpu.make_async_copy(s, d, local_sem.at[i]) for i, (s, d) in enumerate(loads)]
    for load in loads:
        load.start()

    turned[...] = jnp.zeros((BAG_PAD, 128), I32)
    turned[0 : sz.bag, :] = (watch_ids[...] & 0xFFFF) | (search_ids[...] << 16)
    upright[...] = turned[...].T
    for r4 in range(ROWS_IN_GROUP):
        lines_own[:, r4 * BAG_PAD : (r4 + 1) * BAG_PAD] = upright[
            pl.ds(r4, sz.groups, stride=ROWS_IN_GROUP), :
        ]
    share = sz.groups // nc

    def share_of(col):
        return pl.ds(pl.multiple_of(col * share, share), share)

    ids[b] = lines_own[...]
    side[b] = jnp.zeros((8, 128), I32)
    side[b, 0:1, :] = pos_ids[...]
    side[b, 1:2, :] = jnp.full((1, 128), valid_count[0], I32)
    side[b, 2 : 2 + demo_ids.shape[0], :] = demo_ids[...]

    pl.semaphore_wait(barrier, nb * nc - 1)
    last_sends = []
    for i in range(1, nb):
        for k in range(nc):
            place = ids.at[b, share_of(c)]
            copy = send(place, place, ids_s.at[k, i - 1], ids_r.at[k], (batch_peer(i), col_peer(k)))
            copy.start()
            last_sends.append(copy)

    for i in range(1, nb):
        copy = send(side.at[b], side.at[b], sd_s.at[i - 1], sd_r.at[i - 1], (batch_peer(i), c))
        copy.start()
        last_sends.append(copy)

    negs = neg_ids[...]
    lines = sz.neg_lines
    missing = 2 * lines - negs.shape[0]
    second = jnp.concatenate([negs[lines:], jnp.full((missing, 128), -1, I32)], axis=0)
    negs = jnp.concatenate([negs[:lines], second], axis=1)
    neg_local = negs - offset
    own = (neg_local >= 0) & (neg_local < sz.vocab)
    own_bf = one_where(own, BF16)
    upper = one_where(iota((CHUNK, CHUNK), 0) < iota((CHUNK, CHUNK), 1), BF16)
    before = dot_as(own_bf, upper, 1, 0)
    in_row = dot_as(own_bf, jnp.ones((CHUNK, CHUNK), BF16), 1, 0)
    lower = one_where(iota((lines, lines), 1) < iota((lines, lines), 0), BF16)
    rows_before = dot_as(lower, in_row.astype(BF16), 1, 0)
    neg_dest[...] = jnp.where(own, before + rows_before, -1.0)
    owned_count = dot_as(jnp.ones((8, lines), BF16), in_row.astype(BF16), 1, 0)
    most = jnp.zeros((1, 1), F32)
    for shard in range(nb):
        part = negs - shard * sz.vocab
        hits = jnp.where((part >= 0) & (part < sz.vocab), 1.0, 0.0)
        most = jnp.maximum(most, jnp.sum(jnp.sum(hits, axis=1, keepdims=True), axis=0, keepdims=True))
    fits_out[...] = jnp.where(most <= float(cap), 1, 0)
    for digit in range(4):
        neg_digits[digit] = ((neg_local >> (4 * digit)) & 15).astype(F32)

    def compact(k, total):
        place = neg_dest[pl.ds(k, 1), :]
        hot = one_where(place == iota((cap, CHUNK), 0).astype(F32), FP8)
        line = iota((32, CHUNK), 0)
        value = jnp.where(line == 4, 1.0, 0.0)
        for digit in range(4):
            value = jnp.where(line == digit, neg_digits[digit, pl.ds(k, 1), :], value)
        return total + dot_as(value.astype(FP8), hot, 1, 1)

    slot = lax.fori_loop(0, lines, compact, jnp.zeros((32, cap), F32))
    neg_low = slot[0:1] + 16.0 * slot[1:2]
    neg_high = jnp.where(slot[4:5] > 0.5, slot[2:3] + 16.0 * slot[3:4], -1.0)
    slots[...] = jnp.zeros((sz.tiles, 8, CHUNK), F32)
    for k in range(sz.cap_tiles):
        slots[k, 0:1, :] = neg_high[:, k * CHUNK : (k + 1) * CHUNK]
        slots[k, 1:2, :] = neg_low[:, k * CHUNK : (k + 1) * CHUNK]

    for t in range(2):
        loads[t].wait()

    def turn(n, _):
        t, hh = n // sz.high_parts, n % sz.high_parts
        base = pl.multiple_of(hh * 4 * LOW, 4 * LOW)
        stack = jnp.concatenate([tabs[t, :, pl.ds(base + i * LOW, LOW)] for i in range(4)], axis=0)
        mix[t, pl.ds(pl.multiple_of(hh * LOW, LOW), LOW), :] = stack.T
        return 0

    lax.fori_loop(0, 2 * sz.high_parts, turn, 0)

    loads[2].wait()

    def stack_up(hh, _):
        for i in range(4):
            tall[pl.ds(pl.multiple_of((hh * 4 + i) * width, width), width), :] = tabs[
                2, :, pl.ds(pl.multiple_of((hh * 4 + i) * LOW, LOW), LOW)
            ]
        return 0

    lax.fori_loop(0, sz.high_parts, stack_up, 0)

    def pick_tile(k, _):
        high, low = slots[k, 0:1, :], slots[k, 1:2, :]
        low_hot = one_where(low.astype(BF16) == iota((LOW, CHUNK), 0).astype(BF16), BF16)
        total = jnp.zeros((width, CHUNK), F32)
        for part in range(4):
            tall_rows = width * sz.high // 4
            got = dot_as(tall[part * tall_rows : (part + 1) * tall_rows, :], low_hot, 1, 0)
            for i in range(sz.high // 4):
                at = float(part * (sz.high // 4) + i)
                total = total + jnp.where(high == at, got[i * width : (i + 1) * width], 0.0)
        picked[k] = total.astype(BF16)
        return 0

    lax.fori_loop(0, sz.cap_tiles, pick_tile, 0)
    neg_part = picked.at[pl.ds(0, sz.cap_tiles)]
    for i in range(1, nc):
        copy = send(neg_part, neg_all.at[c], ne_s.at[i - 1], ne_r.at[i - 1], (b, col_peer(i)))
        copy.start()
        last_sends.append(copy)
    for k in range(sz.cap_tiles):
        neg_all[c, k] = picked[k]

    loads[3].wait()
    w1[nc * 128 :, :] = jnp.zeros((128, w1.shape[1]), BF16)
    for i in range(nc):
        at = x_place(i)
        w1[at : at + width, :] = w1_raw[i * width : (i + 1) * width, :]
        w1[at + width : at + 128, :] = w1_raw[embed + i * width : embed + (i + 1) * width, :]
    w1[nc * 128 : nc * 128 + sz.demo_width, :] = w1_raw[2 * embed :, :]
    loads[4].wait()
    loads[5].wait()

    w1_own[...] = jnp.zeros(w1_own.shape, BF16)
    w1_own[0 : 2 * width, :] = w1[pl.ds(pl.multiple_of((lax.rem(c, 2) * 2 + c // 2) * 128, 128), 128), :]
    w1_own[2 * width : 2 * width + sz.demo_width, :] = w1_raw[2 * embed :, :]
    for k in range(nc):
        place = ids.at[pl.ds(0, nb - 1), share_of(col_from(k))]
        send(place, place, ids_s.at[k, 0], ids_r.at[k], (b, c)).wait_recv()

    users_shape = (nb, CHUNK)
    at_block = iota(users_shape, 1) // sz.quarter == iota(users_shape, 0)

    def demo_part():
        bucket_total = jnp.zeros((buckets.shape[0], sz.total), BF16)
        bucket_line = iota((buckets.shape[0], sz.total), 0).astype(BF16)
        for field in range(demo_ids.shape[0]):
            line = jnp.concatenate([side[j, 2 + field : 3 + field, :] for j in range(nb)], axis=1)
            bucket_total = bucket_total + one_where(line.astype(F32).astype(BF16) == bucket_line, BF16)
        buckets[...] = bucket_total
        demo_rows = demo_table[...].astype(F32).T.astype(BF16)
        x[:, nc * 128 :] = jnp.zeros((sz.total, 128), BF16)
        x[:, nc * 128 : nc * 128 + sz.demo_width] = dot_as(bucket_total, demo_rows, 0, 0).astype(BF16)

    def pos_part():
        for i in range(1, nb):
            place = side.at[batch_from(i)]
            send(place, place, sd_s.at[i - 1], sd_r.at[i - 1], (b, c)).wait_recv()
        all_pos = jnp.concatenate([side[j, 0:1, :] for j in range(nb)], axis=0)
        pos_local = all_pos - offset
        pos_owned = (pos_local >= 0) & (pos_local < sz.vocab)
        pos_pair = jnp.concatenate(
            [
                jnp.where(pos_owned, pos_local >> 8, 255).astype(F32),
                (pos_local & 255).astype(F32),
            ],
            axis=0,
        ).astype(BF16)
        for quarter in range(nc):
            shape = (128, CHUNK)
            pick = one_where(iota(shape, 0) == quarter * sz.quarter + iota(shape, 1) % sz.quarter, BF16)
            wide = dot_as(pos_pair, pick, 1, 0)
            high = jnp.sum(jnp.where(at_block, wide[0:nb], 0.0), axis=0, keepdims=True)
            low = jnp.sum(jnp.where(at_block, wide[nb : 2 * nb], 0.0), axis=0, keepdims=True)
            slots[sz.cap_tiles + quarter, 0:1, :] = jnp.where(high > 254.0, -1.0, high)
            slots[sz.cap_tiles + quarter, 1:2, :] = low
        slots_out[...] = slots[...]
        lax.fori_loop(sz.cap_tiles, sz.tiles, pick_tile, 0)
        pos_all[c] = picked[sz.cap_tiles + c]
        for i in range(1, nc):
            pos_send(i).start()

    def slot_rows():
        for i in range(1, nc):
            src = col_from(i)
            send(neg_all.at[src], neg_all.at[src], ne_s.at[i - 1], ne_r.at[i - 1], (b, c)).wait_recv()
            send(pos_all.at[src], pos_all.at[src], pe_s.at[i - 1], pe_r.at[i - 1], (b, c)).wait_recv()
        for i in range(nc):
            for k in range(sz.cap_tiles):
                e_cols[i * width : (i + 1) * width, k * CHUNK : (k + 1) * CHUNK] = neg_all[i, k]
            e_cols[i * width : (i + 1) * width, cap:] = pos_all[i]
        e_rows[...] = e_cols[...].T
        for i in range(1, nb):
            home_send(i).start()

    def home_send(i):
        to = batch_peer(i)
        rows = e_rows.at[pl.ds(pl.multiple_of(cap + to * sz.quarter, sz.quarter), sz.quarter)]
        return send(rows, home.at[i - 1], ho_s.at[i - 1], ho_r.at[i - 1], (to, c))

    def pos_send(i):
        to = col_peer(i)
        return send(picked.at[sz.cap_tiles + to], pos_all.at[c], pe_s.at[i - 1], pe_r.at[i - 1], (b, to))

    span = sz.span
    piece = span // nb
    lane_mod = iota((16, CHUNK), 1) % BAG_PAD
    lane_r4 = iota((16, CHUNK), 1) // BAG_PAD
    odd_group = iota((16, CHUNK), 0) & 1
    blocks = span // sz.rows
    parts_in_block = sz.groups // 16

    def count_copy(t, table, slot_at):
        rows = pl.ds(pl.multiple_of(t * span, span), span)
        return pltpu.make_async_copy(
            counts.at[table, slot_at], counts_out.at[table, :, :, rows], count_sem.at[table, slot_at]
        )

    def bag_table(t, table, between):
        slot_at = lax.rem(t, 2)

        @pl.when(t >= 2)
        def _():
            count_copy(t - 2, table, slot_at).wait()

        code_line = iota((4 * sz.high, CHUNK), 0).astype(BF16)
        low_line = iota((LOW, CHUNK), 0).astype(BF16)

        def groups_of(q, _):
            block = t * blocks + q // parts_in_block
            word = ids[block, pl.ds(pl.multiple_of((q % parts_in_block) * 16, 16), 16), :]
            value = lax.shift_right_logical(word, 16 * table) & 0xFFFF
            local = value - offset
            mine = (local >= 0) & (local < sz.vocab) & (lane_mod < sz.bag)
            code = jnp.where(mine, ((local >> 8) ^ odd_group) * 4 + lane_r4, -1).astype(F32).astype(BF16)
            low = (local & 255).astype(F32).astype(BF16)
            low_half = iota((sz.high // 2, 8, LOW), 1) < 4
            for quad in range(4):
                pairs = []
                for pair in range(2):
                    found = []
                    for g in (quad * 4 + pair * 2, quad * 4 + pair * 2 + 1):
                        left = one_where(code[g : g + 1, :] == code_line, FP8)
                        right = one_where(low[g : g + 1, :] == low_line, FP8)
                        found.append(dot_as(left, right, 1, 1).reshape(sz.high // 2, 8, LOW))
                    even = jnp.where(low_half, found[0], found[1])
                    odd = jnp.where(low_half, found[1], found[0])
                    pairs.append((even, odd))
                line = pl.ds(pl.multiple_of(q * 64 + quad * 16, 16), 16)
                for part in range(sz.high):
                    both = [pairs[k][part % 2][part // 2] for k in range(2)]
                    counts[table, slot_at, part // 4, part % 4, line, :] = jnp.concatenate(
                        both, axis=0
                    ).astype(BF16)
            return 0

        lax.fori_loop(0, blocks * parts_in_block, groups_of, 0)
        count_copy(t, table, slot_at).start()
        between()
        left = jnp.concatenate(
            [counts[table, slot_at, hh].reshape(4 * span, LOW) for hh in range(sz.high_parts)], axis=1
        )
        total = dot_as(left, mix[table], 1, 0)
        left_side = iota((span, 128), 1) < width
        first = jnp.where(left_side, total[0:span, 0:128], flip_rows(total[span : 2 * span, 0:128]))
        second = jnp.where(left_side, total[2 * span : 3 * span, 128:], flip_rows(total[3 * span :, 128:]))
        both = first + second
        found_sums[table] = both + pltpu.roll(both, width, 1)

    def bag_sums(t):
        joined = jnp.where(iota((span, 128), 1) < width, found_sums[0], found_sums[1])
        sums[t] = joined.astype(BF16)
        for i in range(1, nb):
            to = batch_peer(i)
            send(
                sums.at[t, pl.ds(pl.multiple_of(to * piece, piece), piece)], pieces.at[t, i - 1],
                rs_s.at[t, i - 1], rs_r.at[t], (to, c),
            ).start()

    def lanes_of(col):
        return pl.ds(pl.multiple_of((lax.rem(col, 2) * 2 + col // 2) * 128, 128), 128)

    def x_at(t, col):
        return x.at[pl.ds(pl.multiple_of(t * span, span), span), lanes_of(col)]

    def x_pair(t, col):
        return x.at[
            pl.ds(pl.multiple_of(t * span, span), span),
            pl.ds(pl.multiple_of(lax.rem(col, 2) * 256, 256), 256),
        ]

    def x_piece(t, owner):
        return x.at[
            pl.ds(pl.multiple_of(t * span + owner * piece, piece), piece), lanes_of(c)
        ]

    def reduce_step(t, direct=False):
        send(pieces.at[t], pieces.at[t], rs_s.at[t, 0], rs_r.at[t], (b, c)).wait_recv()
        total = sums[t, pl.ds(pl.multiple_of(b * piece, piece), piece), :].astype(F32)
        for i in range(nb - 1):
            total = total + pieces[t, i].astype(F32)
        x[
            pl.ds(pl.multiple_of(t * span + b * piece, piece), piece), lanes_of(c)
        ] = (total / sz.bag).astype(BF16)
        for i in range(1, nb):
            send(x_piece(t, b), x_piece(t, b), ag_s.at[t, i - 1], ag_r.at[t], (batch_peer(i), c)).start()
        if direct:
            for i in range(nb):
                for k in range(1, nc):
                    direct_send(t, i, k).start()

    def direct_send(t, i, k):
        return send(
            x_piece(t, b), x_piece(t, b), dx_s.at[k - 1, i], dx_r.at[k - 1], (batch_peer(i), col_peer(k))
        )

    def direct_wait(t):
        send(pieces.at[t], pieces.at[t], ag_s.at[t, 0], ag_r.at[t], (b, c)).wait_recv()
        for k in range(1, nc):
            place = x_at(t, col_from(k))
            send(place, place, dx_s.at[k - 1, 0], dx_r.at[k - 1], (b, c)).wait_recv()

    def cross_step(t):
        send(pieces.at[t], pieces.at[t], ag_s.at[t, 0], ag_r.at[t], (b, c)).wait_recv()
        send(x_at(t, c), x_at(t, c), xx_s.at[t], xx_r.at[t], (b, cx)).start()

    def core_step(t):
        send(x_at(t, cx), x_at(t, cx), xx_s.at[t], xx_r.at[t], (b, cx)).wait_recv()
        send(x_pair(t, c), x_pair(t, c), co_s.at[t], co_r.at[t], (b, ck)).start()

    def full_step(t):
        send(x_pair(t, ck), x_pair(t, ck), co_s.at[t], co_r.at[t], (b, ck)).wait_recv()

    def tower(k):
        at = pl.ds(pl.multiple_of(k * span, span), span)
        pre = dot_as(x[at, :], w1[...], 1, 0) + b_first[...]
        pre1[at, :] = pre
        value = gelu(pre).astype(BF16)
        acts1[at, :] = value
        pre = dot_as(value, w2[...], 1, 0) + b_second[...]
        pre2[at, :] = pre
        value = gelu(pre).astype(BF16)
        acts2[at, :] = value
        users[at, :] = (dot_as(value, w3[...], 1, 0) + b_third[...]).astype(BF16)

    def tower_quarter():
        places = [
            pl.ds(pl.multiple_of(last * span + j * sz.rows + c * sz.quarter, sz.quarter), sz.quarter)
            for j in range(blocks)
        ]
        rows = jnp.concatenate([x[at, :] for at in places], axis=0)
        value = gelu(dot_as(rows, w1[...], 1, 0) + b_first[...]).astype(BF16)
        value = gelu(dot_as(value, w2[...], 1, 0) + b_second[...]).astype(BF16)
        found = (dot_as(value, w3[...], 1, 0) + b_third[...]).astype(BF16)
        for j, at in enumerate(places):
            users[at, :] = found[j * sz.quarter : (j + 1) * sz.quarter]

    def slopes(k):
        at = pl.ds(pl.multiple_of(k * span, span), span)
        slopes1[at, :] = gelu_slope(pre1[at, :]).astype(BF16)
        slopes2[at, :] = gelu_slope(pre2[at, :]).astype(BF16)

    bag_ticks = 2 * sz.steps
    last = sz.steps - 1

    def tick(n, _):
        half = n // 2
        odd = lax.rem(n, 2) == 1

        def between():
            @pl.when(odd & (n >= 3))
            def _():
                reduce_step((n - 3) // 2)

        @pl.when(n < bag_ticks)
        def _():
            bag_table(half, lax.rem(n, 2), between)

        @pl.when((n < bag_ticks) & odd)
        def _():
            bag_sums(half)

        @pl.when(n == bag_ticks)
        def _():
            pos_part()

        @pl.when(n == bag_ticks + 1)
        def _():
            demo_part()

        @pl.when(n == bag_ticks + 3)
        def _():
            slot_rows()

        @pl.when((~odd) & (n >= 6) & (n <= bag_ticks))
        def _():
            full_step((n - 6) // 2)

        done = jnp.where(n <= bag_ticks + 1, 0, jnp.where(n == bag_ticks + 2, 1, last))
        ready = jnp.where(
            n <= bag_ticks, 0, jnp.where(n == bag_ticks + 1, 1, last)
        )

        def some_tower(k, _):
            @pl.when(k == last - 1)
            def _():
                full_step(k)

            tower(k)
            return 0

        lax.fori_loop(done, ready, some_tower, 0)

        @pl.when((~odd) & (n >= 4) & (n <= bag_ticks))
        def _():
            cross_step((n - 4) // 2)

        @pl.when(n == bag_ticks)
        def _():
            reduce_step(last, direct=True)

        @pl.when(odd & (n >= 5) & (n <= bag_ticks + 1))
        def _():
            core_step((n - 5) // 2)

        return 0

    lax.fori_loop(0, bag_ticks + 4, tick, 0)
    direct_wait(last)
    tower_quarter()

    valid = jnp.concatenate([side[j, 1:2, :] for j in range(nb)], axis=0)
    valid_wide = jnp.concatenate([valid] * (sz.users // 128), axis=1).astype(F32)
    live_count = jnp.sum(jnp.where(at_block, valid_wide, 0.0), axis=0, keepdims=True)
    valid_total = jnp.sum(valid_wide, axis=0, keepdims=True)
    user_place = c * sz.quarter + iota((1, sz.users), 1) % sz.quarter
    weight = jnp.where(user_place.astype(F32) < live_count, 1.0 / valid_total, 0.0)

    user_out[...] = users[pl.ds(pl.multiple_of(b * sz.rows + c * sz.quarter, sz.quarter), sz.quarter), :]

    def users_of(quarter):
        return jnp.concatenate(
            [
                users[pl.ds(pl.multiple_of(j * sz.rows + quarter * sz.quarter, sz.quarter), sz.quarter), :]
                for j in range(nb)
            ],
            axis=0,
        )

    quarter_users = users_of(c)
    logits = dot_as(e_rows[...], quarter_users, 1, 1)
    neg_logits, pos_logits = logits[0:cap], logits[cap:]
    slot_ok = iota((cap, sz.users), 0).astype(F32) < owned_count[0:1, : sz.users]
    pos_here = slots[sz.cap_tiles + c, 0:1, :]
    pos_ok = (iota((sz.users, sz.users), 0) == iota((sz.users, sz.users), 1)) & (pos_here >= 0.0)
    neg_logits = jnp.where(slot_ok, neg_logits, NEG_FLOOR)
    pos_masked = jnp.where(pos_ok, pos_logits, NEG_FLOOR)
    peak = jnp.maximum(
        jnp.max(neg_logits, axis=0, keepdims=True), jnp.max(pos_masked, axis=0, keepdims=True)
    )
    bare = jnp.where(slot_ok, jnp.exp(neg_logits - peak), 0.0)
    mass = jnp.sum(bare, axis=0, keepdims=True) + jnp.sum(
        jnp.where(pos_ok, jnp.exp(pos_masked - peak), 0.0), axis=0, keepdims=True
    )
    pos_value = jnp.sum(jnp.where(pos_ok, pos_logits, 0.0), axis=0, keepdims=True)
    stats[b] = jnp.concatenate([peak, mass, pos_value, jnp.zeros((5, sz.users), F32)], axis=0)
    for i in range(1, nb):
        copy = send(stats.at[b], stats.at[b], st_s.at[i - 1], st_r.at[i - 1], (batch_peer(i), c))
        copy.start()
        last_sends.append(copy)

    probs[...] = bare.astype(BF16)
    grad_user = dot_as(probs[...], e_rows[0:cap, :], 0, 0)
    for j in range(nb):
        g_send[j] = grad_user[j * sz.quarter : (j + 1) * sz.quarter].astype(BF16)
    for i in range(1, nb):
        to = batch_peer(i)
        copy = send(g_send.at[to], g_recv.at[i - 1], gs_s.at[i - 1], gs_r.at[i - 1], (to, c))
        copy.start()
        last_sends.append(copy)

    def some_slopes(k, _):
        slopes(k)
        return 0

    lax.fori_loop(0, last, some_slopes, 0)
    for i in range(1, nb):
        src = batch_from(i)
        send(stats.at[src], stats.at[src], st_s.at[i - 1], st_r.at[i - 1], (b, c)).wait_recv()
    order = [batch_from(i) for i in range(nb)]
    peaks = [stats[j, 0:1, :] for j in range(nb)]
    top = peaks[0]
    for j in range(1, nb):
        top = jnp.maximum(top, peaks[j])
    full_mass = jnp.zeros((1, sz.users), F32)
    pos_logit = jnp.zeros((1, sz.users), F32)
    for j in range(nb):
        full_mass = full_mass + stats[j, 1:2, :] * jnp.exp(peaks[j] - top)
        pos_logit = pos_logit + stats[j, 2:3, :]
    lse = top + jnp.log(full_mass)
    loss_part = jnp.sum(weight * (lse - pos_logit), axis=1, keepdims=True)
    scale = weight / full_mass
    pos_grad = weight * (jnp.exp(pos_logit - top) / full_mass - 1.0)
    lines_of = [jnp.exp(stats[j, 0:1, :] - top) * scale for j in order]
    lines_of += [pos_grad, jnp.zeros((16 - nb - 1, sz.users), F32)]
    factors[...] = jnp.concatenate(lines_of, axis=0).T
    probs[...] = jnp.where(slot_ok, jnp.exp(neg_logits - top) * scale, 0.0).astype(BF16)
    gp_all[c] = jnp.broadcast_to(jnp.where(pos_here >= 0.0, pos_grad, 0.0), (8, sz.users))
    loss_all[c] = jnp.broadcast_to(loss_part, (8, 128))
    for i in range(1, nc):
        to = col_peer(i)
        for copy in (
            send(gp_all.at[c], gp_all.at[c], gp_s.at[i - 1], gp_r.at[i - 1], (b, to)),
            send(loss_all.at[c], loss_all.at[c], lo_s.at[i - 1], lo_r.at[i - 1], (b, to)),
        ):
            copy.start()
            last_sends.append(copy)
    rows_grad = dot_as(probs[...], quarter_users, 1, 0)
    rows_grad = rows_grad.T.astype(BF16)
    for i in range(nc):
        rg_send[i] = rows_grad[i * width : (i + 1) * width]
    for i in range(1, nc):
        to = col_peer(i)
        copy = send(rg_send.at[to], rg_recv.at[c], rg_s.at[i - 1], rg_r.at[i - 1], (b, to))
        copy.start()
        last_sends.append(copy)
    rg_recv[c] = rg_send[c]
    for i in range(1, nb):
        send(g_send.at[0], g_recv.at[i - 1], gs_s.at[i - 1], gs_r.at[i - 1], (b, c)).wait_recv()
    factor = factors[pl.ds(pl.multiple_of(b * sz.quarter, sz.quarter), sz.quarter), :]
    total = factor[:, 0:1] * g_send[b].astype(F32)
    own_pos = e_rows[pl.ds(pl.multiple_of(cap + b * sz.quarter, sz.quarter), sz.quarter), :].astype(F32)
    for i in range(1, nb):
        home_send(i).wait_recv()
        total = total + factor[:, i : i + 1] * g_recv[i - 1].astype(F32)
        own_pos = own_pos + home[i - 1].astype(F32)
    total = total + factor[:, nb : nb + 1].astype(BF16).astype(F32) * own_pos

    def gu_at(block, col):
        return gu.at[block, pl.ds(pl.multiple_of(col * sz.quarter, sz.quarter), sz.quarter), :]

    def gu_all(col):
        return gu.at[:, pl.ds(pl.multiple_of(col * sz.quarter, sz.quarter), sz.quarter), :]

    gu[b, pl.ds(pl.multiple_of(c * sz.quarter, sz.quarter), sz.quarter), :] = total.astype(BF16)
    for i in range(1, nb):
        copy = send(gu_at(b, c), gu_at(b, c), ga_s.at[i - 1], ga_r.at[i - 1], (batch_peer(i), c))
        copy.start()
        last_sends.append(copy)
    for i in range(nb):
        copy = send(gu_at(b, c), gu_at(b, c), gx_s.at[i], gx_r.at[i], (batch_peer(i), cx))
        copy.start()
        last_sends.append(copy)

    tower(last)
    slopes(last)
    out_copies = [(x, x_out), (acts1, act1_out), (acts2, act2_out), (buckets, buckets_out)]
    out_copies = [pltpu.make_async_copy(s, d, out_sem.at[i]) for i, (s, d) in enumerate(out_copies)]
    for copy in out_copies:
        copy.start()
    for k in range(nc):
        low = slots[sz.cap_tiles + k, 1:2, :].astype(BF16)
        hot = one_where(low == iota((LOW, CHUNK), 0).astype(BF16), BF16)
        low_rows[k * CHUNK : (k + 1) * CHUNK, :] = hot.T
    pick_own = one_where(iota((width, embed), 1) == c * width + iota((width, embed), 0), BF16)
    for i in range(1, nc):
        src = col_from(i)
        send(gp_all.at[src], gp_all.at[src], gp_s.at[i - 1], gp_r.at[i - 1], (b, c)).wait_recv()
    pos_rows = []
    for quarter in range(nc):
        own_part = dot_as(pick_own, users_of(quarter), 1, 1)
        grad = gp_all[quarter, 0:1, :].astype(BF16).astype(F32)
        mine = slots[sz.cap_tiles + quarter, 0:1, :] >= 0.0
        pos_rows.append(jnp.where(mine, grad * own_part, 0.0).astype(BF16))
    pos_rows = jnp.concatenate(pos_rows, axis=1)
    pos_parts = jnp.concatenate(
        [slots[sz.cap_tiles + k, 0:1, :] for k in range(nc)], axis=1
    ).astype(BF16)

    def pos_scatter(n, _):
        found = scattered(n, pos_parts, pos_rows, low_rows[...])
        for j in range(2):
            for i in range(4):
                pos_table[n * 2 + j, :, i * LOW : (i + 1) * LOW] = found[
                    (j * 4 + i) * width : (j * 4 + i + 1) * width
                ].astype(BF16)
        return 0

    lax.fori_loop(0, sz.high_parts // 2, pos_scatter, 0)
    pos_copy = pltpu.make_async_copy(pos_table, pos_table_out, out_sem.at[5])
    pos_copy.start()
    for i in range(1, nb):
        src = batch_from(i)
        send(gu_at(src, c), gu_at(src, c), ga_s.at[i - 1], ga_r.at[i - 1], (b, c)).wait_recv()
    copy = send(gu_all(c), gu_all(c), gc_s.at[0], gc_r.at[0], (b, ck))
    copy.start()
    last_sends.append(copy)

    def rows_at(ref, col):
        return ref.at[:, pl.ds(pl.multiple_of(col * sz.quarter, sz.quarter), sz.quarter), :]

    def down_copies(col, i):
        return [
            pltpu.make_async_copy(rows_at(kept, col), rows_at(out, col), down_sem.at[i, k])
            for k, (kept, out) in enumerate(((gps, gps_out), (gpf, gpf_out), (gx, gx_out)))
        ]

    def down(i, col):
        def spread_out(ref, value):
            for j in range(nb):
                ref[j, pl.ds(pl.multiple_of(col * sz.quarter, sz.quarter), sz.quarter), :] = value[
                    j * sz.quarter : (j + 1) * sz.quarter
                ]

        def gathered(ref):
            return jnp.concatenate(
                [
                    ref[pl.ds(pl.multiple_of(j * sz.rows + col * sz.quarter, sz.quarter), sz.quarter), :]
                    for j in range(nb)
                ],
                axis=0,
            )

        top = jnp.concatenate(
            [gu[j, pl.ds(pl.multiple_of(col * sz.quarter, sz.quarter), sz.quarter), :] for j in range(nb)],
            axis=0,
        )
        second = (dot_as(top, w3[...], 1, 1) * gathered(slopes2).astype(F32)).astype(BF16)
        spread_out(gps, second)
        first = (dot_as(second, w2[...], 1, 1) * gathered(slopes1).astype(F32)).astype(BF16)
        spread_out(gpf, first)
        spread_out(gx, dot_as(first, w1_own[...], 1, 1).astype(BF16))
        for copy in down_copies(col, i):
            copy.start()

    def quarter_down(i, _):
        flip = jnp.where(i == 0, c, jnp.where(i == 1, ck, jnp.where(i == 2, cx, ckx)))

        @pl.when(i == 1)
        def _():
            send(gu_all(ck), gu_all(ck), gc_s.at[0], gc_r.at[0], (b, ck)).wait_recv()

        @pl.when(i == 2)
        def _():
            for k in range(nb):
                src = batch_from(k)
                send(gu_at(src, cx), gu_at(src, cx), gx_s.at[k], gx_r.at[k], (b, cx)).wait_recv()
            send(gu_all(cx), gu_all(cx), gc_s.at[1], gc_r.at[1], (b, ck)).start()

        @pl.when(i == 3)
        def _():
            send(gu_all(ckx), gu_all(ckx), gc_s.at[1], gc_r.at[1], (b, ck)).wait_recv()

        down(i, flip)
        return 0

    lax.fori_loop(0, nc, quarter_down, 0)
    gu_copy = pltpu.make_async_copy(gu, gu_out, out_sem.at[4])
    gu_copy.start()

    for i in range(1, nc):
        src = col_from(i)
        send(loss_all.at[src], loss_all.at[src], lo_s.at[i - 1], lo_r.at[i - 1], (b, c)).wait_recv()
        send(rg_recv.at[src], rg_recv.at[src], rg_s.at[i - 1], rg_r.at[i - 1], (b, c)).wait_recv()
    loss = loss_all[0]
    neg_total = rg_recv[0].astype(F32)
    for i in range(1, nc):
        loss = loss + loss_all[i]
        neg_total = neg_total + rg_recv[i].astype(F32)
    neg_rows_out[...] = neg_total.astype(BF16)
    loss_out[...] = loss[0:1, 0:1]

    last_sends.append(send(gu_all(cx), gu_all(cx), gc_s.at[1], gc_r.at[1], (b, ck)))
    for i in range(1, nc):
        last_sends.append(pos_send(i))
    for i in range(1, nb):
        last_sends.append(home_send(i))
    for copy in last_sends:
        copy.wait_send()

    def drain(t, _):
        for i in range(1, nb):
            send(sums.at[t, pl.ds(0, piece)], pieces.at[t, 0], rs_s.at[t, i - 1], rs_r.at[t], (b, c)).wait_send()
            send(x_piece(t, b), x_piece(t, b), ag_s.at[t, i - 1], ag_r.at[t], (b, c)).wait_send()

        @pl.when(t < last)
        def _():
            send(x_at(t, c), x_at(t, c), xx_s.at[t], xx_r.at[t], (b, cx)).wait_send()
            send(x_pair(t, c), x_pair(t, c), co_s.at[t], co_r.at[t], (b, ck)).wait_send()

        return 0

    lax.fori_loop(0, sz.steps, drain, 0)
    for i in range(nb):
        for k in range(1, nc):
            direct_send(last, i, k).wait_send()
    for table in range(2):
        for t in (sz.steps - 2, sz.steps - 1):
            count_copy(t, table, t % 2).wait()
    gu_copy.wait()
    pos_copy.wait()
    for copy in out_copies:
        copy.wait()
    for i, col in enumerate((c, ck, cx, ckx)):
        for copy in down_copies(col, i):
            copy.wait()


def front(sz, args):
    nb, nc, total = sz.batch, sz.col, sz.total
    width, embed, cap, users = sz.width, sz.embed, sz.cap, sz.users
    slots = cap + users
    first, second = args["w_second"].shape
    buckets = args["demo_table"].shape[0]
    x_width = sz.x_width
    vmem = pl.BlockSpec(memory_space=pltpu.VMEM)
    smem = pl.BlockSpec(memory_space=pltpu.SMEM)
    hbm = pl.BlockSpec(memory_space=pl.ANY)
    dma = pltpu.SemaphoreType.DMA

    def shape(dims, kind=BF16):
        return jax.ShapeDtypeStruct(dims, kind)

    outs = [
        (shape((2, sz.high_parts, 4, total, LOW)), hbm), (shape((total, x_width)), hbm),
        (shape((total, first)), hbm), (shape((total, second)), hbm), (shape((nb, sz.rows, embed)), hbm),
        (shape((nb, sz.rows, second)), hbm), (shape((nb, sz.rows, first)), hbm),
        (shape((nb, sz.rows, 256)), hbm), (shape((buckets, total)), hbm),
        (shape((width, cap)), vmem), (shape((sz.high_parts, width, 4 * LOW)), hbm),
        (shape((sz.tiles, 8, CHUNK), F32), vmem),
        (shape((sz.quarter, embed)), vmem), (shape((1, 1), F32), vmem), (shape((1, 1), I32), vmem),
    ]
    scratch = [
        pltpu.VMEM((3, width, sz.vocab), BF16),
        pltpu.VMEM((sz.high * width, LOW), BF16),
        pltpu.VMEM((2, sz.high_parts * LOW, 4 * width), BF16),
        pltpu.VMEM(args["w_first"].shape, BF16),
        pltpu.VMEM((x_width, first), BF16),
        pltpu.VMEM((256, first), BF16),
        pltpu.VMEM((first, second), BF16),
        pltpu.VMEM((second, embed), BF16),
        pltpu.VMEM((BAG_PAD, 128), I32),
        pltpu.VMEM((sz.rows, BAG_PAD), I32),
        pltpu.VMEM((sz.groups, CHUNK), I32),
        pltpu.VMEM((nb, sz.groups, CHUNK), I32),
        pltpu.VMEM((nb, 8, 128), I32),
        pltpu.VMEM((sz.neg_lines, CHUNK), F32),
        pltpu.VMEM((4, sz.neg_lines, CHUNK), F32),
        pltpu.VMEM((2, 2, sz.high_parts, 4, sz.span, LOW), BF16),
        pltpu.VMEM((2, sz.span, 128), F32),
        pltpu.VMEM((sz.steps, sz.span, 128), BF16),
        pltpu.VMEM((sz.steps, nb - 1, sz.span // nb, 128), BF16),
        pltpu.VMEM((total, x_width), BF16),
        pltpu.VMEM((total, first), F32),
        pltpu.VMEM((total, second), F32),
        pltpu.VMEM((total, first), BF16),
        pltpu.VMEM((total, first), BF16),
        pltpu.VMEM((total, second), BF16),
        pltpu.VMEM((total, second), BF16),
        pltpu.VMEM((total, embed), BF16),
        pltpu.VMEM((buckets, total), BF16),
        pltpu.VMEM((sz.tiles, 8, CHUNK), F32),
        pltpu.VMEM((sz.tiles, width, CHUNK), BF16),
        pltpu.VMEM((nc, sz.cap_tiles, width, CHUNK), BF16),
        pltpu.VMEM((nc, width, users), BF16),
        pltpu.VMEM((embed, slots), BF16),
        pltpu.VMEM((slots, embed), BF16),
        pltpu.VMEM((nc * CHUNK, LOW), BF16),
        pltpu.VMEM((sz.high_parts, width, 4 * LOW), BF16),
        pltpu.VMEM((cap, users), BF16),
        pltpu.VMEM((nb, 8, users), F32),
        pltpu.VMEM((users, 16), F32),
        pltpu.VMEM((nb - 1, sz.quarter, embed), BF16),
        pltpu.VMEM((nb, sz.quarter, embed), BF16),
        pltpu.VMEM((nb - 1, sz.quarter, embed), BF16),
        pltpu.VMEM((nb, sz.rows, embed), BF16),
        pltpu.VMEM((nb, sz.rows, second), BF16),
        pltpu.VMEM((nb, sz.rows, first), BF16),
        pltpu.VMEM((nb, sz.rows, 256), BF16),
        pltpu.VMEM((nc, width, cap), BF16),
        pltpu.VMEM((nc, width, cap), BF16),
        pltpu.VMEM((nc, 8, users), F32),
        pltpu.VMEM((nc, 8, 128), F32),
        dma((6,)), dma((6,)), dma((nc, 3)), dma((2, 2)),
        dma((nc, nb - 1)), dma((nc,)), dma((nb - 1,)), dma((nb - 1,)), dma((nc - 1, nb)), dma((nc - 1,)),
        dma((sz.steps, nb - 1)), dma((sz.steps,)), dma((sz.steps, nb - 1)), dma((sz.steps,)),
        dma((sz.steps,)), dma((sz.steps,)), dma((sz.steps,)), dma((sz.steps,)),
        dma((nc - 1,)), dma((nc - 1,)), dma((nc - 1,)), dma((nc - 1,)), dma((nb - 1,)), dma((nb - 1,)),
        dma((nb - 1,)), dma((nb - 1,)), dma((nb - 1,)), dma((nb - 1,)),
        dma((nb - 1,)), dma((nb - 1,)), dma((nb,)), dma((nb,)), dma((2,)), dma((2,)),
        dma((nc - 1,)), dma((nc - 1,)), dma((nc - 1,)), dma((nc - 1,)), dma((nc - 1,)), dma((nc - 1,)),
    ]
    operands = [
        (args["watch_ids"].T, vmem), (args["search_ids"].T, vmem), (args["demo_ids"].T, vmem),
        (args["pos_ids"].reshape(1, -1), vmem), (args["neg_ids"].reshape(-1, 128), vmem),
        (args["demo_table"].T, vmem), (args["b_first"].reshape(1, -1), vmem),
        (args["b_second"].reshape(1, -1), vmem), (args["b_third"].reshape(1, -1), vmem),
        (args["valid_counts"], smem),
        (args["watch_table"], hbm), (args["search_table"], hbm), (args["out_table"], hbm),
        (args["w_first"], hbm), (args["w_second"], hbm), (args["w_third"], hbm),
    ]
    return pl.pallas_call(
        functools.partial(front_kernel, sz),
        out_shape=[o for o, _ in outs],
        in_specs=[s for _, s in operands],
        out_specs=[s for _, s in outs],
        scratch_shapes=scratch,
        compiler_params=pltpu.CompilerParams(
            collective_id=0, has_side_effects=True, vmem_limit_bytes=63 * 2**20
        ),
        name="front",
    )(*[o for o, _ in operands])


def back_kernel(
    sz, neg_rows, slots, user_in, loss_in, pos_in, counts, x_in, act1_in, act2_in, gu_in, gps_in, gpf_in, gx_in, buckets_in,
    watch_out, search_out, table_out, gw1_out, gw2_out, gw3_out, demo_out, gb1_out, gb2_out, gb3_out, user_out, loss_out,
    pos_table, x, act1, act2, gu, gps, gpf, gx, buckets, grads, ring,
    lines, low_rows, gw1, gw2, gw3, in_sem, ring_sem, line_sem, out_sem,
):
    width, cap, total, nb = sz.width, sz.cap, sz.total, sz.batch
    parts, nc, embed = sz.high_parts, sz.col, sz.embed
    depth = ring.shape[0]
    names = [
        (gx_in, gx), (pos_in, pos_table), (act2_in, act2), (gu_in, gu), (act1_in, act1), (gps_in, gps), (x_in, x), (gpf_in, gpf),
        (buckets_in, buckets),
    ]
    loads = [pltpu.make_async_copy(s, d, in_sem.at[i]) for i, (s, d) in enumerate(names)]
    loads[0].start()
    loads[1].start()
    user_out[...] = user_in[...]
    loss_out[...] = loss_in[...]

    def ring_load(hh):
        at = lax.rem(hh, depth)
        return pltpu.make_async_copy(counts.at[:, hh], ring.at[at], ring_sem.at[at])

    early = depth - 1
    for n in range(early):
        ring_load(n).start()
    for load in loads[2:]:
        load.start()
    for n in range(early, depth):
        ring_load(n).start()
    loads[0].wait()

    own_grads = gx[...].reshape(total, gx.shape[2])[:, 0:128]
    grads[0] = own_grads.T
    grads[1] = flip_rows(own_grads.astype(F32)).astype(BF16).T

    def line_store(out, slot, hh):
        at = pl.ds(pl.multiple_of(hh * 4 * LOW, 4 * LOW), 4 * LOW)
        return pltpu.make_async_copy(lines.at[slot], out.at[:, at], line_sem.at[slot])

    def put(slot, found, factor):
        for i in range(4):
            lines[slot, :, i * LOW : (i + 1) * LOW] = found[i] * factor

    for k in range(sz.cap_tiles):
        low = slots[k, 1:2, :].astype(BF16)
        hot = one_where(low == iota((LOW, CHUNK), 0).astype(BF16), BF16)
        low_rows[k * CHUNK : (k + 1) * CHUNK, :] = hot.T
    high = jnp.concatenate([slots[k, 0:1, :] for k in range(sz.cap_tiles)], axis=1).astype(BF16)
    loads[1].wait()

    def scatter(n, _):
        found = scattered(n, high, neg_rows[...], low_rows[...])
        for j in range(2):

            @pl.when(n >= 1)
            def _():
                line_store(table_out, 4 + j, (n - 1) * 2 + j).wait()

            rows = [found[(j * 4 + i) * width : (j * 4 + i + 1) * width] for i in range(4)]
            rows = [rows[i] + pos_table[n * 2 + j, :, i * LOW : (i + 1) * LOW].astype(F32) for i in range(4)]
            put(4 + j, rows, 1.0)
            line_store(table_out, 4 + j, n * 2 + j).start()
        return 0

    lax.fori_loop(0, parts // 2, scatter, 0)
    def bags(hh, _):
        ring_load(hh).wait()
        for table, out in enumerate((watch_out, search_out)):
            slot = table * 2 + lax.rem(hh, 2)
            found = [
                dot_as(
                    grads[i % 2, table * width : (table + 1) * width, :],
                    ring[lax.rem(hh, depth), table, i], 1, 0,
                )
                for i in range(4)
            ]

            @pl.when(hh >= 2)
            def _():
                line_store(out, slot, hh - 2).wait()

            put(slot, found, 1.0 / sz.bag)
            line_store(out, slot, hh).start()

        @pl.when(hh + depth < parts)
        def _():
            ring_load(hh + depth).start()

        return 0

    lax.fori_loop(0, parts // 2, bags, 0)

    for load in loads[2:]:
        load.wait()
    gu_rows = gu[...].reshape(total, embed)
    second = gps[...].reshape(total, gps.shape[2])
    first = gpf[...].reshape(total, gpf.shape[2])
    demo_grad = gx[...].reshape(total, 256)[:, 128:]
    gw3[...] = dot_as(act2[...], gu_rows, 0, 0)
    gw2[...] = dot_as(act1[...], second, 0, 0)
    gw1[...] = dot_as(x[...], first, 0, 0)
    stores = [(gw3, gw3_out), (gw2, gw2_out)]
    for i in range(nc):
        at = x_place(i)
        stores.append((gw1.at[pl.ds(at, width)], gw1_out.at[pl.ds(i * width, width)]))
        stores.append((gw1.at[pl.ds(at + width, width)], gw1_out.at[pl.ds(embed + i * width, width)]))
    stores.append((gw1.at[pl.ds(nc * 128, sz.demo_width)], gw1_out.at[pl.ds(2 * embed, sz.demo_width)]))
    stores = [pltpu.make_async_copy(s, d, out_sem.at[i]) for i, (s, d) in enumerate(stores)]
    for store in stores:
        store.start()
    demo = dot_as(buckets[...], demo_grad, 1, 0)
    demo_out[...] = demo.T[0 : sz.demo_width, :]
    gb1_out[...] = jnp.sum(first.astype(F32), axis=0, keepdims=True)
    gb2_out[...] = jnp.sum(second.astype(F32), axis=0, keepdims=True)
    gb3_out[...] = jnp.sum(gu_rows.astype(F32), axis=0, keepdims=True)

    lax.fori_loop(parts // 2, parts, bags, 0)

    for table, out in enumerate((watch_out, search_out)):
        for hh in (parts - 2, parts - 1):
            line_store(out, table * 2 + hh % 2, hh).wait()
    for j in range(2):
        line_store(table_out, 4 + j, parts - 2 + j).wait()
    for store in stores:
        store.wait()


def back(sz, args, kept):
    vmem = pl.BlockSpec(memory_space=pltpu.VMEM)
    hbm = pl.BlockSpec(memory_space=pl.ANY)
    total, nb = sz.total, sz.batch
    first, second = args["w_second"].shape
    embed, buckets = sz.embed, args["demo_table"].shape[0]
    dma = pltpu.SemaphoreType.DMA

    def shape(dims, kind=F32):
        return jax.ShapeDtypeStruct(dims, kind)

    table = shape((sz.width, sz.vocab))
    outs = [(table, hbm)] * 3 + [
        (shape((args["w_first"].shape)), hbm), (shape((first, second)), hbm), (shape((second, embed)), hbm),
        (shape((sz.demo_width, buckets)), vmem), (shape((1, first)), vmem), (shape((1, second)), vmem),
        (shape((1, embed)), vmem), (shape((sz.quarter, embed), BF16), vmem), (shape((1, 1)), vmem),
    ]
    slots = sz.cap
    return pl.pallas_call(
        functools.partial(back_kernel, sz),
        out_shape=[o for o, _ in outs],
        in_specs=[vmem] * 4 + [hbm] * 10,
        out_specs=[s for _, s in outs],
        scratch_shapes=[
            pltpu.VMEM((sz.high_parts, sz.width, 4 * LOW), BF16),
            pltpu.VMEM((total, sz.x_width), BF16), pltpu.VMEM((total, first), BF16),
            pltpu.VMEM((total, second), BF16), pltpu.VMEM((nb, sz.rows, embed), BF16),
            pltpu.VMEM((nb, sz.rows, second), BF16), pltpu.VMEM((nb, sz.rows, first), BF16),
            pltpu.VMEM((nb, sz.rows, 256), BF16), pltpu.VMEM((buckets, total), BF16),
            pltpu.VMEM((2, 128, total), BF16), pltpu.VMEM((4, 2, 4, total, LOW), BF16),
            pltpu.VMEM((6, sz.width, 4 * LOW), F32), pltpu.VMEM((slots, LOW), BF16),
            pltpu.VMEM((sz.x_width, first), F32), pltpu.VMEM((first, second), F32),
            pltpu.VMEM((second, embed), F32),
            dma((9,)), dma((4,)), dma((6,)), dma((3 + 2 * sz.col,)),
        ],
        compiler_params=pltpu.CompilerParams(vmem_limit_bytes=62 * 2**20),
        name="back",
    )(*kept)


def fast_device(sz, *inputs):
    names = (
        "watch_ids", "search_ids", "demo_ids", "pos_ids", "neg_ids", "valid_counts", "watch_table",
        "search_table", "demo_table", "out_table", "w_first", "b_first", "w_second", "b_second",
        "w_third", "b_third",
    )
    args = dict(zip(names, inputs))
    (
        counts, x, act1, act2, gu, gps, gpf, gx, buckets, neg_rows, pos_table, slots, user_vecs, loss, fits,
    ) = front(sz, args)

    def finish(*operands):
        kept = (neg_rows, slots, user_vecs, loss, pos_table, counts, x, act1, act2, gu, gps, gpf, gx, buckets)
        watch, search, table, gw1, gw2, gw3, demo, gb1, gb2, gb3, user, mean = back(sz, args, kept)
        return (
            user, mean.reshape(()), watch, search, table, demo.T, gw1, gb1.reshape(-1),
            gw2, gb2.reshape(-1), gw3, gb3.reshape(-1),
        )

    def general(*operands):
        return per_device(RingCollectives(), *operands)

    return lax.cond(fits.reshape(()) > 0, finish, general, *inputs)


def fast_sizes(mesh, shapes):
    watch, demo, negs, table, first = shapes
    batch, col = mesh.shape["batch"], mesh.shape["col"]
    rows, width, vocab = watch[0] // batch, table[0] // col, table[1] // batch
    demo_width = first[0] - 2 * table[0]
    sz = Sizes(batch, col, rows, watch[1], width, vocab, negs[0], table[0], demo_width)
    good = (
        batch == 8 and col == 4 and rows == 128 and watch[1] <= BAG_PAD and width == 64
        and vocab == 32 * LOW and table[1] <= 65536 and demo[1] <= 4 and demo_width <= 128
        and negs[0] % 128 == 0 and negs[0] <= 256 * CHUNK
    )
    return sz if good else None


def solution(mesh):
    in_specs = (
        P("batch", None),
        P("batch", None),
        P("batch", None),
        P("batch"),
        P(),
        P("batch"),
        P("col", "batch"),
        P("col", "batch"),
        P(),
        P("col", "batch"),
        P(),
        P(),
        P(),
        P(),
        P(),
        P(),
    )
    out_specs = (
        P(("batch", "col"), None),
        P(),
        P("col", "batch"),
        P("col", "batch"),
        P("col", "batch"),
        P(),
        P(),
        P(),
        P(),
        P(),
        P(),
        P(),
    )
    def whole(*inputs):
        shapes = [inputs[i].shape for i in (0, 2, 4, 6, 10)]
        sz = fast_sizes(mesh, shapes)
        if sz is None:
            body = functools.partial(per_device, Collectives())
        else:
            body = functools.partial(fast_device, sz)
        return jax.shard_map(
            body, mesh=mesh, in_specs=in_specs, out_specs=out_specs, check_vma=False
        )(*inputs)

    return whole
```
